32 devices in a mesh: batch: 2 (over x), seq: 16 (over z, y, core).
Axes of the slice: x: 2, y: 2, z: 4, core: 2. Of those that a mesh axis runs over, the one named last changes fastest.
Arguments:
- query_gate: float32 [4, 4096, 128], P('batch', 'seq'), may hold values from -6 to 6
- key_gate: float32 [4, 4096, 128], P('batch', 'seq'), may hold values from -6 to 6
- value_input: float32 [4, 4096, 128], P('batch', 'seq'), may hold values from -6 to 6
- filters: float32 [128, 4096], P('seq'), may hold values from -1 to 1, as said below
- skip_gain: float32 [128], replicated, may hold values from 0.5 to 1.5
- cotangent: float32 [4, 4096, 128], P('batch', 'seq'), may hold values from -6 to 6
Outputs:
- output: float32 [4, 4096, 128], P('batch', 'seq')
- query_grad: float32 [4, 4096, 128], P('batch', 'seq')
- key_grad: float32 [4, 4096, 128], P('batch', 'seq')
- value_grad: float32 [4, 4096, 128], P('batch', 'seq')
- filter_grad: float32 [128, 4096], P('seq', 'batch')
The draws below stay inside these ranges and needn't reach their ends.
Inputs may be any that keep to these rules, and one draw needn't show every extreme that they name: `filters`: each channel's filter has a sum of squares of one.
All inputs are finite; a program needn't handle non-finite values.
Results may differ from the reference program's by a relative error of at most 0.0001.
Values sent between devices are 32-bit elements; how exact they have to be, the bound alone decides.
No kernel may reach another device: no remote copies, remote signals or barrier semaphores. Data moves between devices by JAX's collectives and lax.ppermute only.
A program may use at most 128 MiB of HBM per device.

```python
import math
import jax
import jax.numpy as jnp
from jax import lax

CHAN = 128
LEN = 4096
BATCH = 4


def draw_filters(key, part):
    key_noise = jax.random.fold_in(key, 11)
    key_decay = jax.random.fold_in(key, 12)
    position_index = jnp.arange(LEN, dtype=jnp.float32)
    decay_spans = LEN * jnp.exp(jax.random.uniform(key_decay, (CHAN, 1), jnp.float32, math.log(0.002), math.log(4.0)))
    envelope = jnp.exp(-position_index[None, :] / decay_spans)
    noise_draw = jax.random.normal(key_noise, (CHAN, LEN), jnp.float32)
    raw_filter = noise_draw * envelope
    return raw_filter / jnp.sqrt(jnp.sum(raw_filter * raw_filter, axis=1, keepdims=True))


def block_scale(rng, dims, split, low, high):
    factor_of = 1.0
    for position, shards_of in split:
        steps = jax.random.uniform(jax.random.fold_in(jax.random.fold_in(rng, 6), position), (shards_of,), jnp.float32, low / len(split), high / len(split))
        factor_of = factor_of * jnp.repeat(jnp.exp(steps), dims[position] // shards_of).reshape((-1,) + (1,) * (len(dims) - 1 - position))
    return factor_of


def bell_draw(own_key, dims, spread, bound, pieces=(), held_as=jnp.bfloat16):
    result = jax.random.normal(own_key, dims, jnp.float32) * spread
    if len(pieces) > 0:
        result = block_scale(own_key, dims, pieces, -0.22, 0.18) * result
    return jnp.clip(result, min=-bound, max=bound).astype(held_as)


def setup_inputs(seed: int = 0) -> dict:
    key_list = jax.random.split(jax.random.key(seed), 7)
    query_gate = bell_draw(key_list[0], (BATCH, LEN, CHAN), 1.0, 6.0, ((0, 2), (1, 16)), jnp.float32)
    key_gate = bell_draw(key_list[1], (BATCH, LEN, CHAN), 1.0, 6.0, ((0, 2), (1, 16)), jnp.float32)
    value_input = bell_draw(key_list[2], (BATCH, LEN, CHAN), 1.0, 6.0, ((0, 2), (1, 16)), jnp.float32)
    filters = draw_filters(jax.random.fold_in(key_list[6], 71), 0)
    skip_gain = jnp.clip(jax.random.uniform(key_list[4], (CHAN,), jnp.float32, 0.5, 1.5), 0.5, 1.5)
    cotangent = bell_draw(key_list[5], (BATCH, LEN, CHAN), 1.0, 6.0, ((0, 2), (1, 16)), jnp.float32)
    return {"query_gate": query_gate, "key_gate": key_gate, "value_input": value_input, "filters": filters, "skip_gain": skip_gain, "cotangent": cotangent}


def reference(query_gate, key_gate, value_input, filters, skip_gain, cotangent):
    full_length = 2 * LEN
    mixed = key_gate * value_input
    upstream = cotangent * query_gate
    mixed_spectrum = jnp.fft.rfft(jnp.transpose(mixed, (0, 2, 1)), n=full_length, axis=-1)
    upstream_spectrum = jnp.fft.rfft(jnp.transpose(upstream, (0, 2, 1)), n=full_length, axis=-1)
    filter_spectrum = jnp.fft.rfft(filters, n=full_length, axis=-1)
    convolved = jnp.fft.irfft(mixed_spectrum * filter_spectrum[None], n=full_length, axis=-1)[..., :LEN]
    back_term = jnp.fft.irfft(jnp.conj(filter_spectrum)[None] * upstream_spectrum, n=full_length, axis=-1)[..., :LEN]
    filter_sum = lax.optimization_barrier(jnp.sum(jnp.conj(mixed_spectrum) * upstream_spectrum, axis=0))
    filter_grad = jnp.fft.irfft(filter_sum, n=full_length, axis=-1)[..., :LEN] / math.sqrt(LEN)
    hidden_state = jnp.transpose(convolved, (0, 2, 1)) + skip_gain * mixed
    output = query_gate * hidden_state
    query_grad = cotangent * hidden_state
    mixed_grad = jnp.transpose(back_term, (0, 2, 1)) + skip_gain * upstream
    key_grad = mixed_grad * value_input
    value_grad = mixed_grad * key_gate
    return (output, query_grad, key_grad, value_grad, filter_grad)
```

```python
import math

import jax
import jax.numpy as jnp
import ml_dtypes
import numpy as np
from jax import lax
from jax.experimental import pallas as pl
from jax.experimental.pallas import tpu as pltpu
from jax.sharding import PartitionSpec as P

VMEM_BYTES = 48 * 1024 * 1024
ROW_CHUNK = 128


def add(a, b):
    if a is None:
        return b
    if b is None:
        return a
    return a + b


def sub(a, b):
    if b is None:
        return a
    if a is None:
        return -b
    return a - b


def scale(a, factor):
    if a is None or factor == 1.0:
        return a
    if factor == -1.0:
        return -a
    return a * factor


def turn(x, step, period):
    if x is None:
        return None
    re, im = x
    step = step % period
    if (4 * step) % period == 0:
        quarter = 4 * step // period
        if quarter == 0:
            return (re, im)
        if quarter == 1:
            return (im, scale(re, -1.0))
        if quarter == 2:
            return (scale(re, -1.0), scale(im, -1.0))
        return (scale(im, -1.0), re)
    angle = -2.0 * math.pi * step / period
    c, s = math.cos(angle), math.sin(angle)
    if (8 * step) % period == 0:
        root = math.sqrt(0.5)
        total, difference = add(re, im), sub(re, im)
        if c * s > 0:
            return (scale(difference, math.copysign(root, c)), scale(total, math.copysign(root, c)))
        return (scale(total, math.copysign(root, c)), scale(sub(im, re), math.copysign(root, c)))
    return (sub(scale(re, c), scale(im, s)), add(scale(re, s), scale(im, c)))


def complex_add(x, y):
    if x is None:
        return y
    if y is None:
        return x
    return (add(x[0], y[0]), add(x[1], y[1]))


def complex_sub(x, y):
    if y is None:
        return x
    if x is None:
        return (scale(y[0], -1.0), scale(y[1], -1.0))
    return (sub(x[0], y[0]), sub(x[1], y[1]))


def small_dft(values):
    size = len(values)
    if size == 1:
        return list(values)
    even = small_dft(values[0::2])
    odd = small_dft(values[1::2])
    odd = [turn(value, step, size) for step, value in enumerate(odd)]
    return [complex_add(e, o) for e, o in zip(even, odd)] + [
        complex_sub(e, o) for e, o in zip(even, odd)
    ]


def factors_of(size):
    first = 1
    while first * first < size:
        first *= 2
    return (size // first, first)


def across_rows(load, emit, count, kept, store, fetch):
    first, second = factors_of(count)
    for b in range(second):
        values = small_dft([load(second * a + b) for a in range(first)])
        for p, value in enumerate(values):
            store(b, p, turn(value, b * p, count))
    for p in range(first):
        values = small_dft([fetch(b, p) for b in range(second)])
        for q, value in enumerate(values):
            k1 = p + first * q
            if k1 < kept:
                emit(k1, value)


def tables(count, lanes):
    k1 = np.arange(count)[:, None]
    n2 = np.arange(lanes)[None, :]
    phase = -2.0 * np.pi * ((k1 * n2) % (count * lanes)) / (count * lanes)
    twist = np.concatenate([np.cos(phase), np.sin(phase)], axis=1).astype(np.float32)
    j = np.arange(lanes)
    phase = -2.0 * np.pi * ((j[:, None] * j[None, :]) % lanes) / lanes
    c, s = np.cos(phase), np.sin(phase)
    matrix = np.block([[c, s], [-s, c]]).astype(np.float32)
    high = matrix.astype(ml_dtypes.bfloat16)
    low = (matrix - high.astype(np.float32)).astype(ml_dtypes.bfloat16)
    return twist, np.concatenate([high, high, low], axis=0)


def lane_dft(x, matrix):
    high = x.astype(jnp.bfloat16)
    low = (x - high.astype(jnp.float32)).astype(jnp.bfloat16)
    return jnp.dot(
        jnp.concatenate([high, low, high], axis=1), matrix, preferred_element_type=jnp.float32
    )


def gate_kernel(query_ref, key_ref, value_ref, cotangent_ref, sent_ref):
    shards, _, batch, channels, tokens = sent_ref.shape
    for b in range(batch):
        mixed = key_ref[b] * value_ref[b]
        upstream = cotangent_ref[b] * query_ref[b]
        sent_ref[:, 0, b] = jnp.transpose(mixed).reshape(shards, channels, tokens)
        sent_ref[:, 1, b] = jnp.transpose(upstream).reshape(shards, channels, tokens)


def spectral_kernel(
    lag_scale, held_ref, filter_ref, twist_ref, matrix_ref, back_ref, lag_ref,
    middle, turned, filter_spec, mixed_spec, upstream_spec,
):
    shards, _, batch, channels, tokens = held_ref.shape
    count, width = twist_ref.shape
    lanes = width // 2
    length = shards * tokens
    live = count // 2
    pieces = tokens // lanes
    groups = lag_ref.shape[0]
    me = lax.axis_index("batch")

    def store(b, p, value):
        first, _ = factors_of(count)
        row = b * first + p
        re, im = value
        middle[row, :, :lanes] = jnp.zeros_like(im) if re is None else re
        middle[row, :, lanes:] = jnp.zeros_like(re) if im is None else im

    def fetch(b, p):
        first, _ = factors_of(count)
        row = b * first + p
        return (middle[row, :, :lanes], middle[row, :, lanes:])

    def place(k1, value):
        c, s = twist_ref[k1 : k1 + 1, :lanes], twist_ref[k1 : k1 + 1, lanes:]
        turned[k1, :, :lanes] = value[0] * c - value[1] * s
        turned[k1, :, lanes:] = value[0] * s + value[1] * c

    per_chunk = ROW_CHUNK // channels

    def chunks():
        for start in range(0, count, per_chunk):
            yield slice(start, min(start + per_chunk, count))

    def flat(x):
        return x.reshape(x.shape[0] * channels, width)

    def forward(load, spec):
        across_rows(load, place, count, count, store, fetch)
        for part in chunks():
            out = lane_dft(flat(turned[part]), matrix_ref[...])
            spec[part] = out.reshape(-1, channels, width)

    def inverse(product, emit):
        for part in chunks():
            re, im = product(part)
            x = jnp.concatenate([flat2(re), flat2(im)], axis=1)
            turned[part] = lane_dft(x, matrix_ref[...]).reshape(-1, channels, width)

        def load(k1):
            c, s = twist_ref[k1 : k1 + 1, :lanes], twist_ref[k1 : k1 + 1, lanes:]
            re, im = turned[k1, :, :lanes], turned[k1, :, lanes:]
            return (re * c - im * s, re * s + im * c)

        across_rows(load, emit, count, live, store, fetch)

    def flat2(x):
        return x.reshape(x.shape[0] * channels, lanes)

    def parts(spec, part):
        return spec[part, :, :lanes], spec[part, :, lanes:]

    def load_filter(n1):
        if n1 >= live:
            return None
        return (filter_ref[:, n1 * lanes : (n1 + 1) * lanes] * (0.5 / length), None)

    forward(load_filter, filter_spec)
    for pair in range(batch // 2):

        def load_kind(kind):
            def load(n1):
                if n1 >= live:
                    return None
                shard, piece = n1 // pieces, n1 % pieces
                span = slice(piece * lanes, (piece + 1) * lanes)
                return (
                    held_ref[shard, kind, 2 * pair, :, span],
                    held_ref[shard, kind, 2 * pair + 1, :, span],
                )

            return load

        def emit_kind(kind):
            def emit(n1, value):
                shard, piece = n1 // pieces, n1 % pieces
                span = slice(piece * lanes, (piece + 1) * lanes)
                back_ref[shard, kind, 2 * pair, :, span] = value[0]
                back_ref[shard, kind, 2 * pair + 1, :, span] = -value[1]

            return emit

        def convolve(part):
            fr, fi = parts(filter_spec, part)
            mr, mi = parts(mixed_spec, part)
            return (fr * mr - fi * mi, -(fr * mi + fi * mr))

        def correlate(part):
            fr, fi = parts(filter_spec, part)
            ur, ui = parts(upstream_spec, part)
            return (fr * ur + fi * ui, fi * ur - fr * ui)

        def lags(part):
            mr, mi = parts(mixed_spec, part)
            ur, ui = parts(upstream_spec, part)
            return (mr * ur + mi * ui, mi * ur - mr * ui)

        def emit_lag(n1, value):
            at = n1 * lanes
            share = length // groups
            slot = lax.rem(at // share - me + groups, groups)
            span = slice(at % share, at % share + lanes)
            if pair == 0:
                lag_ref[slot, :, span] = value[0] * lag_scale
            else:
                lag_ref[slot, :, span] += value[0] * lag_scale

        forward(load_kind(0), mixed_spec)
        inverse(convolve, emit_kind(0))
        forward(load_kind(1), upstream_spec)
        inverse(correlate, emit_kind(1))
        inverse(lags, emit_lag)


def output_kernel(
    query_ref, key_ref, value_ref, cotangent_ref, skip_ref, home_ref,
    output_ref, query_grad_ref, key_grad_ref, value_grad_ref,
):
    shards, _, batch, channels, tokens = home_ref.shape
    skip = skip_ref[...]
    for b in range(batch):
        query, key, value, cotangent = query_ref[b], key_ref[b], value_ref[b], cotangent_ref[b]
        convolved = jnp.transpose(home_ref[:, 0, b].reshape(shards * channels, tokens))
        hidden = convolved + skip * (key * value)
        output_ref[b] = query * hidden
        query_grad_ref[b] = cotangent * hidden
        back = jnp.transpose(home_ref[:, 1, b].reshape(shards * channels, tokens))
        mixed_grad = back + skip * (cotangent * query)
        key_grad_ref[b] = mixed_grad * value
        value_grad_ref[b] = mixed_grad * key


def per_device(query_gate, key_gate, value_input, filters, skip_gain, cotangent, *, shards, groups):
    batch, tokens, all_channels = query_gate.shape
    channels, length = filters.shape
    lanes = 128 if 2 * length // 128 <= 64 else tokens
    count = 2 * length // lanes
    twist, matrix = tables(count, lanes)
    params = pltpu.CompilerParams(vmem_limit_bytes=VMEM_BYTES)
    swap = jax.ShapeDtypeStruct((shards, 2, batch, channels, tokens), jnp.float32)
    sent = pl.pallas_call(gate_kernel, out_shape=swap, compiler_params=params, name="gate")(
        query_gate, key_gate, value_input, cotangent
    )
    held = lax.all_to_all(sent, "seq", split_axis=0, concat_axis=0, tiled=True)
    block = pltpu.VMEM((count, channels, 2 * lanes), jnp.float32)

    def body(*refs):
        spectral_kernel(1.0 / (2.0 * length * math.sqrt(length)), *refs)

    back, lag = pl.pallas_call(
        body,
        out_shape=(swap, jax.ShapeDtypeStruct((groups, channels, length // groups), jnp.float32)),
        scratch_shapes=[block] * 5,
        compiler_params=params,
        name="spectral",
    )(held, filters, twist, matrix)
    filter_grad = lag[0]
    for step in range(1, groups):
        pairs = [(source, (source + step) % groups) for source in range(groups)]
        filter_grad = filter_grad + lax.ppermute(lag[step], "batch", pairs)
    home = lax.all_to_all(back, "seq", split_axis=0, concat_axis=0, tiled=True)
    token_out = jax.ShapeDtypeStruct(query_gate.shape, jnp.float32)
    output, query_grad, key_grad, value_grad = pl.pallas_call(
        output_kernel, out_shape=(token_out,) * 4, compiler_params=params, name="outputs"
    )(query_gate, key_gate, value_input, cotangent, skip_gain.reshape(1, all_channels), home)
    return (output, query_grad, key_grad, value_grad, filter_grad)


def solution(mesh):
    in_specs = (
        P("batch", "seq", None),
        P("batch", "seq", None),
        P("batch", "seq", None),
        P("seq", None),
        P(),
        P("batch", "seq", None),
    )
    out_specs = (
        P("batch", "seq", None),
        P("batch", "seq", None),
        P("batch", "seq", None),
        P("batch", "seq", None),
        P("seq", "batch"),
    )
    shards, groups = mesh.shape["seq"], mesh.shape["batch"]

    def whole(*arrays):
        return per_device(*arrays, shards=shards, groups=groups)

    return jax.shard_map(whole, mesh=mesh, in_specs=in_specs, out_specs=out_specs, check_vma=False)
```

```python
import math

import jax
import jax.numpy as jnp
import ml_dtypes
import numpy as np
from jax import lax
from jax.experimental import pallas as pl
from jax.experimental.pallas import tpu as pltpu
from jax.sharding import PartitionSpec as P

VMEM_BYTES = 48 * 1024 * 1024
ROW_CHUNK = 128


def add(a, b):
    if a is None:
        return b
    if b is None:
        return a
    return a + b


def sub(a, b):
    if b is None:
        return a
    if a is None:
        return -b
    return a - b


def scale(a, factor):
    if a is None or factor == 1.0:
        return a
    if factor == -1.0:
        return -a
    return a * factor


def turn(x, step, period):
    if x is None:
        return None
    re, im = x
    step = step % period
    if (4 * step) % period == 0:
        quarter = 4 * step // period
        if quarter == 0:
            return (re, im)
        if quarter == 1:
            return (im, scale(re, -1.0))
        if quarter == 2:
            return (scale(re, -1.0), scale(im, -1.0))
        return (scale(im, -1.0), re)
    angle = -2.0 * math.pi * step / period
    c, s = math.cos(angle), math.sin(angle)
    if (8 * step) % period == 0:
        root = math.sqrt(0.5)
        total, difference = add(re, im), sub(re, im)
        if c * s > 0:
            return (scale(difference, math.copysign(root, c)), scale(total, math.copysign(root, c)))
        return (scale(total, math.copysign(root, c)), scale(sub(im, re), math.copysign(root, c)))
    return (sub(scale(re, c), scale(im, s)), add(scale(re, s), scale(im, c)))


def complex_add(x, y):
    if x is None:
        return y
    if y is None:
        return x
    return (add(x[0], y[0]), add(x[1], y[1]))


def complex_sub(x, y):
    if y is None:
        return x
    if x is None:
        return (scale(y[0], -1.0), scale(y[1], -1.0))
    return (sub(x[0], y[0]), sub(x[1], y[1]))


def small_dft(values):
    size = len(values)
    if size == 1:
        return list(values)
    even = small_dft(values[0::2])
    odd = small_dft(values[1::2])
    odd = [turn(value, step, size) for step, value in enumerate(odd)]
    return [complex_add(e, o) for e, o in zip(even, odd)] + [
        complex_sub(e, o) for e, o in zip(even, odd)
    ]


def factors_of(size):
    first = 1
    while first * first < size:
        first *= 2
    return (size // first, first)


def across_rows(load, emit, count, kept, store, fetch):
    first, second = factors_of(count)
    for b in range(second):
        values = small_dft([load(second * a + b) for a in range(first)])
        for p, value in enumerate(values):
            store(b, p, turn(value, b * p, count))
    for p in range(first):
        values = small_dft([fetch(b, p) for b in range(second)])
        for q, value in enumerate(values):
            k1 = p + first * q
            if k1 < kept:
                emit(k1, value)


def tables(count, lanes):
    k1 = np.arange(count)[:, None]
    n2 = np.arange(lanes)[None, :]
    phase = -2.0 * np.pi * ((k1 * n2) % (count * lanes)) / (count * lanes)
    twist = np.concatenate([np.cos(phase), np.sin(phase)], axis=1).astype(np.float32)
    j = np.arange(lanes)
    phase = -2.0 * np.pi * ((j[:, None] * j[None, :]) % lanes) / lanes
    c, s = np.cos(phase), np.sin(phase)
    matrix = np.block([[c, s], [-s, c]]).astype(np.float32)
    high = matrix.astype(ml_dtypes.bfloat16)
    low = (matrix - high.astype(np.float32)).astype(ml_dtypes.bfloat16)
    return twist, np.concatenate([high, high, low], axis=0)


def lane_dft(x, matrix):
    high = x.astype(jnp.bfloat16)
    low = (x - high.astype(jnp.float32)).astype(jnp.bfloat16)
    return jnp.dot(
        jnp.concatenate([high, low, high], axis=1), matrix, preferred_element_type=jnp.float32
    )


def gate_kernel(query_hbm, key_hbm, value_hbm, cotangent_hbm, *refs):
    *sent, held, turned, sems = refs
    shards = len(sent)
    _, batch, channels, tokens = sent[0].shape
    me = lax.axis_index("seq")
    sources = (key_hbm, value_hbm, cotangent_hbm, query_hbm)

    def copy(b, i):
        return pltpu.make_async_copy(sources[i].at[b], held.at[i, b], sems.at[i, b])

    for b in range(batch):
        for i in range(4):
            copy(b, i).start()
    for b in range(batch):
        for kind in range(2):
            copy(b, 2 * kind).wait()
            copy(b, 2 * kind + 1).wait()
            product = held[2 * kind, b] * held[2 * kind + 1, b]
            turned[:, kind, b] = jnp.transpose(product).reshape(shards, channels, tokens)
    for step in range(shards):
        sent[step][...] = turned[me ^ step]


def spectral_kernel(
    shards, lag_scale, filter_ref, twist_ref, matrix_ref, *refs
):
    received, refs = refs[:shards], refs[shards:]
    returned, refs = refs[:shards], refs[shards:]
    lag_ref, held_ref, back_ref, middle, turned, filter_spec, mixed_spec, upstream_spec = refs
    _, _, batch, channels, tokens = held_ref.shape
    count, width = twist_ref.shape
    lanes = width // 2
    length = shards * tokens
    live = count // 2
    pieces = tokens // lanes
    groups = lag_ref.shape[0]
    group = lax.axis_index("batch")
    me = lax.axis_index("seq")
    for step in range(shards):
        held_ref[me ^ step] = received[step][...]

    def store(b, p, value):
        first, _ = factors_of(count)
        row = b * first + p
        re, im = value
        middle[row, :, :lanes] = jnp.zeros_like(im) if re is None else re
        middle[row, :, lanes:] = jnp.zeros_like(re) if im is None else im

    def fetch(b, p):
        first, _ = factors_of(count)
        row = b * first + p
        return (middle[row, :, :lanes], middle[row, :, lanes:])

    def place(k1, value):
        c, s = twist_ref[k1 : k1 + 1, :lanes], twist_ref[k1 : k1 + 1, lanes:]
        turned[k1, :, :lanes] = value[0] * c - value[1] * s
        turned[k1, :, lanes:] = value[0] * s + value[1] * c

    per_chunk = ROW_CHUNK // channels

    def chunks():
        for start in range(0, count, per_chunk):
            yield slice(start, min(start + per_chunk, count))

    def flat(x):
        return x.reshape(x.shape[0] * channels, width)

    def forward(load, spec):
        across_rows(load, place, count, count, store, fetch)
        for part in chunks():
            out = lane_dft(flat(turned[part]), matrix_ref[...])
            spec[part] = out.reshape(-1, channels, width)

    def inverse(product, emit):
        for part in chunks():
            re, im = product(part)
            x = jnp.concatenate([flat2(re), flat2(im)], axis=1)
            turned[part] = lane_dft(x, matrix_ref[...]).reshape(-1, channels, width)

        def load(k1):
            c, s = twist_ref[k1 : k1 + 1, :lanes], twist_ref[k1 : k1 + 1, lanes:]
            re, im = turned[k1, :, :lanes], turned[k1, :, lanes:]
            return (re * c - im * s, re * s + im * c)

        across_rows(load, emit, count, live, store, fetch)

    def flat2(x):
        return x.reshape(x.shape[0] * channels, lanes)

    def parts(spec, part):
        return spec[part, :, :lanes], spec[part, :, lanes:]

    def load_filter(n1):
        if n1 >= live:
            return None
        return (filter_ref[:, n1 * lanes : (n1 + 1) * lanes] * (0.5 / length), None)

    forward(load_filter, filter_spec)
    for pair in range(batch // 2):

        def load_kind(kind):
            def load(n1):
                if n1 >= live:
                    return None
                shard, piece = n1 // pieces, n1 % pieces
                span = slice(piece * lanes, (piece + 1) * lanes)
                return (
                    held_ref[shard, kind, 2 * pair, :, span],
                    held_ref[shard, kind, 2 * pair + 1, :, span],
                )

            return load

        def emit_kind(kind):
            def emit(n1, value):
                shard, piece = n1 // pieces, n1 % pieces
                span = slice(piece * lanes, (piece + 1) * lanes)
                back_ref[shard, kind, 2 * pair, :, span] = value[0]
                back_ref[shard, kind, 2 * pair + 1, :, span] = -value[1]

            return emit

        def convolve(part):
            fr, fi = parts(filter_spec, part)
            mr, mi = parts(mixed_spec, part)
            return (fr * mr - fi * mi, -(fr * mi + fi * mr))

        def correlate(part):
            fr, fi = parts(filter_spec, part)
            ur, ui = parts(upstream_spec, part)
            return (fr * ur + fi * ui, fi * ur - fr * ui)

        def lags(part):
            mr, mi = parts(mixed_spec, part)
            ur, ui = parts(upstream_spec, part)
            return (mr * ur + mi * ui, mi * ur - mr * ui)

        def emit_lag(n1, value):
            at = n1 * lanes
            share = length // groups
            slot = lax.rem(at // share - group + groups, groups)
            span = slice(at % share, at % share + lanes)
            if pair == 0:
                lag_ref[slot, :, span] = value[0] * lag_scale
            else:
                lag_ref[slot, :, span] += value[0] * lag_scale

        forward(load_kind(0), mixed_spec)
        inverse(convolve, emit_kind(0))
        forward(load_kind(1), upstream_spec)
        inverse(correlate, emit_kind(1))
        inverse(lags, emit_lag)
    for step in range(shards):
        returned[step][...] = back_ref[me ^ step]


def output_kernel(query_ref, key_ref, value_ref, cotangent_ref, skip_ref, *refs):
    *home, output_ref, query_grad_ref, key_grad_ref, value_grad_ref, turned = refs
    _, batch, channels, tokens = home[0].shape
    me = lax.axis_index("seq")
    for step, block in enumerate(home):
        turned[me ^ step] = block[...]
    skip = skip_ref[...]

    def columns(kind, b):
        return jnp.transpose(turned[:, kind, b].reshape(len(home) * channels, tokens))

    for b in range(batch):
        query, key, value, cotangent = query_ref[b], key_ref[b], value_ref[b], cotangent_ref[b]
        hidden = columns(0, b) + skip * (key * value)
        output_ref[b] = query * hidden
        query_grad_ref[b] = cotangent * hidden
        mixed_grad = columns(1, b) + skip * (cotangent * query)
        key_grad_ref[b] = mixed_grad * value
        value_grad_ref[b] = mixed_grad * key


def exchange(blocks):
    shards = len(blocks)
    received = [blocks[0]] + [None] * (shards - 1)
    for step in range(shards - 1, 0, -1):
        pairs = [(source, source ^ step) for source in range(shards)]
        received[step] = lax.ppermute(blocks[step], "seq", pairs)
    return received


def per_device(query_gate, key_gate, value_input, filters, skip_gain, cotangent, *, shards, groups):
    batch, tokens, all_channels = query_gate.shape
    channels, length = filters.shape
    lanes = 128 if 2 * length // 128 <= 64 else tokens
    count = 2 * length // lanes
    twist, matrix = tables(count, lanes)
    params = pltpu.CompilerParams(vmem_limit_bytes=VMEM_BYTES)
    block = jax.ShapeDtypeStruct((2, batch, channels, tokens), jnp.float32)
    swap = pltpu.VMEM((shards, 2, batch, channels, tokens), jnp.float32)
    sent = pl.pallas_call(
        gate_kernel,
        out_shape=(block,) * shards,
        in_specs=[pl.BlockSpec(memory_space=pltpu.HBM)] * 4,
        scratch_shapes=[
            pltpu.VMEM((4, batch, tokens, all_channels), jnp.float32),
            swap,
            pltpu.SemaphoreType.DMA((4, batch)),
        ],
        compiler_params=params,
        name="gate",
    )(*(
        pltpu.with_memory_space_constraint(x, pltpu.HBM)
        for x in (query_gate, key_gate, value_input, cotangent)
    ))
    received = exchange(sent)
    spectrum = pltpu.VMEM((count, channels, 2 * lanes), jnp.float32)

    def body(*refs):
        spectral_kernel(shards, 1.0 / (2.0 * length * math.sqrt(length)), *refs)

    *returned, lag = pl.pallas_call(
        body,
        out_shape=(block,) * shards
        + (jax.ShapeDtypeStruct((groups, channels, length // groups), jnp.float32),),
        scratch_shapes=[swap] * 2 + [spectrum] * 5,
        compiler_params=params,
        name="spectral",
    )(filters, twist, matrix, *received)
    home = exchange(returned)
    filter_grad = lag[0]
    for step in range(1, groups):
        pairs = [(source, (source + step) % groups) for source in range(groups)]
        filter_grad = filter_grad + lax.ppermute(lag[step], "batch", pairs)
    token_out = jax.ShapeDtypeStruct(query_gate.shape, jnp.float32)
    output, query_grad, key_grad, value_grad = pl.pallas_call(
        output_kernel,
        out_shape=(token_out,) * 4,
        scratch_shapes=[swap],
        compiler_params=params,
        name="outputs",
    )(query_gate, key_gate, value_input, cotangent, skip_gain.reshape(1, all_channels), *home)
    return (output, query_grad, key_grad, value_grad, filter_grad)


def solution(mesh):
    in_specs = (
        P("batch", "seq", None),
        P("batch", "seq", None),
        P("batch", "seq", None),
        P("seq", None),
        P(),
        P("batch", "seq", None),
    )
    out_specs = (
        P("batch", "seq", None),
        P("batch", "seq", None),
        P("batch", "seq", None),
        P("batch", "seq", None),
        P("seq", "batch"),
    )
    shards, groups = mesh.shape["seq"], mesh.shape["batch"]

    def whole(*arrays):
        return per_device(*arrays, shards=shards, groups=groups)

    return jax.shard_map(whole, mesh=mesh, in_specs=in_specs, out_specs=out_specs, check_vma=False)
```

```python
import functools
import math

import jax
import jax.numpy as jnp
import ml_dtypes
import numpy as np
from jax import lax
from jax.experimental import pallas as pl
from jax.experimental.pallas import tpu as pltpu
from jax.sharding import PartitionSpec as P

VMEM_BYTES = 48 * 1024 * 1024
ROW_CHUNK = 128


def add(a, b):
    if a is None:
        return b
    if b is None:
        return a
    return a + b


def sub(a, b):
    if b is None:
        return a
    if a is None:
        return -b
    return a - b


def scale(a, factor):
    if a is None or factor == 1.0:
        return a
    if factor == -1.0:
        return -a
    return a * factor


def turn(x, step, period):
    if x is None:
        return None
    re, im = x
    step = step % period
    if (4 * step) % period == 0:
        quarter = 4 * step // period
        if quarter == 0:
            return (re, im)
        if quarter == 1:
            return (im, scale(re, -1.0))
        if quarter == 2:
            return (scale(re, -1.0), scale(im, -1.0))
        return (scale(im, -1.0), re)
    angle = -2.0 * math.pi * step / period
    c, s = math.cos(angle), math.sin(angle)
    if (8 * step) % period == 0:
        root = math.sqrt(0.5)
        total, difference = add(re, im), sub(re, im)
        if c * s > 0:
            return (scale(difference, math.copysign(root, c)), scale(total, math.copysign(root, c)))
        return (scale(total, math.copysign(root, c)), scale(sub(im, re), math.copysign(root, c)))
    return (sub(scale(re, c), scale(im, s)), add(scale(re, s), scale(im, c)))


def complex_add(x, y):
    if x is None:
        return y
    if y is None:
        return x
    return (add(x[0], y[0]), add(x[1], y[1]))


def complex_sub(x, y):
    if y is None:
        return x
    if x is None:
        return (scale(y[0], -1.0), scale(y[1], -1.0))
    return (sub(x[0], y[0]), sub(x[1], y[1]))


def small_dft(values):
    size = len(values)
    if size == 1:
        return list(values)
    even = small_dft(values[0::2])
    odd = small_dft(values[1::2])
    odd = [turn(value, step, size) for step, value in enumerate(odd)]
    return [complex_add(e, o) for e, o in zip(even, odd)] + [
        complex_sub(e, o) for e, o in zip(even, odd)
    ]


def factors_of(size):
    first = 1
    while first * first < size:
        first *= 2
    return (size // first, first)


def across_rows(load, emit, count, kept, store, fetch):
    first, second = factors_of(count)
    for b in range(second):
        values = small_dft([load(second * a + b) for a in range(first)])
        for p, value in enumerate(values):
            store(b, p, turn(value, b * p, count))
    for p in range(first):
        values = small_dft([fetch(b, p) for b in range(second)])
        for q, value in enumerate(values):
            k1 = p + first * q
            if k1 < kept:
                emit(k1, value)


def tables(count, lanes):
    k1 = np.arange(count)[:, None]
    n2 = np.arange(lanes)[None, :]
    phase = -2.0 * np.pi * ((k1 * n2) % (count * lanes)) / (count * lanes)
    twist = np.concatenate([np.cos(phase), np.sin(phase)], axis=1).astype(np.float32)
    j = np.arange(lanes)
    phase = -2.0 * np.pi * ((j[:, None] * j[None, :]) % lanes) / lanes
    c, s = np.cos(phase), np.sin(phase)
    matrix = np.block([[c, s], [-s, c]]).astype(np.float32)
    high = matrix.astype(ml_dtypes.bfloat16)
    low = (matrix - high.astype(np.float32)).astype(ml_dtypes.bfloat16)
    return twist, np.concatenate([high, high, low], axis=0)


def lane_dft(x, matrix):
    high = x.astype(jnp.bfloat16)
    low = (x - high.astype(jnp.float32)).astype(jnp.bfloat16)
    return jnp.dot(
        jnp.concatenate([high, low, high], axis=1), matrix, preferred_element_type=jnp.float32
    )


def gate_kernel(query_hbm, key_hbm, value_hbm, cotangent_hbm, mixed_ref, upstream_ref, held, sems):
    shards, batch, channels, tokens = mixed_ref.shape
    sources = (key_hbm, value_hbm, cotangent_hbm, query_hbm)

    def copy(b, i):
        return pltpu.make_async_copy(sources[i].at[b], held.at[i, b], sems.at[i, b])

    for i in range(4):
        for b in range(batch):
            copy(b, i).start()
    for kind, sent in enumerate((mixed_ref, upstream_ref)):
        for b in range(batch):
            copy(b, 2 * kind).wait()
            copy(b, 2 * kind + 1).wait()
            product = held[2 * kind, b] * held[2 * kind + 1, b]
            sent[:, b] = jnp.transpose(product).reshape(shards, channels, tokens)


def transforms(twist_ref, matrix_ref, middle, turned):
    count, channels, width = turned.shape
    lanes = width // 2
    first, _ = factors_of(count)
    per_chunk = ROW_CHUNK // channels
    chunks = [slice(at, min(at + per_chunk, count)) for at in range(0, count, per_chunk)]

    def store(b, p, value):
        re, im = value
        middle[b * first + p, :, :lanes] = jnp.zeros_like(im) if re is None else re
        middle[b * first + p, :, lanes:] = jnp.zeros_like(re) if im is None else im

    def fetch(b, p):
        return (middle[b * first + p, :, :lanes], middle[b * first + p, :, lanes:])

    def twist(k1, value):
        c, s = twist_ref[k1 : k1 + 1, :lanes], twist_ref[k1 : k1 + 1, lanes:]
        return (value[0] * c - value[1] * s, value[0] * s + value[1] * c)

    def place(k1, value):
        turned[k1, :, :lanes], turned[k1, :, lanes:] = twist(k1, value)

    def forward(load, spec):
        across_rows(load, place, count, count, store, fetch)
        for part in chunks:
            x = turned[part].reshape(-1, width)
            spec[part] = lane_dft(x, matrix_ref[...]).reshape(-1, channels, width)

    def inverse(left, right, conjugate_left, emit):
        for part in chunks:
            lr, li = left[part, :, :lanes], left[part, :, lanes:]
            rr, ri = right[part, :, :lanes], right[part, :, lanes:]
            if conjugate_left:
                re, im = lr * rr + li * ri, li * rr - lr * ri
            else:
                re, im = lr * rr - li * ri, -(lr * ri + li * rr)
            x = jnp.concatenate([re.reshape(-1, lanes), im.reshape(-1, lanes)], axis=1)
            turned[part] = lane_dft(x, matrix_ref[...]).reshape(-1, channels, width)

        def load(k1):
            return twist(k1, (turned[k1, :, :lanes], turned[k1, :, lanes:]))

        across_rows(load, emit, count, count // 2, store, fetch)

    return forward, inverse


def token_blocks(ref, lanes, pair, live):
    pieces = ref.shape[3] // lanes

    def where(n1):
        at = n1 % pieces * lanes
        return n1 // pieces, slice(at, at + lanes)

    def load(n1):
        if n1 >= live:
            return None
        shard, span = where(n1)
        return (ref[shard, 2 * pair, :, span], ref[shard, 2 * pair + 1, :, span])

    def emit(n1, value):
        shard, span = where(n1)
        ref[shard, 2 * pair, :, span] = value[0]
        ref[shard, 2 * pair + 1, :, span] = -value[1]

    return load, emit


def filter_kernel(filter_ref, twist_ref, matrix_ref, spec_ref, middle, turned):
    length = filter_ref.shape[1]
    lanes = twist_ref.shape[1] // 2
    forward, _ = transforms(twist_ref, matrix_ref, middle, turned)

    def load(n1):
        if n1 * lanes >= length:
            return None
        return (filter_ref[:, n1 * lanes : (n1 + 1) * lanes] * (0.5 / length), None)

    forward(load, spec_ref)


def convolve_kernel(
    conjugate, held_ref, filter_ref, twist_ref, matrix_ref, back_ref, spec_ref, middle, turned
):
    count, width = twist_ref.shape
    forward, inverse = transforms(twist_ref, matrix_ref, middle, turned)
    for pair in range(spec_ref.shape[0]):
        load, _ = token_blocks(held_ref, width // 2, pair, count // 2)
        _, emit = token_blocks(back_ref, width // 2, pair, count // 2)
        forward(load, spec_ref.at[pair])
        inverse(filter_ref, spec_ref.at[pair], conjugate, emit)


def lag_kernel(scaling, mixed_ref, upstream_ref, twist_ref, matrix_ref, lag_ref, middle, turned):
    lanes = twist_ref.shape[1] // 2
    groups, _, share = lag_ref.shape
    group = lax.axis_index("batch")
    _, inverse = transforms(twist_ref, matrix_ref, middle, turned)
    for pair in range(mixed_ref.shape[0]):

        def emit(n1, value):
            at = n1 * lanes
            slot = lax.rem(at // share - group + groups, groups)
            span = slice(at % share, at % share + lanes)
            if pair == 0:
                lag_ref[slot, :, span] = value[0] * scaling
            else:
                lag_ref[slot, :, span] += value[0] * scaling

        inverse(mixed_ref.at[pair], upstream_ref.at[pair], True, emit)


def output_kernel(
    query_ref, key_ref, value_ref, cotangent_ref, skip_ref, convolved_ref, back_ref,
    output_ref, query_grad_ref, key_grad_ref, value_grad_ref,
):
    shards, batch, channels, tokens = convolved_ref.shape
    skip = skip_ref[...]

    def rows(ref, b):
        return jnp.transpose(ref[:, b].reshape(shards * channels, tokens))

    for b in range(batch):
        query, key, value, cotangent = query_ref[b], key_ref[b], value_ref[b], cotangent_ref[b]
        hidden = rows(convolved_ref, b) + skip * (key * value)
        output_ref[b] = query * hidden
        query_grad_ref[b] = cotangent * hidden
        mixed_grad = rows(back_ref, b) + skip * (cotangent * query)
        key_grad_ref[b] = mixed_grad * value
        value_grad_ref[b] = mixed_grad * key


def exchange(blocks):
    return lax.all_to_all(blocks, "seq", split_axis=0, concat_axis=0, tiled=True)


def per_device(query_gate, key_gate, value_input, filters, skip_gain, cotangent, *, shards, groups):
    batch, tokens, all_channels = query_gate.shape
    channels, length = filters.shape
    lanes = 128 if 2 * length // 128 <= 64 else tokens
    count = 2 * length // lanes
    twist, matrix = tables(count, lanes)

    lane_work = 2 * 3 * count * channels * (2 * lanes) ** 2

    def of(*shape):
        return jax.ShapeDtypeStruct(shape, jnp.float32)

    def call(kernel, name, stages, out_shape, scratch, *arrays, **options):
        return pl.pallas_call(
            kernel,
            out_shape=out_shape,
            scratch_shapes=scratch,
            compiler_params=pltpu.CompilerParams(vmem_limit_bytes=VMEM_BYTES),
            cost_estimate=pl.CostEstimate(
                flops=stages * lane_work, bytes_accessed=stages * 4 * batch * channels * length,
                transcendentals=0,
            ),
            name=name,
            **options,
        )(*arrays)

    swap = of(shards, batch, channels, tokens)
    spectrum = of(batch // 2, count, channels, 2 * lanes)
    work = [pltpu.VMEM((count, channels, 2 * lanes), jnp.float32)] * 2
    mixed, upstream = call(
        gate_kernel,
        "gate", 1,
        (swap, swap),
        [
            pltpu.VMEM((4, batch, tokens, all_channels), jnp.float32),
            pltpu.SemaphoreType.DMA((4, batch)),
        ],
        *(
            pltpu.with_memory_space_constraint(x, pltpu.HBM)
            for x in (query_gate, key_gate, value_input, cotangent)
        ),
        in_specs=[pl.BlockSpec(memory_space=pltpu.HBM)] * 4,
    )
    mixed = exchange(mixed)
    upstream = exchange(upstream)
    filter_spec = call(
        filter_kernel, "filter", 2, of(count, channels, 2 * lanes), work, filters, twist, matrix
    )
    convolved, mixed_spec = call(
        functools.partial(convolve_kernel, False),
        "convolve", 4, (swap, spectrum), work, mixed, filter_spec, twist, matrix,
    )
    convolved = exchange(convolved)
    filter_spec, mixed_spec = lax.optimization_barrier((filter_spec, mixed_spec))
    back, upstream_spec = call(
        functools.partial(convolve_kernel, True),
        "correlate", 4, (swap, spectrum), work, upstream, filter_spec, twist, matrix,
    )
    back = exchange(back)
    lag = call(
        functools.partial(lag_kernel, 1.0 / (2.0 * length * math.sqrt(length))),
        "lags", 2, of(groups, channels, length // groups), work,
        mixed_spec, upstream_spec, twist, matrix,
    )
    filter_grad = lag[0]
    for step in range(1, groups):
        pairs = [(source, (source + step) % groups) for source in range(groups)]
        filter_grad = filter_grad + lax.ppermute(lag[step], "batch", pairs)
    output, query_grad, key_grad, value_grad = call(
        output_kernel,
        "outputs", 2, (of(*query_gate.shape),) * 4, [],
        query_gate, key_gate, value_input, cotangent, skip_gain.reshape(1, all_channels),
        convolved, back,
    )
    return (output, query_grad, key_grad, value_grad, filter_grad)


def solution(mesh):
    in_specs = (
        P("batch", "seq", None),
        P("batch", "seq", None),
        P("batch", "seq", None),
        P("seq", None),
        P(),
        P("batch", "seq", None),
    )
    out_specs = (
        P("batch", "seq", None),
        P("batch", "seq", None),
        P("batch", "seq", None),
        P("batch", "seq", None),
        P("seq", "batch"),
    )
    shards, groups = mesh.shape["seq"], mesh.shape["batch"]

    def whole(*arrays):
        return per_device(*arrays, shards=shards, groups=groups)

    return jax.shard_map(whole, mesh=mesh, in_specs=in_specs, out_specs=out_specs, check_vma=False)
```

```python
import functools
import math

import jax
import jax.numpy as jnp
import ml_dtypes
import numpy as np
from jax import lax
from jax.experimental import pallas as pl
from jax.experimental.pallas import tpu as pltpu
from jax.sharding import PartitionSpec as P

VMEM_BYTES = 48 * 1024 * 1024
ROW_CHUNK = 128


def add(a, b):
    if a is None:
        return b
    if b is None:
        return a
    return a + b


def sub(a, b):
    if b is None:
        return a
    if a is None:
        return -b
    return a - b


def scale(a, factor):
    if a is None or factor == 1.0:
        return a
    if factor == -1.0:
        return -a
    return a * factor


def turn(x, step, period):
    if x is None:
        return None
    re, im = x
    step = step % period
    if (4 * step) % period == 0:
        quarter = 4 * step // period
        if quarter == 0:
            return (re, im)
        if quarter == 1:
            return (im, scale(re, -1.0))
        if quarter == 2:
            return (scale(re, -1.0), scale(im, -1.0))
        return (scale(im, -1.0), re)
    angle = -2.0 * math.pi * step / period
    c, s = math.cos(angle), math.sin(angle)
    if (8 * step) % period == 0:
        root = math.sqrt(0.5)
        total, difference = add(re, im), sub(re, im)
        if c * s > 0:
            return (scale(difference, math.copysign(root, c)), scale(total, math.copysign(root, c)))
        return (scale(total, math.copysign(root, c)), scale(sub(im, re), math.copysign(root, c)))
    return (sub(scale(re, c), scale(im, s)), add(scale(re, s), scale(im, c)))


def complex_add(x, y):
    if x is None:
        return y
    if y is None:
        return x
    return (add(x[0], y[0]), add(x[1], y[1]))


def complex_sub(x, y):
    if y is None:
        return x
    if x is None:
        return (scale(y[0], -1.0), scale(y[1], -1.0))
    return (sub(x[0], y[0]), sub(x[1], y[1]))


def small_dft(values):
    size = len(values)
    if size == 1:
        return list(values)
    even = small_dft(values[0::2])
    odd = small_dft(values[1::2])
    odd = [turn(value, step, size) for step, value in enumerate(odd)]
    return [complex_add(e, o) for e, o in zip(even, odd)] + [
        complex_sub(e, o) for e, o in zip(even, odd)
    ]


def factors_of(size):
    first = 1
    while first * first < size:
        first *= 2
    return (size // first, first)


def across_rows(load, emit, count, kept, store, fetch):
    first, second = factors_of(count)
    for b in range(second):
        values = small_dft([load(second * a + b) for a in range(first)])
        for p, value in enumerate(values):
            store(b, p, turn(value, b * p, count))
    for p in range(first):
        values = small_dft([fetch(b, p) for b in range(second)])
        for q, value in enumerate(values):
            k1 = p + first * q
            if k1 < kept:
                emit(k1, value)


def tables(count, lanes):
    k1 = np.arange(count)[:, None]
    n2 = np.arange(lanes)[None, :]
    phase = -2.0 * np.pi * ((k1 * n2) % (count * lanes)) / (count * lanes)
    twist = np.concatenate([np.cos(phase), np.sin(phase)], axis=1).astype(np.float32)
    j = np.arange(lanes)
    phase = -2.0 * np.pi * ((j[:, None] * j[None, :]) % lanes) / lanes
    c, s = np.cos(phase), np.sin(phase)
    matrix = np.block([[c, s], [-s, c]]).astype(np.float32)
    high = matrix.astype(ml_dtypes.bfloat16)
    low = (matrix - high.astype(np.float32)).astype(ml_dtypes.bfloat16)
    return twist, np.concatenate([high, high, low], axis=0)


def lane_dft(x, matrix):
    high = x.astype(jnp.bfloat16)
    low = (x - high.astype(jnp.float32)).astype(jnp.bfloat16)
    return jnp.dot(
        jnp.concatenate([high, low, high], axis=1), matrix, preferred_element_type=jnp.float32
    )


def reversed_order(shards):
    width = shards.bit_length() - 1
    return [int(format(place, f"0{width}b")[::-1], 2) if width else 0 for place in range(shards)]


def gate_kernel(order, query_hbm, key_hbm, value_hbm, cotangent_hbm, sent_ref, held, sems):
    shards, _, batch, channels, tokens = sent_ref.shape
    sources = (key_hbm, value_hbm, cotangent_hbm, query_hbm)

    def copy(b, i):
        return pltpu.make_async_copy(sources[i].at[b], held.at[i, b], sems.at[i, b])

    for i in range(4):
        for b in range(batch):
            copy(b, i).start()
    for kind in range(2):
        for b in range(batch):
            copy(b, 2 * kind).wait()
            copy(b, 2 * kind + 1).wait()
            columns = jnp.transpose(held[2 * kind, b] * held[2 * kind + 1, b])
            for place, shard in enumerate(order):
                rows = columns[shard * channels : (shard + 1) * channels]
                sent_ref[place, kind, b] = rows


def transforms(twist_ref, matrix_ref, middle, turned):
    count, channels, width = turned.shape
    lanes = width // 2
    first, _ = factors_of(count)
    per_chunk = ROW_CHUNK // channels
    chunks = [slice(at, min(at + per_chunk, count)) for at in range(0, count, per_chunk)]

    def store(b, p, value):
        re, im = value
        middle[b * first + p, :, :lanes] = jnp.zeros_like(im) if re is None else re
        middle[b * first + p, :, lanes:] = jnp.zeros_like(re) if im is None else im

    def fetch(b, p):
        return (middle[b * first + p, :, :lanes], middle[b * first + p, :, lanes:])

    def twist(k1, value):
        c, s = twist_ref[k1 : k1 + 1, :lanes], twist_ref[k1 : k1 + 1, lanes:]
        return (value[0] * c - value[1] * s, value[0] * s + value[1] * c)

    def place(k1, value):
        turned[k1, :, :lanes], turned[k1, :, lanes:] = twist(k1, value)

    def forward(load, spec):
        across_rows(load, place, count, count, store, fetch)
        for part in chunks:
            x = turned[part].reshape(-1, width)
            spec[part] = lane_dft(x, matrix_ref[...]).reshape(-1, channels, width)

    def inverse(left, right, conjugate_left, emit):
        for part in chunks:
            lr, li = left[part, :, :lanes], left[part, :, lanes:]
            rr, ri = right[part, :, :lanes], right[part, :, lanes:]
            if conjugate_left:
                re, im = lr * rr + li * ri, li * rr - lr * ri
            else:
                re, im = lr * rr - li * ri, -(lr * ri + li * rr)
            x = jnp.concatenate([re.reshape(-1, lanes), im.reshape(-1, lanes)], axis=1)
            turned[part] = lane_dft(x, matrix_ref[...]).reshape(-1, channels, width)

        def load(k1):
            return twist(k1, (turned[k1, :, :lanes], turned[k1, :, lanes:]))

        across_rows(load, emit, count, count // 2, store, fetch)

    return forward, inverse


def token_blocks(ref, order, kind, lanes, pair, live):
    pieces = ref.shape[4] // lanes

    def where(n1):
        at = n1 % pieces * lanes
        return order.index(n1 // pieces), slice(at, at + lanes)

    def load(n1):
        if n1 >= live:
            return None
        place, span = where(n1)
        return (ref[place, kind, 2 * pair, :, span], ref[place, kind, 2 * pair + 1, :, span])

    def emit(n1, value):
        place, span = where(n1)
        ref[place, kind, 2 * pair, :, span] = value[0]
        ref[place, kind, 2 * pair + 1, :, span] = -value[1]

    return load, emit


def filter_kernel(filter_ref, twist_ref, matrix_ref, spec_ref, middle, turned):
    length = filter_ref.shape[1]
    lanes = twist_ref.shape[1] // 2
    forward, _ = transforms(twist_ref, matrix_ref, middle, turned)

    def load(n1):
        if n1 * lanes >= length:
            return None
        return (filter_ref[:, n1 * lanes : (n1 + 1) * lanes] * (0.5 / length), None)

    forward(load, spec_ref)


def convolve_kernel(
    order, held_ref, filter_ref, twist_ref, matrix_ref, back_ref, mixed_ref, upstream_ref, middle, turned
):
    count, width = twist_ref.shape
    forward, inverse = transforms(twist_ref, matrix_ref, middle, turned)
    for kind, spec_ref in enumerate((mixed_ref, upstream_ref)):
        for pair in range(spec_ref.shape[0]):
            load, _ = token_blocks(held_ref, order, kind, width // 2, pair, count // 2)
            _, emit = token_blocks(back_ref, order, kind, width // 2, pair, count // 2)
            forward(load, spec_ref.at[pair])
            inverse(filter_ref, spec_ref.at[pair], kind == 1, emit)


def lag_kernel(scaling, mixed_ref, upstream_ref, twist_ref, matrix_ref, lag_ref, middle, turned):
    lanes = twist_ref.shape[1] // 2
    groups, _, share = lag_ref.shape
    group = lax.axis_index("batch")
    _, inverse = transforms(twist_ref, matrix_ref, middle, turned)
    for pair in range(mixed_ref.shape[0]):

        def emit(n1, value):
            at = n1 * lanes
            slot = lax.rem(at // share - group + groups, groups)
            span = slice(at % share, at % share + lanes)
            if pair == 0:
                lag_ref[slot, :, span] = value[0] * scaling
            else:
                lag_ref[slot, :, span] += value[0] * scaling

        inverse(mixed_ref.at[pair], upstream_ref.at[pair], True, emit)


def output_kernel(
    order, query_ref, key_ref, value_ref, cotangent_ref, skip_ref, home_ref,
    output_ref, query_grad_ref, key_grad_ref, value_grad_ref,
):
    shards, _, batch, _, _ = home_ref.shape
    skip = skip_ref[...]

    def rows(kind, b):
        blocks = [home_ref[order.index(shard), kind, b] for shard in range(shards)]
        return jnp.transpose(jnp.concatenate(blocks, axis=0))

    for b in range(batch):
        query, key, value, cotangent = query_ref[b], key_ref[b], value_ref[b], cotangent_ref[b]
        hidden = rows(0, b) + skip * (key * value)
        output_ref[b] = query * hidden
        query_grad_ref[b] = cotangent * hidden
        mixed_grad = rows(1, b) + skip * (cotangent * query)
        key_grad_ref[b] = mixed_grad * value
        value_grad_ref[b] = mixed_grad * key


def per_device(query_gate, key_gate, value_input, filters, skip_gain, cotangent, *, shards, groups):
    batch, tokens, all_channels = query_gate.shape
    channels, length = filters.shape
    lanes = 128 if 2 * length // 128 <= 64 else tokens
    count = 2 * length // lanes
    twist, matrix = tables(count, lanes)
    order = reversed_order(shards)
    lane_work = 2 * 3 * count * channels * (2 * lanes) ** 2

    def of(*shape):
        return jax.ShapeDtypeStruct(shape, jnp.float32)

    def call(kernel, name, stages, out_shape, scratch, *arrays, **options):
        return pl.pallas_call(
            kernel,
            out_shape=out_shape,
            scratch_shapes=scratch,
            compiler_params=pltpu.CompilerParams(vmem_limit_bytes=VMEM_BYTES),
            cost_estimate=pl.CostEstimate(
                flops=stages * lane_work, bytes_accessed=stages * 4 * batch * channels * length,
                transcendentals=0,
            ),
            name=name,
            **options,
        )(*arrays)

    def exchange(blocks):
        return lax.all_to_all(
            blocks, "seq", split_axis=0, concat_axis=0, tiled=True, axis_index_groups=[order]
        )

    swap = of(shards, 2, batch, channels, tokens)
    spectrum = of(batch // 2, count, channels, 2 * lanes)
    work = [pltpu.VMEM((count, channels, 2 * lanes), jnp.float32)] * 2
    sent = call(
        functools.partial(gate_kernel, order),
        "gate", 1, swap,
        [
            pltpu.VMEM((4, batch, tokens, all_channels), jnp.float32),
            pltpu.SemaphoreType.DMA((4, batch)),
        ],
        *(
            pltpu.with_memory_space_constraint(x, pltpu.HBM)
            for x in (query_gate, key_gate, value_input, cotangent)
        ),
        in_specs=[pl.BlockSpec(memory_space=pltpu.HBM)] * 4,
    )
    held = exchange(sent)
    filter_spec = call(
        filter_kernel, "filter", 2, of(count, channels, 2 * lanes), work, filters, twist, matrix
    )
    back, mixed_spec, upstream_spec = call(
        functools.partial(convolve_kernel, order),
        "convolve", 8, (swap, spectrum, spectrum), work, held, filter_spec, twist, matrix,
    )
    home = exchange(back)
    lag = call(
        functools.partial(lag_kernel, 1.0 / (2.0 * length * math.sqrt(length))),
        "lags", 2, of(groups, channels, length // groups), work,
        mixed_spec, upstream_spec, twist, matrix,
    )
    filter_grad = lag[0]
    for step in range(1, groups):
        pairs = [(source, (source + step) % groups) for source in range(groups)]
        filter_grad = filter_grad + lax.ppermute(lag[step], "batch", pairs)
    output, query_grad, key_grad, value_grad = call(
        functools.partial(output_kernel, order),
        "outputs", 2, (of(*query_gate.shape),) * 4, [],
        query_gate, key_gate, value_input, cotangent, skip_gain.reshape(1, all_channels),
        home,
    )
    return (output, query_grad, key_grad, value_grad, filter_grad)


def solution(mesh):
    in_specs = (
        P("batch", "seq", None),
        P("batch", "seq", None),
        P("batch", "seq", None),
        P("seq", None),
        P(),
        P("batch", "seq", None),
    )
    out_specs = (
        P("batch", "seq", None),
        P("batch", "seq", None),
        P("batch", "seq", None),
        P("batch", "seq", None),
        P("seq", "batch"),
    )
    shards, groups = mesh.shape["seq"], mesh.shape["batch"]

    def whole(*arrays):
        return per_device(*arrays, shards=shards, groups=groups)

    return jax.shard_map(whole, mesh=mesh, in_specs=in_specs, out_specs=out_specs, check_vma=False)
```

```python
import functools
import math

import jax
import jax.numpy as jnp
import ml_dtypes
import numpy as np
from jax import lax
from jax.experimental import pallas as pl
from jax.experimental.pallas import tpu as pltpu
from jax.sharding import PartitionSpec as P

VMEM_BYTES = 48 * 1024 * 1024
ROW_CHUNK = 128


def add(a, b):
    if a is None:
        return b
    if b is None:
        return a
    return a + b


def sub(a, b):
    if b is None:
        return a
    if a is None:
        return -b
    return a - b


def scale(a, factor):
    if a is None or factor == 1.0:
        return a
    if factor == -1.0:
        return -a
    return a * factor


def turn(x, step, period):
    if x is None:
        return None
    re, im = x
    step = step % period
    if (4 * step) % period == 0:
        quarter = 4 * step // period
        if quarter == 0:
            return (re, im)
        if quarter == 1:
            return (im, scale(re, -1.0))
        if quarter == 2:
            return (scale(re, -1.0), scale(im, -1.0))
        return (scale(im, -1.0), re)
    angle = -2.0 * math.pi * step / period
    c, s = math.cos(angle), math.sin(angle)
    if (8 * step) % period == 0:
        root = math.sqrt(0.5)
        total, difference = add(re, im), sub(re, im)
        if c * s > 0:
            return (scale(difference, math.copysign(root, c)), scale(total, math.copysign(root, c)))
        return (scale(total, math.copysign(root, c)), scale(sub(im, re), math.copysign(root, c)))
    return (sub(scale(re, c), scale(im, s)), add(scale(re, s), scale(im, c)))


def complex_add(x, y):
    if x is None:
        return y
    if y is None:
        return x
    return (add(x[0], y[0]), add(x[1], y[1]))


def complex_sub(x, y):
    if y is None:
        return x
    if x is None:
        return (scale(y[0], -1.0), scale(y[1], -1.0))
    return (sub(x[0], y[0]), sub(x[1], y[1]))


def small_dft(values):
    size = len(values)
    if size == 1:
        return list(values)
    even = small_dft(values[0::2])
    odd = small_dft(values[1::2])
    odd = [turn(value, step, size) for step, value in enumerate(odd)]
    return [complex_add(e, o) for e, o in zip(even, odd)] + [
        complex_sub(e, o) for e, o in zip(even, odd)
    ]


def factors_of(size):
    first = 1
    while first * first < size:
        first *= 2
    return (size // first, first)


def across_rows(load, emit, count, kept, store, fetch):
    first, second = factors_of(count)
    for b in range(second):
        values = small_dft([load(second * a + b) for a in range(first)])
        for p, value in enumerate(values):
            store(b, p, turn(value, b * p, count))
    for p in range(first):
        values = small_dft([fetch(b, p) for b in range(second)])
        for q, value in enumerate(values):
            k1 = p + first * q
            if k1 < kept:
                emit(k1, value)


def tables(count, lanes):
    k1 = np.arange(count)[:, None]
    n2 = np.arange(lanes)[None, :]
    phase = -2.0 * np.pi * ((k1 * n2) % (count * lanes)) / (count * lanes)
    twist = np.concatenate([np.cos(phase), np.sin(phase)], axis=1).astype(np.float32)
    j = np.arange(lanes)
    phase = -2.0 * np.pi * ((j[:, None] * j[None, :]) % lanes) / lanes
    c, s = np.cos(phase), np.sin(phase)
    matrix = np.block([[c, s], [-s, c]]).astype(np.float32)
    high = matrix.astype(ml_dtypes.bfloat16)
    low = (matrix - high.astype(np.float32)).astype(ml_dtypes.bfloat16)
    return twist, np.concatenate([high, high, low], axis=0)


def lane_dft(x, matrix):
    high = x.astype(jnp.bfloat16)
    low = (x - high.astype(jnp.float32)).astype(jnp.bfloat16)
    return jnp.dot(
        jnp.concatenate([high, low, high], axis=1), matrix, preferred_element_type=jnp.float32
    )


def spread_order(shards):
    return [5 * place % shards for place in range(shards)]


def gate_kernel(order, query_hbm, key_hbm, value_hbm, cotangent_hbm, sent_ref, held, sems):
    shards, _, batch, channels, tokens = sent_ref.shape
    sources = (key_hbm, value_hbm, cotangent_hbm, query_hbm)

    def copy(b, i):
        return pltpu.make_async_copy(sources[i].at[b], held.at[i, b], sems.at[i, b])

    for i in range(4):
        for b in range(batch):
            copy(b, i).start()
    for kind in range(2):
        for b in range(batch):
            copy(b, 2 * kind).wait()
            copy(b, 2 * kind + 1).wait()
            columns = jnp.transpose(held[2 * kind, b] * held[2 * kind + 1, b])
            for place, shard in enumerate(order):
                rows = columns[shard * channels : (shard + 1) * channels]
                sent_ref[place, kind, b] = rows


def transforms(twist_ref, matrix_ref, middle, turned):
    count, channels, width = turned.shape
    lanes = width // 2
    first, _ = factors_of(count)
    per_chunk = ROW_CHUNK // channels
    chunks = [slice(at, min(at + per_chunk, count)) for at in range(0, count, per_chunk)]

    def store(b, p, value):
        re, im = value
        middle[b * first + p, :, :lanes] = jnp.zeros_like(im) if re is None else re
        middle[b * first + p, :, lanes:] = jnp.zeros_like(re) if im is None else im

    def fetch(b, p):
        return (middle[b * first + p, :, :lanes], middle[b * first + p, :, lanes:])

    def twist(k1, value):
        c, s = twist_ref[k1 : k1 + 1, :lanes], twist_ref[k1 : k1 + 1, lanes:]
        return (value[0] * c - value[1] * s, value[0] * s + value[1] * c)

    def place(k1, value):
        turned[k1, :, :lanes], turned[k1, :, lanes:] = twist(k1, value)

    def forward(load, spec):
        across_rows(load, place, count, count, store, fetch)
        for part in chunks:
            x = turned[part].reshape(-1, width)
            spec[part] = lane_dft(x, matrix_ref[...]).reshape(-1, channels, width)

    def inverse(left, right, conjugate_left, emit):
        for part in chunks:
            lr, li = left[part, :, :lanes], left[part, :, lanes:]
            rr, ri = right[part, :, :lanes], right[part, :, lanes:]
            if conjugate_left:
                re, im = lr * rr + li * ri, li * rr - lr * ri
            else:
                re, im = lr * rr - li * ri, -(lr * ri + li * rr)
            x = jnp.concatenate([re.reshape(-1, lanes), im.reshape(-1, lanes)], axis=1)
            turned[part] = lane_dft(x, matrix_ref[...]).reshape(-1, channels, width)

        def load(k1):
            return twist(k1, (turned[k1, :, :lanes], turned[k1, :, lanes:]))

        across_rows(load, emit, count, count // 2, store, fetch)

    return forward, inverse


def token_blocks(ref, order, kind, lanes, pair, live):
    pieces = ref.shape[4] // lanes

    def where(n1):
        at = n1 % pieces * lanes
        return order.index(n1 // pieces), slice(at, at + lanes)

    def load(n1):
        if n1 >= live:
            return None
        place, span = where(n1)
        return (ref[place, kind, 2 * pair, :, span], ref[place, kind, 2 * pair + 1, :, span])

    def emit(n1, value):
        place, span = where(n1)
        ref[place, kind, 2 * pair, :, span] = value[0]
        ref[place, kind, 2 * pair + 1, :, span] = -value[1]

    return load, emit


def filter_kernel(filter_ref, twist_ref, matrix_ref, spec_ref, middle, turned):
    length = filter_ref.shape[1]
    lanes = twist_ref.shape[1] // 2
    forward, _ = transforms(twist_ref, matrix_ref, middle, turned)

    def load(n1):
        if n1 * lanes >= length:
            return None
        return (filter_ref[:, n1 * lanes : (n1 + 1) * lanes] * (0.5 / length), None)

    forward(load, spec_ref)


def convolve_kernel(
    order, held_ref, filter_ref, twist_ref, matrix_ref, back_ref, mixed_ref, upstream_ref, middle, turned
):
    count, width = twist_ref.shape
    forward, inverse = transforms(twist_ref, matrix_ref, middle, turned)
    for kind, spec_ref in enumerate((mixed_ref, upstream_ref)):
        for pair in range(spec_ref.shape[0]):
            load, _ = token_blocks(held_ref, order, kind, width // 2, pair, count // 2)
            _, emit = token_blocks(back_ref, order, kind, width // 2, pair, count // 2)
            forward(load, spec_ref.at[pair])
            inverse(filter_ref, spec_ref.at[pair], kind == 1, emit)


def lag_kernel(scaling, mixed_ref, upstream_ref, twist_ref, matrix_ref, lag_ref, middle, turned):
    lanes = twist_ref.shape[1] // 2
    groups, _, share = lag_ref.shape
    group = lax.axis_index("batch")
    _, inverse = transforms(twist_ref, matrix_ref, middle, turned)
    for pair in range(mixed_ref.shape[0]):

        def emit(n1, value):
            at = n1 * lanes
            slot = lax.rem(at // share - group + groups, groups)
            span = slice(at % share, at % share + lanes)
            if pair == 0:
                lag_ref[slot, :, span] = value[0] * scaling
            else:
                lag_ref[slot, :, span] += value[0] * scaling

        inverse(mixed_ref.at[pair], upstream_ref.at[pair], True, emit)


def output_kernel(
    order, query_ref, key_ref, value_ref, cotangent_ref, skip_ref, home_ref,
    output_ref, query_grad_ref, key_grad_ref, value_grad_ref,
):
    shards, _, batch, _, _ = home_ref.shape
    skip = skip_ref[...]

    def rows(kind, b):
        blocks = [home_ref[order.index(shard), kind, b] for shard in range(shards)]
        return jnp.transpose(jnp.concatenate(blocks, axis=0))

    for b in range(batch):
        query, key, value, cotangent = query_ref[b], key_ref[b], value_ref[b], cotangent_ref[b]
        hidden = rows(0, b) + skip * (key * value)
        output_ref[b] = query * hidden
        query_grad_ref[b] = cotangent * hidden
        mixed_grad = rows(1, b) + skip * (cotangent * query)
        key_grad_ref[b] = mixed_grad * value
        value_grad_ref[b] = mixed_grad * key


def per_device(query_gate, key_gate, value_input, filters, skip_gain, cotangent, *, shards, groups):
    batch, tokens, all_channels = query_gate.shape
    channels, length = filters.shape
    lanes = 128 if 2 * length // 128 <= 64 else tokens
    count = 2 * length // lanes
    twist, matrix = tables(count, lanes)
    order = spread_order(shards)
    lane_work = 2 * 3 * count * channels * (2 * lanes) ** 2

    def of(*shape):
        return jax.ShapeDtypeStruct(shape, jnp.float32)

    def call(kernel, name, stages, out_shape, scratch, *arrays, **options):
        return pl.pallas_call(
            kernel,
            out_shape=out_shape,
            scratch_shapes=scratch,
            compiler_params=pltpu.CompilerParams(vmem_limit_bytes=VMEM_BYTES),
            cost_estimate=pl.CostEstimate(
                flops=stages * lane_work, bytes_accessed=stages * 4 * batch * channels * length,
                transcendentals=0,
            ),
            name=name,
            **options,
        )(*arrays)

    def exchange(blocks):
        return lax.all_to_all(
            blocks, "seq", split_axis=0, concat_axis=0, tiled=True, axis_index_groups=[order]
        )

    swap = of(shards, 2, batch, channels, tokens)
    spectrum = of(batch // 2, count, channels, 2 * lanes)
    work = [pltpu.VMEM((count, channels, 2 * lanes), jnp.float32)] * 2
    sent = call(
        functools.partial(gate_kernel, order),
        "gate", 1, swap,
        [
            pltpu.VMEM((4, batch, tokens, all_channels), jnp.float32),
            pltpu.SemaphoreType.DMA((4, batch)),
        ],
        *(
            pltpu.with_memory_space_constraint(x, pltpu.HBM)
            for x in (query_gate, key_gate, value_input, cotangent)
        ),
        in_specs=[pl.BlockSpec(memory_space=pltpu.HBM)] * 4,
    )
    held = exchange(sent)
    filter_spec = call(
        filter_kernel, "filter", 2, of(count, channels, 2 * lanes), work, filters, twist, matrix
    )
    back, mixed_spec, upstream_spec = call(
        functools.partial(convolve_kernel, order),
        "convolve", 8, (swap, spectrum, spectrum), work, held, filter_spec, twist, matrix,
    )
    home = exchange(back)
    lag = call(
        functools.partial(lag_kernel, 1.0 / (2.0 * length * math.sqrt(length))),
        "lags", 2, of(groups, channels, length // groups), work,
        mixed_spec, upstream_spec, twist, matrix,
    )
    filter_grad = lag[0]
    for step in range(1, groups):
        pairs = [(source, (source + step) % groups) for source in range(groups)]
        filter_grad = filter_grad + lax.ppermute(lag[step], "batch", pairs)
    output, query_grad, key_grad, value_grad = call(
        functools.partial(output_kernel, order),
        "outputs", 2, (of(*query_gate.shape),) * 4, [],
        query_gate, key_gate, value_input, cotangent, skip_gain.reshape(1, all_channels),
        home,
    )
    return (output, query_grad, key_grad, value_grad, filter_grad)


def solution(mesh):
    in_specs = (
        P("batch", "seq", None),
        P("batch", "seq", None),
        P("batch", "seq", None),
        P("seq", None),
        P(),
        P("batch", "seq", None),
    )
    out_specs = (
        P("batch", "seq", None),
        P("batch", "seq", None),
        P("batch", "seq", None),
        P("batch", "seq", None),
        P("seq", "batch"),
    )
    shards, groups = mesh.shape["seq"], mesh.shape["batch"]

    def whole(*arrays):
        return per_device(*arrays, shards=shards, groups=groups)

    return jax.shard_map(whole, mesh=mesh, in_specs=in_specs, out_specs=out_specs, check_vma=False)
```

```python
import functools
import math

import jax
import jax.numpy as jnp
import ml_dtypes
import numpy as np
from jax import lax
from jax.experimental import pallas as pl
from jax.experimental.pallas import tpu as pltpu
from jax.sharding import PartitionSpec as P

VMEM_BYTES = 48 * 1024 * 1024
ROW_CHUNK = 128


def add(a, b):
    if a is None:
        return b
    if b is None:
        return a
    return a + b


def sub(a, b):
    if b is None:
        return a
    if a is None:
        return -b
    return a - b


def scale(a, factor):
    if a is None or factor == 1.0:
        return a
    if factor == -1.0:
        return -a
    return a * factor


def turn(x, step, period):
    if x is None:
        return None
    re, im = x
    step = step % period
    if (4 * step) % period == 0:
        quarter = 4 * step // period
        if quarter == 0:
            return (re, im)
        if quarter == 1:
            return (im, scale(re, -1.0))
        if quarter == 2:
            return (scale(re, -1.0), scale(im, -1.0))
        return (scale(im, -1.0), re)
    angle = -2.0 * math.pi * step / period
    c, s = math.cos(angle), math.sin(angle)
    if (8 * step) % period == 0:
        root = math.sqrt(0.5)
        total, difference = add(re, im), sub(re, im)
        if c * s > 0:
            return (scale(difference, math.copysign(root, c)), scale(total, math.copysign(root, c)))
        return (scale(total, math.copysign(root, c)), scale(sub(im, re), math.copysign(root, c)))
    return (sub(scale(re, c), scale(im, s)), add(scale(re, s), scale(im, c)))


def complex_add(x, y):
    if x is None:
        return y
    if y is None:
        return x
    return (add(x[0], y[0]), add(x[1], y[1]))


def complex_sub(x, y):
    if y is None:
        return x
    if x is None:
        return (scale(y[0], -1.0), scale(y[1], -1.0))
    return (sub(x[0], y[0]), sub(x[1], y[1]))


def small_dft(values):
    size = len(values)
    if size == 1:
        return list(values)
    even = small_dft(values[0::2])
    odd = small_dft(values[1::2])
    odd = [turn(value, step, size) for step, value in enumerate(odd)]
    return [complex_add(e, o) for e, o in zip(even, odd)] + [
        complex_sub(e, o) for e, o in zip(even, odd)
    ]


def factors_of(size):
    first = 1
    while first * first < size:
        first *= 2
    return (size // first, first)


def across_rows(load, emit, count, kept, store, fetch):
    first, second = factors_of(count)
    for b in range(second):
        values = small_dft([load(second * a + b) for a in range(first)])
        for p, value in enumerate(values):
            store(b, p, turn(value, b * p, count))
    for p in range(first):
        values = small_dft([fetch(b, p) for b in range(second)])
        for q, value in enumerate(values):
            k1 = p + first * q
            if k1 < kept:
                emit(k1, value)


def tables(count, lanes):
    k1 = np.arange(count)[:, None]
    n2 = np.arange(lanes)[None, :]
    phase = -2.0 * np.pi * ((k1 * n2) % (count * lanes)) / (count * lanes)
    twist = np.concatenate([np.cos(phase), np.sin(phase)], axis=1).astype(np.float32)
    j = np.arange(lanes)
    phase = -2.0 * np.pi * ((j[:, None] * j[None, :]) % lanes) / lanes
    c, s = np.cos(phase), np.sin(phase)
    matrix = np.block([[c, s], [-s, c]]).astype(np.float32)
    high = matrix.astype(ml_dtypes.bfloat16)
    low = (matrix - high.astype(np.float32)).astype(ml_dtypes.bfloat16)
    return twist, np.concatenate([high, high, low], axis=0)


def lane_dft(x, matrix):
    high = x.astype(jnp.bfloat16)
    low = (x - high.astype(jnp.float32)).astype(jnp.bfloat16)
    return jnp.dot(
        jnp.concatenate([high, low, high], axis=1), matrix, preferred_element_type=jnp.float32
    )


def near_base(me, shards):
    return me // (shards // 2) * (shards // 2)


def gate_kernel(query_hbm, key_hbm, value_hbm, cotangent_hbm, near_ref, *refs):
    *far, blocks, held, sems = refs
    shards, _, batch, channels, tokens = blocks.shape
    me = lax.axis_index("seq")
    sources = (key_hbm, value_hbm, cotangent_hbm, query_hbm)

    def copy(b, i):
        return pltpu.make_async_copy(sources[i].at[b], held.at[i, b], sems.at[i, b])

    for i in range(4):
        for b in range(batch):
            copy(b, i).start()
    for kind in range(2):
        for b in range(batch):
            copy(b, 2 * kind).wait()
            copy(b, 2 * kind + 1).wait()
            product = held[2 * kind, b] * held[2 * kind + 1, b]
            blocks[:, kind, b] = jnp.transpose(product).reshape(shards, channels, tokens)
    hand_out(blocks, me, near_ref, far)


def hand_out(blocks, me, near_ref, far):
    shards = blocks.shape[0]
    near_ref[...] = blocks[pl.ds(near_base(me, shards), shards // 2)]
    for i, ref in enumerate(far):
        ref[...] = blocks[me ^ (shards // 2 + i)]


def take_in(blocks, me, near_ref, far):
    shards = blocks.shape[0]
    blocks[pl.ds(near_base(me, shards), shards // 2)] = near_ref[...]
    for i, ref in enumerate(far):
        blocks[me ^ (shards // 2 + i)] = ref[...]


def transforms(twist_ref, matrix_ref, middle, turned):
    count, channels, width = turned.shape
    lanes = width // 2
    first, _ = factors_of(count)
    per_chunk = ROW_CHUNK // channels
    chunks = [slice(at, min(at + per_chunk, count)) for at in range(0, count, per_chunk)]

    def store(b, p, value):
        re, im = value
        middle[b * first + p, :, :lanes] = jnp.zeros_like(im) if re is None else re
        middle[b * first + p, :, lanes:] = jnp.zeros_like(re) if im is None else im

    def fetch(b, p):
        return (middle[b * first + p, :, :lanes], middle[b * first + p, :, lanes:])

    def twist(k1, value):
        c, s = twist_ref[k1 : k1 + 1, :lanes], twist_ref[k1 : k1 + 1, lanes:]
        return (value[0] * c - value[1] * s, value[0] * s + value[1] * c)

    def place(k1, value):
        turned[k1, :, :lanes], turned[k1, :, lanes:] = twist(k1, value)

    def forward(load, spec):
        across_rows(load, place, count, count, store, fetch)
        for part in chunks:
            x = turned[part].reshape(-1, width)
            spec[part] = lane_dft(x, matrix_ref[...]).reshape(-1, channels, width)

    def inverse(left, right, conjugate_left, emit):
        for part in chunks:
            lr, li = left[part, :, :lanes], left[part, :, lanes:]
            rr, ri = right[part, :, :lanes], right[part, :, lanes:]
            if conjugate_left:
                re, im = lr * rr + li * ri, li * rr - lr * ri
            else:
                re, im = lr * rr - li * ri, -(lr * ri + li * rr)
            x = jnp.concatenate([re.reshape(-1, lanes), im.reshape(-1, lanes)], axis=1)
            turned[part] = lane_dft(x, matrix_ref[...]).reshape(-1, channels, width)

        def load(k1):
            return twist(k1, (turned[k1, :, :lanes], turned[k1, :, lanes:]))

        across_rows(load, emit, count, count // 2, store, fetch)

    return forward, inverse


def token_blocks(ref, kind, lanes, pair, live):
    pieces = ref.shape[4] // lanes

    def where(n1):
        at = n1 % pieces * lanes
        return n1 // pieces, slice(at, at + lanes)

    def load(n1):
        if n1 >= live:
            return None
        shard, span = where(n1)
        return (ref[shard, kind, 2 * pair, :, span], ref[shard, kind, 2 * pair + 1, :, span])

    def emit(n1, value):
        shard, span = where(n1)
        ref[shard, kind, 2 * pair, :, span] = value[0]
        ref[shard, kind, 2 * pair + 1, :, span] = -value[1]

    return load, emit


def filter_kernel(filter_ref, twist_ref, matrix_ref, spec_ref, middle, turned):
    length = filter_ref.shape[1]
    lanes = twist_ref.shape[1] // 2
    forward, _ = transforms(twist_ref, matrix_ref, middle, turned)

    def load(n1):
        if n1 * lanes >= length:
            return None
        return (filter_ref[:, n1 * lanes : (n1 + 1) * lanes] * (0.5 / length), None)

    forward(load, spec_ref)


def convolve_kernel(far, filter_ref, twist_ref, matrix_ref, near_ref, *refs):
    far_refs, refs = refs[:far], refs[far:]
    near_back, refs = refs[0], refs[1:]
    far_back, refs = refs[:far], refs[far:]
    mixed_ref, upstream_ref, held_ref, back_ref, middle, turned = refs
    me = lax.axis_index("seq")
    take_in(held_ref, me, near_ref, far_refs)
    count, width = twist_ref.shape
    forward, inverse = transforms(twist_ref, matrix_ref, middle, turned)
    for kind, spec_ref in enumerate((mixed_ref, upstream_ref)):
        for pair in range(spec_ref.shape[0]):
            load, _ = token_blocks(held_ref, kind, width // 2, pair, count // 2)
            _, emit = token_blocks(back_ref, kind, width // 2, pair, count // 2)
            forward(load, spec_ref.at[pair])
            inverse(filter_ref, spec_ref.at[pair], kind == 1, emit)
    hand_out(back_ref, me, near_back, far_back)


def lag_kernel(scaling, mixed_ref, upstream_ref, twist_ref, matrix_ref, lag_ref, middle, turned):
    lanes = twist_ref.shape[1] // 2
    groups, _, share = lag_ref.shape
    group = lax.axis_index("batch")
    _, inverse = transforms(twist_ref, matrix_ref, middle, turned)
    for pair in range(mixed_ref.shape[0]):

        def emit(n1, value):
            at = n1 * lanes
            slot = lax.rem(at // share - group + groups, groups)
            span = slice(at % share, at % share + lanes)
            if pair == 0:
                lag_ref[slot, :, span] = value[0] * scaling
            else:
                lag_ref[slot, :, span] += value[0] * scaling

        inverse(mixed_ref.at[pair], upstream_ref.at[pair], True, emit)


def output_kernel(query_ref, key_ref, value_ref, cotangent_ref, skip_ref, near_ref, *refs):
    *far, output_ref, query_grad_ref, key_grad_ref, value_grad_ref, home_ref = refs
    shards, _, batch, channels, tokens = home_ref.shape
    take_in(home_ref, lax.axis_index("seq"), near_ref, far)
    skip = skip_ref[...]

    def rows(kind, b):
        return jnp.transpose(home_ref[:, kind, b].reshape(shards * channels, tokens))

    for b in range(batch):
        query, key, value, cotangent = query_ref[b], key_ref[b], value_ref[b], cotangent_ref[b]
        hidden = rows(0, b) + skip * (key * value)
        output_ref[b] = query * hidden
        query_grad_ref[b] = cotangent * hidden
        mixed_grad = rows(1, b) + skip * (cotangent * query)
        key_grad_ref[b] = mixed_grad * value
        value_grad_ref[b] = mixed_grad * key


def per_device(query_gate, key_gate, value_input, filters, skip_gain, cotangent, *, shards, groups):
    batch, tokens, all_channels = query_gate.shape
    channels, length = filters.shape
    lanes = 128 if 2 * length // 128 <= 64 else tokens
    count = 2 * length // lanes
    twist, matrix = tables(count, lanes)
    half = shards // 2
    lane_work = 2 * 3 * count * channels * (2 * lanes) ** 2

    def of(*shape):
        return jax.ShapeDtypeStruct(shape, jnp.float32)

    def call(kernel, name, stages, out_shape, scratch, *arrays, **options):
        return pl.pallas_call(
            kernel,
            out_shape=out_shape,
            scratch_shapes=scratch,
            compiler_params=pltpu.CompilerParams(vmem_limit_bytes=VMEM_BYTES),
            cost_estimate=pl.CostEstimate(
                flops=stages * lane_work, bytes_accessed=stages * 4 * batch * channels * length,
                transcendentals=0,
            ),
            name=name,
            **options,
        )(*arrays)

    def exchange(near, *far):
        groups_of = [list(range(first, first + half)) for first in (0, half)]
        near = lax.all_to_all(
            near, "seq", split_axis=0, concat_axis=0, tiled=True, axis_index_groups=groups_of
        )
        steps = enumerate(far, half)
        far = [
            lax.ppermute(block, "seq", [(source, source ^ step) for source in range(shards)])
            for step, block in steps
        ]
        return near, *far

    block = (2, batch, channels, tokens)
    moved = (of(half, *block),) + (of(*block),) * half
    whole = pltpu.VMEM((shards,) + block, jnp.float32)
    spectrum = of(batch // 2, count, channels, 2 * lanes)
    work = [pltpu.VMEM((count, channels, 2 * lanes), jnp.float32)] * 2
    sent = call(
        gate_kernel,
        "gate", 1, moved,
        [
            whole,
            pltpu.VMEM((4, batch, tokens, all_channels), jnp.float32),
            pltpu.SemaphoreType.DMA((4, batch)),
        ],
        *(
            pltpu.with_memory_space_constraint(x, pltpu.HBM)
            for x in (query_gate, key_gate, value_input, cotangent)
        ),
        in_specs=[pl.BlockSpec(memory_space=pltpu.HBM)] * 4,
    )
    held = exchange(*sent)
    filter_spec = call(
        filter_kernel, "filter", 2, of(count, channels, 2 * lanes), work, filters, twist, matrix
    )
    *back, mixed_spec, upstream_spec = call(
        functools.partial(convolve_kernel, half),
        "convolve", 8, moved + (spectrum, spectrum), [whole, whole] + work,
        filter_spec, twist, matrix, *held,
    )
    home = exchange(*back)
    lag = call(
        functools.partial(lag_kernel, 1.0 / (2.0 * length * math.sqrt(length))),
        "lags", 2, of(groups, channels, length // groups), work,
        mixed_spec, upstream_spec, twist, matrix,
    )
    filter_grad = lag[0]
    for step in range(1, groups):
        pairs = [(source, (source + step) % groups) for source in range(groups)]
        filter_grad = filter_grad + lax.ppermute(lag[step], "batch", pairs)
    output, query_grad, key_grad, value_grad = call(
        output_kernel,
        "outputs", 2, (of(*query_gate.shape),) * 4, [whole],
        query_gate, key_gate, value_input, cotangent, skip_gain.reshape(1, all_channels),
        *home,
    )
    return (output, query_grad, key_grad, value_grad, filter_grad)


def solution(mesh):
    in_specs = (
        P("batch", "seq", None),
        P("batch", "seq", None),
        P("batch", "seq", None),
        P("seq", None),
        P(),
        P("batch", "seq", None),
    )
    out_specs = (
        P("batch", "seq", None),
        P("batch", "seq", None),
        P("batch", "seq", None),
        P("batch", "seq", None),
        P("seq", "batch"),
    )
    shards, groups = mesh.shape["seq"], mesh.shape["batch"]

    def whole(*arrays):
        return per_device(*arrays, shards=shards, groups=groups)

    return jax.shard_map(whole, mesh=mesh, in_specs=in_specs, out_specs=out_specs, check_vma=False)
```

```python
import functools
import math

import jax
import jax.numpy as jnp
import ml_dtypes
import numpy as np
from jax import lax
from jax.experimental import pallas as pl
from jax.experimental.pallas import tpu as pltpu
from jax.sharding import PartitionSpec as P

VMEM_BYTES = 48 * 1024 * 1024
ROW_CHUNK = 128


def add(a, b):
    if a is None:
        return b
    if b is None:
        return a
    return a + b


def sub(a, b):
    if b is None:
        return a
    if a is None:
        return -b
    return a - b


def scale(a, factor):
    if a is None or factor == 1.0:
        return a
    if factor == -1.0:
        return -a
    return a * factor


def turn(x, step, period):
    if x is None:
        return None
    re, im = x
    step = step % period
    if (4 * step) % period == 0:
        quarter = 4 * step // period
        if quarter == 0:
            return (re, im)
        if quarter == 1:
            return (im, scale(re, -1.0))
        if quarter == 2:
            return (scale(re, -1.0), scale(im, -1.0))
        return (scale(im, -1.0), re)
    angle = -2.0 * math.pi * step / period
    c, s = math.cos(angle), math.sin(angle)
    if (8 * step) % period == 0:
        root = math.sqrt(0.5)
        total, difference = add(re, im), sub(re, im)
        if c * s > 0:
            return (scale(difference, math.copysign(root, c)), scale(total, math.copysign(root, c)))
        return (scale(total, math.copysign(root, c)), scale(sub(im, re), math.copysign(root, c)))
    return (sub(scale(re, c), scale(im, s)), add(scale(re, s), scale(im, c)))


def complex_add(x, y):
    if x is None:
        return y
    if y is None:
        return x
    return (add(x[0], y[0]), add(x[1], y[1]))


def complex_sub(x, y):
    if y is None:
        return x
    if x is None:
        return (scale(y[0], -1.0), scale(y[1], -1.0))
    return (sub(x[0], y[0]), sub(x[1], y[1]))


def small_dft(values):
    size = len(values)
    if size == 1:
        return list(values)
    even = small_dft(values[0::2])
    odd = small_dft(values[1::2])
    odd = [turn(value, step, size) for step, value in enumerate(odd)]
    return [complex_add(e, o) for e, o in zip(even, odd)] + [
        complex_sub(e, o) for e, o in zip(even, odd)
    ]


def factors_of(size):
    first = 1
    while first * first < size:
        first *= 2
    return (size // first, first)


def across_rows(load, emit, count, kept, store, fetch):
    first, second = factors_of(count)
    for b in range(second):
        values = small_dft([load(second * a + b) for a in range(first)])
        for p, value in enumerate(values):
            store(b, p, turn(value, b * p, count))
    for p in range(first):
        values = small_dft([fetch(b, p) for b in range(second)])
        for q, value in enumerate(values):
            k1 = p + first * q
            if k1 < kept:
                emit(k1, value)


def tables(count, lanes):
    k1 = np.arange(count)[:, None]
    n2 = np.arange(lanes)[None, :]
    phase = -2.0 * np.pi * ((k1 * n2) % (count * lanes)) / (count * lanes)
    twist = np.concatenate([np.cos(phase), np.sin(phase)], axis=1).astype(np.float32)
    j = np.arange(lanes)
    phase = -2.0 * np.pi * ((j[:, None] * j[None, :]) % lanes) / lanes
    c, s = np.cos(phase), np.sin(phase)
    matrix = np.block([[c, s], [-s, c]]).astype(np.float32)
    high = matrix.astype(ml_dtypes.bfloat16)
    low = (matrix - high.astype(np.float32)).astype(ml_dtypes.bfloat16)
    return twist, np.concatenate([high, high, low], axis=0)


def lane_dft(x, matrix):
    high = x.astype(jnp.bfloat16)
    low = (x - high.astype(jnp.float32)).astype(jnp.bfloat16)
    return jnp.dot(
        jnp.concatenate([high, low, high], axis=1), matrix, preferred_element_type=jnp.float32
    )


def block_rows(kind, sequence, piece, batch, pieces, channels):
    first = ((kind * batch + sequence) * pieces + piece) * channels
    return slice(first, first + channels)


def gate_kernel(batch, query_hbm, key_hbm, value_hbm, cotangent_hbm, sent_hbm, held, sent, sems, out_sems):
    shards, rows, lanes = sent.shape
    _, _, tokens, all_channels = held.shape
    channels, pieces = all_channels // shards, tokens // lanes
    sources = (key_hbm, value_hbm, cotangent_hbm, query_hbm)

    def copy(b, i):
        return pltpu.make_async_copy(sources[i].at[b], held.at[i, b], sems.at[i, b])

    def send(kind):
        span = pl.ds(kind * (rows // 2), rows // 2)
        return pltpu.make_async_copy(sent.at[:, span], sent_hbm.at[:, span], out_sems.at[kind])

    for i in range(4):
        for b in range(batch):
            copy(b, i).start()
    for kind in range(2):
        for b in range(batch):
            copy(b, 2 * kind).wait()
            copy(b, 2 * kind + 1).wait()
            columns = jnp.transpose(held[2 * kind, b] * held[2 * kind + 1, b])
            columns = columns.reshape(shards, channels, tokens)
            for piece in range(pieces):
                at = block_rows(kind, b, piece, batch, pieces, channels)
                sent[:, at] = columns[:, :, piece * lanes : (piece + 1) * lanes]
        send(kind).start()
    for kind in range(2):
        send(kind).wait()


def transforms(twist_ref, matrix_ref, middle, turned):
    count, channels, width = turned.shape
    lanes = width // 2
    first, _ = factors_of(count)
    per_chunk = ROW_CHUNK // channels
    chunks = [slice(at, min(at + per_chunk, count)) for at in range(0, count, per_chunk)]

    def store(b, p, value):
        re, im = value
        middle[b * first + p, :, :lanes] = jnp.zeros_like(im) if re is None else re
        middle[b * first + p, :, lanes:] = jnp.zeros_like(re) if im is None else im

    def fetch(b, p):
        return (middle[b * first + p, :, :lanes], middle[b * first + p, :, lanes:])

    def twist(k1, value):
        c, s = twist_ref[k1 : k1 + 1, :lanes], twist_ref[k1 : k1 + 1, lanes:]
        return (value[0] * c - value[1] * s, value[0] * s + value[1] * c)

    def place(k1, value):
        turned[k1, :, :lanes], turned[k1, :, lanes:] = twist(k1, value)

    def forward(load, spec):
        across_rows(load, place, count, count, store, fetch)
        for part in chunks:
            x = turned[part].reshape(-1, width)
            spec[part] = lane_dft(x, matrix_ref[...]).reshape(-1, channels, width)

    def inverse(left, right, conjugate_left, emit):
        for part in chunks:
            lr, li = left[part, :, :lanes], left[part, :, lanes:]
            rr, ri = right[part, :, :lanes], right[part, :, lanes:]
            if conjugate_left:
                re, im = lr * rr + li * ri, li * rr - lr * ri
            else:
                re, im = lr * rr - li * ri, -(lr * ri + li * rr)
            x = jnp.concatenate([re.reshape(-1, lanes), im.reshape(-1, lanes)], axis=1)
            turned[part] = lane_dft(x, matrix_ref[...]).reshape(-1, channels, width)

        def load(k1):
            return twist(k1, (turned[k1, :, :lanes], turned[k1, :, lanes:]))

        across_rows(load, emit, count, count // 2, store, fetch)

    return forward, inverse


def token_blocks(ref, kind, pair, batch, channels, live):
    pieces = ref.shape[1] // (2 * batch * channels)

    def where(n1, sequence):
        at = block_rows(kind, 2 * pair + sequence, n1 % pieces, batch, pieces, channels)
        return n1 // pieces, at

    def load(n1):
        if n1 >= live:
            return None
        return (ref[where(n1, 0)], ref[where(n1, 1)])

    def emit(n1, value):
        ref[where(n1, 0)] = value[0]
        ref[where(n1, 1)] = -value[1]

    return load, emit


def filter_kernel(filter_ref, twist_ref, matrix_ref, spec_ref, middle, turned):
    length = filter_ref.shape[1]
    lanes = twist_ref.shape[1] // 2
    forward, _ = transforms(twist_ref, matrix_ref, middle, turned)

    def load(n1):
        if n1 * lanes >= length:
            return None
        return (filter_ref[:, n1 * lanes : (n1 + 1) * lanes] * (0.5 / length), None)

    forward(load, spec_ref)


def convolve_kernel(
    held_ref, filter_ref, twist_ref, matrix_ref, back_hbm, mixed_ref, upstream_ref,
    back, middles, turneds, out_sems,
):
    pairs, count, channels, _ = mixed_ref.shape
    half = back.shape[1] // 2
    kinds = (mixed_ref, upstream_ref)
    scratch = [
        transforms(twist_ref, matrix_ref, middles.at[kind], turneds.at[kind]) for kind in range(2)
    ]

    def send(kind):
        span = pl.ds(kind * half, half)
        return pltpu.make_async_copy(back.at[:, span], back_hbm.at[:, span], out_sems.at[kind])

    for pair in range(pairs):
        for kind in range(2):
            load, _ = token_blocks(held_ref, kind, pair, 2 * pairs, channels, count // 2)
            scratch[kind][0](load, kinds[kind].at[pair])
        for kind in range(2):
            _, emit = token_blocks(back, kind, pair, 2 * pairs, channels, count // 2)
            scratch[kind][1](filter_ref, kinds[kind].at[pair], kind == 1, emit)
            if pair == pairs - 1:
                send(kind).start()
    for kind in range(2):
        send(kind).wait()


def lag_kernel(scaling, mixed_ref, upstream_ref, twist_ref, matrix_ref, lag_ref, middle, turned):
    lanes = twist_ref.shape[1] // 2
    groups, _, share = lag_ref.shape
    group = lax.axis_index("batch")
    _, inverse = transforms(twist_ref, matrix_ref, middle, turned)
    for pair in range(mixed_ref.shape[0]):

        def emit(n1, value):
            at = n1 * lanes
            slot = lax.rem(at // share - group + groups, groups)
            span = slice(at % share, at % share + lanes)
            if pair == 0:
                lag_ref[slot, :, span] = value[0] * scaling
            else:
                lag_ref[slot, :, span] += value[0] * scaling

        inverse(mixed_ref.at[pair], upstream_ref.at[pair], True, emit)


def output_kernel(
    query_ref, key_ref, value_ref, cotangent_ref, skip_ref, home_ref, *refs
):
    *results, ready, out_sems = refs
    shards, _, lanes = home_ref.shape
    batch, tokens, all_channels = query_ref.shape
    channels, pieces = all_channels // shards, tokens // lanes
    skip = skip_ref[...]

    def columns(kind, b):
        parts = [
            home_ref[:, block_rows(kind, b, piece, batch, pieces, channels)]
            for piece in range(pieces)
        ]
        return jnp.concatenate(
            [jnp.transpose(part.reshape(all_channels, lanes)) for part in parts], axis=0
        )

    def finish(i, b):
        return pltpu.make_async_copy(ready.at[i, b], results[i].at[b], out_sems.at[i, b])

    for b in range(batch):
        query, key, value, cotangent = query_ref[b], key_ref[b], value_ref[b], cotangent_ref[b]
        hidden = columns(0, b) + skip * (key * value)
        ready[0, b] = query * hidden
        finish(0, b).start()
        ready[1, b] = cotangent * hidden
        finish(1, b).start()
        mixed_grad = columns(1, b) + skip * (cotangent * query)
        ready[2, b] = mixed_grad * value
        finish(2, b).start()
        ready[3, b] = mixed_grad * key
        finish(3, b).start()
    for b in range(batch):
        for i in range(4):
            finish(i, b).wait()


def per_device(query_gate, key_gate, value_input, filters, skip_gain, cotangent, *, shards, groups):
    batch, tokens, all_channels = query_gate.shape
    channels, length = filters.shape
    lanes = 128 if 2 * length // 128 <= 64 else tokens
    count = 2 * length // lanes
    twist, matrix = tables(count, lanes)
    lane_work = 2 * 3 * count * channels * (2 * lanes) ** 2

    def of(*shape):
        return jax.ShapeDtypeStruct(shape, jnp.float32)

    def call(kernel, name, stages, out_shape, scratch, *arrays, **options):
        return pl.pallas_call(
            kernel,
            out_shape=out_shape,
            scratch_shapes=scratch,
            compiler_params=pltpu.CompilerParams(vmem_limit_bytes=VMEM_BYTES),
            cost_estimate=pl.CostEstimate(
                flops=stages * lane_work, bytes_accessed=stages * 4 * batch * channels * length,
                transcendentals=0,
            ),
            name=name,
            **options,
        )(*arrays)

    def exchange(blocks):
        return lax.all_to_all(blocks, "seq", split_axis=0, concat_axis=0, tiled=True)

    rows = 2 * batch * channels * tokens // lanes
    swap = of(shards, rows, lanes)
    anywhere = pl.BlockSpec(memory_space=pl.ANY)
    in_vmem = pl.BlockSpec(memory_space=pltpu.VMEM)
    spectrum = of(batch // 2, count, channels, 2 * lanes)
    work = [pltpu.VMEM((count, channels, 2 * lanes), jnp.float32)] * 2
    sent = call(
        functools.partial(gate_kernel, batch),
        "gate", 1, swap,
        [
            pltpu.VMEM((4, batch, tokens, all_channels), jnp.float32),
            pltpu.VMEM((shards, rows, lanes), jnp.float32),
            pltpu.SemaphoreType.DMA((4, batch)),
            pltpu.SemaphoreType.DMA((2,)),
        ],
        *(
            pltpu.with_memory_space_constraint(x, pltpu.HBM)
            for x in (query_gate, key_gate, value_input, cotangent)
        ),
        in_specs=[pl.BlockSpec(memory_space=pltpu.HBM)] * 4,
        out_specs=anywhere,
    )
    held = exchange(sent)
    filter_spec = call(
        filter_kernel, "filter", 2, of(count, channels, 2 * lanes), work, filters, twist, matrix
    )
    back, mixed_spec, upstream_spec = call(
        convolve_kernel,
        "convolve", 8, (swap, spectrum, spectrum),
        [
            pltpu.VMEM((shards, rows, lanes), jnp.float32),
            pltpu.VMEM((2, count, channels, 2 * lanes), jnp.float32),
            pltpu.VMEM((2, count, channels, 2 * lanes), jnp.float32),
            pltpu.SemaphoreType.DMA((2,)),
        ],
        held, filter_spec, twist, matrix,
        out_specs=(anywhere, in_vmem, in_vmem),
    )
    home = exchange(back)
    lag = call(
        functools.partial(lag_kernel, 1.0 / (2.0 * length * math.sqrt(length))),
        "lags", 2, of(groups, channels, length // groups), work,
        mixed_spec, upstream_spec, twist, matrix,
    )
    filter_grad = lag[0]
    for step in range(1, groups):
        pairs = [(source, (source + step) % groups) for source in range(groups)]
        filter_grad = filter_grad + lax.ppermute(lag[step], "batch", pairs)
    output, query_grad, key_grad, value_grad = call(
        output_kernel,
        "outputs", 2, (of(*query_gate.shape),) * 4,
        [
            pltpu.VMEM((4, batch, tokens, all_channels), jnp.float32),
            pltpu.SemaphoreType.DMA((4, batch)),
        ],
        query_gate, key_gate, value_input, cotangent, skip_gain.reshape(1, all_channels),
        home,
        out_specs=(anywhere,) * 4,
    )
    return (output, query_grad, key_grad, value_grad, filter_grad)


def solution(mesh):
    in_specs = (
        P("batch", "seq", None),
        P("batch", "seq", None),
        P("batch", "seq", None),
        P("seq", None),
        P(),
        P("batch", "seq", None),
    )
    out_specs = (
        P("batch", "seq", None),
        P("batch", "seq", None),
        P("batch", "seq", None),
        P("batch", "seq", None),
        P("seq", "batch"),
    )
    shards, groups = mesh.shape["seq"], mesh.shape["batch"]

    def whole(*arrays):
        return per_device(*arrays, shards=shards, groups=groups)

    return jax.shard_map(whole, mesh=mesh, in_specs=in_specs, out_specs=out_specs, check_vma=False)
```

```python
import functools
import math

import jax
import jax.numpy as jnp
import ml_dtypes
import numpy as np
from jax import lax
from jax.experimental import pallas as pl
from jax.experimental.pallas import tpu as pltpu
from jax.sharding import PartitionSpec as P

VMEM_BYTES = 48 * 1024 * 1024
ROW_CHUNK = 128


def add(a, b):
    if a is None:
        return b
    if b is None:
        return a
    return a + b


def sub(a, b):
    if b is None:
        return a
    if a is None:
        return -b
    return a - b


def scale(a, factor):
    if a is None or factor == 1.0:
        return a
    if factor == -1.0:
        return -a
    return a * factor


def turn(x, step, period):
    if x is None:
        return None
    re, im = x
    step = step % period
    if (4 * step) % period == 0:
        quarter = 4 * step // period
        if quarter == 0:
            return (re, im)
        if quarter == 1:
            return (im, scale(re, -1.0))
        if quarter == 2:
            return (scale(re, -1.0), scale(im, -1.0))
        return (scale(im, -1.0), re)
    angle = -2.0 * math.pi * step / period
    c, s = math.cos(angle), math.sin(angle)
    if (8 * step) % period == 0:
        root = math.sqrt(0.5)
        total, difference = add(re, im), sub(re, im)
        if c * s > 0:
            return (scale(difference, math.copysign(root, c)), scale(total, math.copysign(root, c)))
        return (scale(total, math.copysign(root, c)), scale(sub(im, re), math.copysign(root, c)))
    return (sub(scale(re, c), scale(im, s)), add(scale(re, s), scale(im, c)))


def complex_add(x, y):
    if x is None:
        return y
    if y is None:
        return x
    return (add(x[0], y[0]), add(x[1], y[1]))


def complex_sub(x, y):
    if y is None:
        return x
    if x is None:
        return (scale(y[0], -1.0), scale(y[1], -1.0))
    return (sub(x[0], y[0]), sub(x[1], y[1]))


def small_dft(values):
    size = len(values)
    if size == 1:
        return list(values)
    even = small_dft(values[0::2])
    odd = small_dft(values[1::2])
    odd = [turn(value, step, size) for step, value in enumerate(odd)]
    return [complex_add(e, o) for e, o in zip(even, odd)] + [
        complex_sub(e, o) for e, o in zip(even, odd)
    ]


def factors_of(size):
    first = 1
    while first * first < size:
        first *= 2
    return (size // first, first)


def across_rows(load, emit, count, kept, store, fetch):
    first, second = factors_of(count)
    for b in range(second):
        values = small_dft([load(second * a + b) for a in range(first)])
        for p, value in enumerate(values):
            store(b, p, turn(value, b * p, count))
    for p in range(first):
        values = small_dft([fetch(b, p) for b in range(second)])
        for q, value in enumerate(values):
            k1 = p + first * q
            if k1 < kept:
                emit(k1, value)


def tables(count, lanes):
    k1 = np.arange(count)[:, None]
    n2 = np.arange(lanes)[None, :]
    phase = -2.0 * np.pi * ((k1 * n2) % (count * lanes)) / (count * lanes)
    twist = np.concatenate([np.cos(phase), np.sin(phase)], axis=1).astype(np.float32)
    j = np.arange(lanes)
    phase = -2.0 * np.pi * ((j[:, None] * j[None, :]) % lanes) / lanes
    c, s = np.cos(phase), np.sin(phase)
    matrix = np.block([[c, s], [-s, c]]).astype(np.float32)
    high = matrix.astype(ml_dtypes.bfloat16)
    low = (matrix - high.astype(np.float32)).astype(ml_dtypes.bfloat16)
    return twist, np.concatenate([high, high, low], axis=0)


def lane_dft(x, matrix):
    high = x.astype(jnp.bfloat16)
    low = (x - high.astype(jnp.float32)).astype(jnp.bfloat16)
    return jnp.dot(
        jnp.concatenate([high, low, high], axis=1), matrix, preferred_element_type=jnp.float32
    )


def is_low(shards):
    return lax.axis_index("seq") < shards // 2


def block_rows(sequence, piece, pieces, channels, part=None):
    first = (sequence * pieces + piece) * 2 * channels
    if part is None:
        return slice(first, first + 2 * channels)
    return slice(first + part * channels, first + (part + 1) * channels)


def gate_kernel(
    query_hbm, key_hbm, value_hbm, cotangent_hbm, own_hbm, other_hbm, held, sent, sems, out_sems
):
    _, half, _, lanes = sent.shape
    _, batch, tokens, all_channels = held.shape
    channels, pieces = all_channels // (2 * half), tokens // lanes
    low = is_low(2 * half)
    sources = (key_hbm, value_hbm, cotangent_hbm, query_hbm)

    def copy(b, i):
        return pltpu.make_async_copy(sources[i].at[b], held.at[i, b], sems.at[i, b])

    def send(kind):
        return pltpu.make_async_copy(
            sent.at[kind], (own_hbm, other_hbm)[kind], out_sems.at[kind]
        )

    def put(kind, b, product):
        columns = jnp.transpose(product).reshape(2, half, channels, tokens)
        for piece in range(pieces):
            for part in range(2):
                at = block_rows(b, piece, pieces, channels, part)
                sent[kind, :, at] = columns[part, :, :, piece * lanes : (piece + 1) * lanes]

    for b in range(batch):
        for i in range(4):
            copy(b, i).start()
    for b in range(batch):
        for i in range(4):
            copy(b, i).wait()
        mixed, upstream = held[0, b] * held[1, b], held[2, b] * held[3, b]
        put(0, b, jnp.where(low, mixed, upstream))
    send(0).start()
    for b in range(batch):
        mixed, upstream = held[0, b] * held[1, b], held[2, b] * held[3, b]
        put(1, b, jnp.where(low, upstream, mixed))
    send(1).start()
    send(0).wait()
    send(1).wait()


def transforms(twist_ref, matrix_ref, middle, turned):
    count, channels, width = turned.shape
    lanes = width // 2
    first, _ = factors_of(count)
    per_chunk = ROW_CHUNK // channels
    chunks = [slice(at, min(at + per_chunk, count)) for at in range(0, count, per_chunk)]

    def store(b, p, value):
        re, im = value
        middle[b * first + p, :, :lanes] = jnp.zeros_like(im) if re is None else re
        middle[b * first + p, :, lanes:] = jnp.zeros_like(re) if im is None else im

    def fetch(b, p):
        return (middle[b * first + p, :, :lanes], middle[b * first + p, :, lanes:])

    def twist(k1, value):
        c, s = twist_ref[k1 : k1 + 1, :lanes], twist_ref[k1 : k1 + 1, lanes:]
        return (value[0] * c - value[1] * s, value[0] * s + value[1] * c)

    def place(k1, value):
        turned[k1, :, :lanes], turned[k1, :, lanes:] = twist(k1, value)

    def forward(load, spec):
        across_rows(load, place, count, count, store, fetch)
        for part in chunks:
            x = turned[part].reshape(-1, width)
            spec[part] = lane_dft(x, matrix_ref[...]).reshape(-1, channels, width)

    def inverse(product, emit, kept):
        for part in chunks:
            re, im = product(part)
            x = jnp.concatenate([re.reshape(-1, lanes), im.reshape(-1, lanes)], axis=1)
            turned[part] = lane_dft(x, matrix_ref[...]).reshape(-1, channels, width)

        def load(k1):
            return twist(k1, (turned[k1, :, :lanes], turned[k1, :, lanes:]))

        across_rows(load, emit, count, kept, store, fetch)

    return forward, inverse


def spectrum_part(ref, part):
    lanes = ref.shape[-1] // 2
    return ref[part, :, :lanes], ref[part, :, lanes:]


def token_blocks(ref, pair, batch, channels, live):
    pieces = ref.shape[1] // (2 * batch * channels)

    def where(n1, sequence):
        return n1 // pieces, block_rows(2 * pair + sequence, n1 % pieces, pieces, channels)

    def load(n1):
        if n1 >= live:
            return None
        return (ref[where(n1, 0)], ref[where(n1, 1)])

    def emit(n1, value):
        ref[where(n1, 0)] = value[0]
        ref[where(n1, 1)] = -value[1]

    return load, emit


def filter_kernel(
    shards, own_ref, other_ref, twist_ref, matrix_ref, near_ref, cross_ref, middle, turned
):
    length = own_ref.shape[1]
    lanes = twist_ref.shape[1] // 2
    low = is_low(shards)
    count = length // lanes
    forward, _ = transforms(twist_ref, matrix_ref, middle, turned)

    def load_half(first):
        def load(n1):
            if n1 >= count // 2:
                return None
            span = slice(first + n1 * lanes, first + (n1 + 1) * lanes)
            own, other = own_ref[:, span], other_ref[:, span]
            taps = jnp.concatenate([jnp.where(low, own, other), jnp.where(low, other, own)], axis=0)
            return (taps * (1.0 / length), None)

        return load

    forward(load_half(0), near_ref)
    forward(load_half(length // 2), cross_ref)
    for k1 in range(count):
        if k1 % 2 == 0:
            cross_ref[k1] += near_ref[k1]
        else:
            cross_ref[k1] -= near_ref[k1]


def near_kernel(
    shards, own_ref, other_ref, filter_ref, twist_ref, matrix_ref,
    back_ref, own_spec, other_spec, lag_mine, lag_theirs, middles, turneds,
):
    pairs, count, rows, width = own_spec.shape
    channels, lanes = rows // 2, width // 2
    low = is_low(shards)
    sign = jnp.where(low, 1.0, -1.0)
    scratch = [transforms(twist_ref, matrix_ref, middles.at[i], turneds.at[i]) for i in range(2)]
    for pair in range(pairs):
        own, other = own_spec.at[pair], other_spec.at[pair]
        load, _ = token_blocks(own_ref, pair, 2 * pairs, channels, count // 2)
        scratch[0][0](load, own)
        load, _ = token_blocks(other_ref, pair, 2 * pairs, channels, count // 2)
        scratch[1][0](load, other)

        def result(part):
            fr, fi = spectrum_part(filter_ref, part)
            ar, ai = spectrum_part(own, part)
            fi = sign * fi
            return (fr * ar - fi * ai, -(fr * ai + fi * ar))

        def lags(part):
            ar, ai = spectrum_part(own, part)
            br, bi = spectrum_part(other, part)
            return (ar * br + ai * bi, sign * (ai * br - ar * bi))

        def emit_lag(n1, value):
            first, second = value[0][:channels], value[0][channels:]
            span = slice(n1 * lanes, (n1 + 1) * lanes)
            mine, theirs = jnp.where(low, first, second), jnp.where(low, second, first)
            if pair == 0:
                lag_mine[:, span] = mine
                lag_theirs[:, span] = theirs
            else:
                lag_mine[:, span] += mine
                lag_theirs[:, span] += theirs

        _, emit = token_blocks(back_ref, pair, 2 * pairs, channels, count // 2)
        scratch[0][1](result, emit, count // 2)
        scratch[1][1](lags, emit_lag, count // 2)


def cross_kernel(
    shards, far_ref, other_spec, near_ref, cross_ref, twist_ref, matrix_ref,
    back_ref, far_spec, middle, turned,
):
    pairs, count, rows, _ = other_spec.shape
    sign = jnp.where(is_low(shards), -1.0, 1.0)
    forward, inverse = transforms(twist_ref, matrix_ref, middle, turned)
    for pair in range(pairs):
        far, other = far_spec.at[pair], other_spec.at[pair]
        load, _ = token_blocks(far_ref, pair, 2 * pairs, rows // 2, count // 2)
        forward(load, far)

        def result(part):
            nr, ni = spectrum_part(near_ref, part)
            cr, ci = spectrum_part(cross_ref, part)
            br, bi = spectrum_part(other, part)
            gr, gi = spectrum_part(far, part)
            ni, ci = sign * ni, sign * ci
            return (
                nr * br - ni * bi + (cr * gr - ci * gi),
                -(nr * bi + ni * br + (cr * gi + ci * gr)),
            )

        _, emit = token_blocks(back_ref, pair, 2 * pairs, rows // 2, count // 2)
        inverse(result, emit, count // 2)


def lag_kernel(
    shards, scaling, own_spec, far_spec, mine_ref, theirs_ref, twist_ref, matrix_ref,
    lag_ref, middle, turned,
):
    pairs, count, rows, width = own_spec.shape
    channels, lanes = rows // 2, width // 2
    groups, _, share = lag_ref.shape
    low = is_low(shards)
    sign = jnp.where(low, 1.0, -1.0)
    group = lax.axis_index("batch")
    _, inverse = transforms(twist_ref, matrix_ref, middle, turned)
    for pair in range(pairs):

        def mine(ref, part):
            x = jnp.where(low, ref[pair, part, :channels], ref[pair, part, channels:])
            return x[..., :lanes], x[..., lanes:]

        def lags(part):
            ar, ai = mine(own_spec, part)
            gr, gi = mine(far_spec, part)
            return (ar * gr + ai * gi, sign * (ai * gr - ar * gi))

        def emit(n1, value):
            total = value[0]
            if n1 >= count // 2:
                at = (n1 - count // 2) * lanes
                if pair == 0:
                    total += mine_ref[:, at : at + lanes] + theirs_ref[:, at : at + lanes]
            else:
                at = (n1 + count // 2) * lanes
            slot = lax.rem(at // share - group + groups, groups)
            span = slice(at % share, at % share + lanes)
            if pair == 0:
                lag_ref[slot, :, span] = total * scaling
            else:
                lag_ref[slot, :, span] += total * scaling

        inverse(lags, emit, count)


def output_kernel(
    query_ref, key_ref, value_ref, cotangent_ref, skip_ref, own_ref, other_ref, *refs
):
    *results, ready, out_sems = refs
    half, _, lanes = own_ref.shape
    batch, tokens, all_channels = query_ref.shape
    channels, pieces = all_channels // (2 * half), tokens // lanes
    low = is_low(2 * half)
    skip = skip_ref[...]

    def columns(ref, b):
        pieces_of = []
        for piece in range(pieces):
            parts = [
                ref[:, block_rows(b, piece, pieces, channels, part)].reshape(half * channels, lanes)
                for part in range(2)
            ]
            pieces_of.append(jnp.transpose(jnp.concatenate(parts, axis=0)))
        return jnp.concatenate(pieces_of, axis=0)

    def finish(i, b):
        return pltpu.make_async_copy(ready.at[i, b], results[i].at[b], out_sems.at[i, b])

    for b in range(batch):
        query, key, value, cotangent = query_ref[b], key_ref[b], value_ref[b], cotangent_ref[b]
        own, other = columns(own_ref, b), columns(other_ref, b)
        hidden = jnp.where(low, own, other) + skip * (key * value)
        ready[0, b] = query * hidden
        finish(0, b).start()
        ready[1, b] = cotangent * hidden
        finish(1, b).start()
        mixed_grad = jnp.where(low, other, own) + skip * (cotangent * query)
        ready[2, b] = mixed_grad * value
        finish(2, b).start()
        ready[3, b] = mixed_grad * key
        finish(3, b).start()
    for b in range(batch):
        for i in range(4):
            finish(i, b).wait()


def per_device(query_gate, key_gate, value_input, filters, skip_gain, cotangent, *, shards, groups):
    batch, tokens, all_channels = query_gate.shape
    channels, length = filters.shape
    lanes = 128 if length // 128 <= 64 else tokens
    count, half, pairs = length // lanes, shards // 2, batch // 2
    twist, matrix = tables(count, lanes)
    lane_work = 2 * 3 * count * 2 * channels * (2 * lanes) ** 2

    def of(*shape):
        return jax.ShapeDtypeStruct(shape, jnp.float32)

    def vmem(*shape):
        return pltpu.VMEM(shape, jnp.float32)

    def call(kernel, name, stages, out_shape, scratch, *arrays, **options):
        return pl.pallas_call(
            kernel,
            out_shape=out_shape,
            scratch_shapes=scratch,
            compiler_params=pltpu.CompilerParams(vmem_limit_bytes=VMEM_BYTES),
            cost_estimate=pl.CostEstimate(
                flops=stages * lane_work, bytes_accessed=stages * 4 * batch * channels * length,
                transcendentals=0,
            ),
            name=name,
            **options,
        )(*arrays)

    def within_half(blocks):
        members = [list(range(first, first + half)) for first in (0, half)]
        return lax.all_to_all(
            blocks, "seq", split_axis=0, concat_axis=0, tiled=True, axis_index_groups=members
        )

    def swap_halves(x):
        return lax.ppermute(x, "seq", [(i, (i + half) % shards) for i in range(shards)])

    rows = 2 * batch * channels * tokens // lanes
    blocks = of(half, rows, lanes)
    spectra = of(pairs, count, 2 * channels, 2 * lanes)
    spectrum = of(count, 2 * channels, 2 * lanes)
    work = [vmem(count, 2 * channels, 2 * lanes)] * 2
    anywhere = pl.BlockSpec(memory_space=pl.ANY)

    other_filters = swap_halves(filters)
    own, other = call(
        gate_kernel,
        "gate", 1, (blocks, blocks),
        [
            vmem(4, batch, tokens, all_channels),
            vmem(2, half, rows, lanes),
            pltpu.SemaphoreType.DMA((4, batch)),
            pltpu.SemaphoreType.DMA((2,)),
        ],
        *(
            pltpu.with_memory_space_constraint(x, pltpu.HBM)
            for x in (query_gate, key_gate, value_input, cotangent)
        ),
        in_specs=[pl.BlockSpec(memory_space=pltpu.HBM)] * 4,
        out_specs=(anywhere,) * 2,
    )
    own = within_half(own)
    far = swap_halves(own)
    other = within_half(other)
    near_filter, cross_filter = call(
        functools.partial(filter_kernel, shards),
        "filter", 4, (spectrum, spectrum), work, filters, other_filters, twist, matrix,
    )
    own_back, own_spec, other_spec, lag_mine, lag_theirs = call(
        functools.partial(near_kernel, shards),
        "near", 8,
        (blocks, spectra, spectra) + (of(channels, length // 2),) * 2,
        [vmem(2, count, 2 * channels, 2 * lanes)] * 2,
        own, other, near_filter, twist, matrix,
    )
    own_home = within_half(own_back)
    lag_theirs = swap_halves(lag_theirs)
    other_back, far_spec = call(
        functools.partial(cross_kernel, shards),
        "cross", 4, (blocks, spectra), work,
        far, other_spec, near_filter, cross_filter, twist, matrix,
    )
    other_home = within_half(other_back)
    lag = call(
        functools.partial(lag_kernel, shards, 1.0 / (length * math.sqrt(length))),
        "lags", 2, of(groups, channels, length // groups),
        [vmem(count, channels, 2 * lanes)] * 2,
        own_spec, far_spec, lag_mine, lag_theirs, twist, matrix,
    )
    filter_grad = lag[0]
    for step in range(1, groups):
        members = [(source, (source + step) % groups) for source in range(groups)]
        filter_grad = filter_grad + lax.ppermute(lag[step], "batch", members)
    output, query_grad, key_grad, value_grad = call(
        output_kernel,
        "outputs", 2, (of(*query_gate.shape),) * 4,
        [vmem(4, batch, tokens, all_channels), pltpu.SemaphoreType.DMA((4, batch))],
        query_gate, key_gate, value_input, cotangent, skip_gain.reshape(1, all_channels),
        own_home, other_home,
        out_specs=(anywhere,) * 4,
    )
    return (output, query_grad, key_grad, value_grad, filter_grad)


def solution(mesh):
    in_specs = (
        P("batch", "seq", None),
        P("batch", "seq", None),
        P("batch", "seq", None),
        P("seq", None),
        P(),
        P("batch", "seq", None),
    )
    out_specs = (
        P("batch", "seq", None),
        P("batch", "seq", None),
        P("batch", "seq", None),
        P("batch", "seq", None),
        P("seq", "batch"),
    )
    shards, groups = mesh.shape["seq"], mesh.shape["batch"]

    def whole(*arrays):
        return per_device(*arrays, shards=shards, groups=groups)

    return jax.shard_map(whole, mesh=mesh, in_specs=in_specs, out_specs=out_specs, check_vma=False)
```

```python
import functools
import math

import jax
import jax.numpy as jnp
import ml_dtypes
import numpy as np
from jax import lax
from jax.experimental import pallas as pl
from jax.experimental.pallas import tpu as pltpu
from jax.sharding import PartitionSpec as P

VMEM_BYTES = 48 * 1024 * 1024
ROW_CHUNK = 128


def add(a, b):
    if a is None:
        return b
    if b is None:
        return a
    return a + b


def sub(a, b):
    if b is None:
        return a
    if a is None:
        return -b
    return a - b


def scale(a, factor):
    if a is None or factor == 1.0:
        return a
    if factor == -1.0:
        return -a
    return a * factor


def turn(x, step, period):
    if x is None:
        return None
    re, im = x
    step = step % period
    if (4 * step) % period == 0:
        quarter = 4 * step // period
        if quarter == 0:
            return (re, im)
        if quarter == 1:
            return (im, scale(re, -1.0))
        if quarter == 2:
            return (scale(re, -1.0), scale(im, -1.0))
        return (scale(im, -1.0), re)
    angle = -2.0 * math.pi * step / period
    c, s = math.cos(angle), math.sin(angle)
    if (8 * step) % period == 0:
        root = math.sqrt(0.5)
        total, difference = add(re, im), sub(re, im)
        if c * s > 0:
            return (scale(difference, math.copysign(root, c)), scale(total, math.copysign(root, c)))
        return (scale(total, math.copysign(root, c)), scale(sub(im, re), math.copysign(root, c)))
    return (sub(scale(re, c), scale(im, s)), add(scale(re, s), scale(im, c)))


def complex_add(x, y):
    if x is None:
        return y
    if y is None:
        return x
    return (add(x[0], y[0]), add(x[1], y[1]))


def complex_sub(x, y):
    if y is None:
        return x
    if x is None:
        return (scale(y[0], -1.0), scale(y[1], -1.0))
    return (sub(x[0], y[0]), sub(x[1], y[1]))


def small_dft(values):
    size = len(values)
    if size == 1:
        return list(values)
    even = small_dft(values[0::2])
    odd = small_dft(values[1::2])
    odd = [turn(value, step, size) for step, value in enumerate(odd)]
    return [complex_add(e, o) for e, o in zip(even, odd)] + [
        complex_sub(e, o) for e, o in zip(even, odd)
    ]


def factors_of(size):
    first = 1
    while first * first < size:
        first *= 2
    return (size // first, first)


def across_rows(load, emit, count, kept, store, fetch):
    first, second = factors_of(count)
    for b in range(second):
        values = small_dft([load(second * a + b) for a in range(first)])
        for p, value in enumerate(values):
            store(b, p, turn(value, b * p, count))
    for p in range(first):
        values = small_dft([fetch(b, p) for b in range(second)])
        for q, value in enumerate(values):
            k1 = p + first * q
            if k1 < kept:
                emit(k1, value)


def tables(count, lanes):
    k1 = np.arange(count)[:, None]
    n2 = np.arange(lanes)[None, :]
    phase = -2.0 * np.pi * ((k1 * n2) % (count * lanes)) / (count * lanes)
    twist = np.concatenate([np.cos(phase), np.sin(phase)], axis=1).astype(np.float32)
    j = np.arange(lanes)
    phase = -2.0 * np.pi * ((j[:, None] * j[None, :]) % lanes) / lanes
    c, s = np.cos(phase), np.sin(phase)
    matrix = np.block([[c, s], [-s, c]]).astype(np.float32)
    high = matrix.astype(ml_dtypes.bfloat16)
    low = (matrix - high.astype(np.float32)).astype(ml_dtypes.bfloat16)
    return twist, np.concatenate([high, high, low], axis=0)


def lane_dft(x, matrix):
    high = x.astype(jnp.bfloat16)
    low = (x - high.astype(jnp.float32)).astype(jnp.bfloat16)
    return jnp.dot(
        jnp.concatenate([high, low, high], axis=1), matrix, preferred_element_type=jnp.float32
    )


def is_low(shards):
    return lax.axis_index("seq") < shards // 2


def block_rows(sequence, piece, pieces, channels, part=None):
    first = (sequence * pieces + piece) * 2 * channels
    if part is None:
        return slice(first, first + 2 * channels)
    return slice(first + part * channels, first + (part + 1) * channels)


def gate_kernel(
    query_hbm, key_hbm, value_hbm, cotangent_hbm, own_hbm, other_hbm, held, sent, sems, out_sems
):
    _, half, _, lanes = sent.shape
    _, batch, tokens, all_channels = held.shape
    channels, pieces = all_channels // (2 * half), tokens // lanes
    low = is_low(2 * half)
    sources = (key_hbm, value_hbm, cotangent_hbm, query_hbm)

    def copy(b, i):
        return pltpu.make_async_copy(sources[i].at[b], held.at[i, b], sems.at[i, b])

    def send(kind):
        return pltpu.make_async_copy(
            sent.at[kind], (own_hbm, other_hbm)[kind], out_sems.at[kind]
        )

    def put(kind, b, product):
        columns = jnp.transpose(product).reshape(2, half, channels, tokens)
        for piece in range(pieces):
            for part in range(2):
                at = block_rows(b, piece, pieces, channels, part)
                sent[kind, :, at] = columns[part, :, :, piece * lanes : (piece + 1) * lanes]

    for b in range(batch):
        for i in range(4):
            copy(b, i).start()
    for b in range(batch):
        for i in range(4):
            copy(b, i).wait()
        mixed, upstream = held[0, b] * held[1, b], held[2, b] * held[3, b]
        put(0, b, jnp.where(low, mixed, upstream))
    send(0).start()
    for b in range(batch):
        mixed, upstream = held[0, b] * held[1, b], held[2, b] * held[3, b]
        put(1, b, jnp.where(low, upstream, mixed))
    send(1).start()
    send(0).wait()
    send(1).wait()


def transforms(twist_ref, matrix_ref, middle, turned):
    count, channels, width = turned.shape
    lanes = width // 2
    first, _ = factors_of(count)
    per_chunk = ROW_CHUNK // channels
    chunks = [slice(at, min(at + per_chunk, count)) for at in range(0, count, per_chunk)]

    def store(b, p, value):
        re, im = value
        middle[b * first + p, :, :lanes] = jnp.zeros_like(im) if re is None else re
        middle[b * first + p, :, lanes:] = jnp.zeros_like(re) if im is None else im

    def fetch(b, p):
        return (middle[b * first + p, :, :lanes], middle[b * first + p, :, lanes:])

    def twist(k1, value):
        c, s = twist_ref[k1 : k1 + 1, :lanes], twist_ref[k1 : k1 + 1, lanes:]
        return (value[0] * c - value[1] * s, value[0] * s + value[1] * c)

    def place(k1, value):
        turned[k1, :, :lanes], turned[k1, :, lanes:] = twist(k1, value)

    def forward(load, spec):
        across_rows(load, place, count, count, store, fetch)
        for part in chunks:
            x = turned[part].reshape(-1, width)
            spec[part] = lane_dft(x, matrix_ref[...]).reshape(-1, channels, width)

    def inverse(product, emit, kept):
        for part in chunks:
            re, im = product(part)
            x = jnp.concatenate([re.reshape(-1, lanes), im.reshape(-1, lanes)], axis=1)
            turned[part] = lane_dft(x, matrix_ref[...]).reshape(-1, channels, width)

        def load(k1):
            return twist(k1, (turned[k1, :, :lanes], turned[k1, :, lanes:]))

        across_rows(load, emit, count, kept, store, fetch)

    return forward, inverse


def spectrum_part(ref, part):
    lanes = ref.shape[-1] // 2
    return ref[part, :, :lanes], ref[part, :, lanes:]


def token_blocks(ref, pair, batch, channels, live):
    pieces = ref.shape[1] // (2 * batch * channels)

    def where(n1, sequence):
        return n1 // pieces, block_rows(2 * pair + sequence, n1 % pieces, pieces, channels)

    def load(n1):
        if n1 >= live:
            return None
        return (ref[where(n1, 0)], ref[where(n1, 1)])

    def emit(n1, value):
        ref[where(n1, 0)] = value[0]
        ref[where(n1, 1)] = -value[1]

    return load, emit


def filter_kernel(
    shards, own_ref, other_ref, twist_ref, matrix_ref, near_ref, cross_ref, middle, turned
):
    length = own_ref.shape[1]
    lanes = twist_ref.shape[1] // 2
    low = is_low(shards)
    count = length // lanes
    forward, _ = transforms(twist_ref, matrix_ref, middle, turned)

    def load_half(first):
        def load(n1):
            if n1 >= count // 2:
                return None
            span = slice(first + n1 * lanes, first + (n1 + 1) * lanes)
            own, other = own_ref[:, span], other_ref[:, span]
            taps = jnp.concatenate([jnp.where(low, own, other), jnp.where(low, other, own)], axis=0)
            return (taps * (1.0 / length), None)

        return load

    forward(load_half(0), near_ref)
    forward(load_half(length // 2), cross_ref)
    for k1 in range(count):
        if k1 % 2 == 0:
            cross_ref[k1] += near_ref[k1]
        else:
            cross_ref[k1] -= near_ref[k1]


def near_kernel(
    shards, own_ref, other_ref, filter_ref, twist_ref, matrix_ref,
    back_ref, own_spec, other_spec, lag_mine, lag_theirs, middles, turneds,
):
    pairs, count, rows, width = own_spec.shape
    channels, lanes = rows // 2, width // 2
    low = is_low(shards)
    sign = jnp.where(low, 1.0, -1.0)
    scratch = [transforms(twist_ref, matrix_ref, middles.at[i], turneds.at[i]) for i in range(2)]
    for pair in range(pairs):
        own, other = own_spec.at[pair], other_spec.at[pair]
        load, _ = token_blocks(own_ref, pair, 2 * pairs, channels, count // 2)
        scratch[0][0](load, own)
        load, _ = token_blocks(other_ref, pair, 2 * pairs, channels, count // 2)
        scratch[1][0](load, other)

        def result(part):
            fr, fi = spectrum_part(filter_ref, part)
            ar, ai = spectrum_part(own, part)
            fi = sign * fi
            return (fr * ar - fi * ai, -(fr * ai + fi * ar))

        def lags(part):
            ar, ai = spectrum_part(own, part)
            br, bi = spectrum_part(other, part)
            return (ar * br + ai * bi, sign * (ai * br - ar * bi))

        def emit_lag(n1, value):
            first, second = value[0][:channels], value[0][channels:]
            span = slice(n1 * lanes, (n1 + 1) * lanes)
            mine, theirs = jnp.where(low, first, second), jnp.where(low, second, first)
            if pair == 0:
                lag_mine[:, span] = mine
                lag_theirs[:, span] = theirs
            else:
                lag_mine[:, span] += mine
                lag_theirs[:, span] += theirs

        _, emit = token_blocks(back_ref, pair, 2 * pairs, channels, count // 2)
        scratch[0][1](result, emit, count // 2)
        scratch[1][1](lags, emit_lag, count // 2)


def cross_kernel(
    shards, own_back, far_hbm, other_spec, near_ref, cross_ref, twist_ref, matrix_ref,
    back_hbm, far_spec, far_ref, back, middle, turned, sems,
):
    pairs, count, rows, _ = other_spec.shape
    half, block, _ = back.shape
    sign = jnp.where(is_low(shards), -1.0, 1.0)
    forward, inverse = transforms(twist_ref, matrix_ref, middle, turned)
    own_copy = pltpu.make_async_copy(own_back, back_hbm.at[:, pl.ds(0, block)], sems.at[half])
    copies = [
        pltpu.make_async_copy(far_hbm.at[i], far_ref.at[i], sems.at[i]) for i in range(half)
    ]
    for copy in copies:
        copy.start()
    own_copy.start()
    for copy in copies:
        copy.wait()
    for pair in range(pairs):
        far, other = far_spec.at[pair], other_spec.at[pair]
        load, _ = token_blocks(far_ref, pair, 2 * pairs, rows // 2, count // 2)
        forward(load, far)

        def result(part):
            nr, ni = spectrum_part(near_ref, part)
            cr, ci = spectrum_part(cross_ref, part)
            br, bi = spectrum_part(other, part)
            gr, gi = spectrum_part(far, part)
            ni, ci = sign * ni, sign * ci
            return (
                nr * br - ni * bi + (cr * gr - ci * gi),
                -(nr * bi + ni * br + (cr * gi + ci * gr)),
            )

        _, emit = token_blocks(back, pair, 2 * pairs, rows // 2, count // 2)
        inverse(result, emit, count // 2)
    done = pltpu.make_async_copy(back, back_hbm.at[:, pl.ds(block, block)], sems.at[half + 1])
    done.start()
    own_copy.wait()
    done.wait()


def lag_kernel(
    shards, scaling, own_spec, far_spec, mine_ref, theirs_ref, twist_ref, matrix_ref,
    lag_ref, middle, turned,
):
    pairs, count, rows, width = own_spec.shape
    channels, lanes = rows // 2, width // 2
    groups, _, share = lag_ref.shape
    low = is_low(shards)
    sign = jnp.where(low, 1.0, -1.0)
    group = lax.axis_index("batch")
    _, inverse = transforms(twist_ref, matrix_ref, middle, turned)
    for pair in range(pairs):

        def mine(ref, part):
            x = jnp.where(low, ref[pair, part, :channels], ref[pair, part, channels:])
            return x[..., :lanes], x[..., lanes:]

        def lags(part):
            ar, ai = mine(own_spec, part)
            gr, gi = mine(far_spec, part)
            return (ar * gr + ai * gi, sign * (ai * gr - ar * gi))

        def emit(n1, value):
            total = value[0]
            if n1 >= count // 2:
                at = (n1 - count // 2) * lanes
                if pair == 0:
                    total += mine_ref[:, at : at + lanes] + theirs_ref[:, at : at + lanes]
            else:
                at = (n1 + count // 2) * lanes
            slot = lax.rem(at // share - group + groups, groups)
            span = slice(at % share, at % share + lanes)
            if pair == 0:
                lag_ref[slot, :, span] = total * scaling
            else:
                lag_ref[slot, :, span] += total * scaling

        inverse(lags, emit, count)


def output_kernel(
    query_ref, key_ref, value_ref, cotangent_ref, skip_ref, home_ref, *refs
):
    *results, ready, out_sems = refs
    half, block, lanes = home_ref.shape
    batch, tokens, all_channels = query_ref.shape
    channels, pieces = all_channels // (2 * half), tokens // lanes
    low = is_low(2 * half)
    skip = skip_ref[...]

    def columns(kind, b):
        pieces_of = []
        for piece in range(pieces):
            parts = []
            for part in range(2):
                at = block_rows(b, piece, pieces, channels, part)
                at = slice(kind * block // 2 + at.start, kind * block // 2 + at.stop)
                parts.append(home_ref[:, at].reshape(half * channels, lanes))
            pieces_of.append(jnp.transpose(jnp.concatenate(parts, axis=0)))
        return jnp.concatenate(pieces_of, axis=0)

    def finish(i, b):
        return pltpu.make_async_copy(ready.at[i, b], results[i].at[b], out_sems.at[i, b])

    for b in range(batch):
        query, key, value, cotangent = query_ref[b], key_ref[b], value_ref[b], cotangent_ref[b]
        own, other = columns(0, b), columns(1, b)
        hidden = jnp.where(low, own, other) + skip * (key * value)
        ready[0, b] = query * hidden
        finish(0, b).start()
        ready[1, b] = cotangent * hidden
        finish(1, b).start()
        mixed_grad = jnp.where(low, other, own) + skip * (cotangent * query)
        ready[2, b] = mixed_grad * value
        finish(2, b).start()
        ready[3, b] = mixed_grad * key
        finish(3, b).start()
    for b in range(batch):
        for i in range(4):
            finish(i, b).wait()


def per_device(query_gate, key_gate, value_input, filters, skip_gain, cotangent, *, shards, groups):
    batch, tokens, all_channels = query_gate.shape
    channels, length = filters.shape
    lanes = 128 if length // 128 <= 64 else tokens
    count, half, pairs = length // lanes, shards // 2, batch // 2
    twist, matrix = tables(count, lanes)

    def of(*shape):
        return jax.ShapeDtypeStruct(shape, jnp.float32)

    def vmem(*shape):
        return pltpu.VMEM(shape, jnp.float32)

    def call(kernel, name, out_shape, scratch, *arrays, **options):
        return pl.pallas_call(
            kernel,
            out_shape=out_shape,
            scratch_shapes=scratch,
            compiler_params=pltpu.CompilerParams(vmem_limit_bytes=VMEM_BYTES),
            cost_estimate=pl.CostEstimate(flops=1, bytes_accessed=1, transcendentals=0),
            name=name,
            **options,
        )(*arrays)

    def within_half(blocks):
        members = [list(range(first, first + half)) for first in (0, half)]
        return lax.all_to_all(
            blocks, "seq", split_axis=0, concat_axis=0, tiled=True, axis_index_groups=members
        )

    def swap_halves(x):
        return lax.ppermute(x, "seq", [(i, (i + half) % shards) for i in range(shards)])

    rows = 2 * batch * channels * tokens // lanes
    blocks = of(half, rows, lanes)
    spectra = of(pairs, count, 2 * channels, 2 * lanes)
    spectrum = of(count, 2 * channels, 2 * lanes)
    work = [vmem(count, 2 * channels, 2 * lanes)] * 2
    anywhere = pl.BlockSpec(memory_space=pl.ANY)
    in_vmem = pl.BlockSpec(memory_space=pltpu.VMEM)

    other_filters = swap_halves(filters)
    own, other = call(
        gate_kernel,
        "gate", (blocks, blocks),
        [
            vmem(4, batch, tokens, all_channels),
            vmem(2, half, rows, lanes),
            pltpu.SemaphoreType.DMA((4, batch)),
            pltpu.SemaphoreType.DMA((2,)),
        ],
        *(
            pltpu.with_memory_space_constraint(x, pltpu.HBM)
            for x in (query_gate, key_gate, value_input, cotangent)
        ),
        in_specs=[pl.BlockSpec(memory_space=pltpu.HBM)] * 4,
        out_specs=(anywhere,) * 2,
    )
    own = within_half(own)
    far = swap_halves(own)
    own_filters, other_filters, own = lax.optimization_barrier((filters, other_filters, own))
    near_filter, cross_filter = call(
        functools.partial(filter_kernel, shards),
        "filter", (spectrum, spectrum), work, own_filters, other_filters, twist, matrix,
    )
    near_filter, other = lax.optimization_barrier((near_filter, other))
    other = within_half(other)
    own_back, own_spec, other_spec, lag_mine, lag_theirs = call(
        functools.partial(near_kernel, shards),
        "near",
        (blocks, spectra, spectra) + (of(channels, length // 2),) * 2,
        [vmem(2, count, 2 * channels, 2 * lanes)] * 2,
        own, other, near_filter, twist, matrix,
    )
    lag_theirs = swap_halves(lag_theirs)
    back, far_spec = call(
        functools.partial(cross_kernel, shards),
        "cross", (of(half, 2 * rows, lanes), spectra),
        [vmem(half, rows, lanes)] * 2 + work + [pltpu.SemaphoreType.DMA((half + 2,))],
        own_back, far, other_spec, near_filter, cross_filter, twist, matrix,
        in_specs=[anywhere, anywhere] + [in_vmem] * 5,
        out_specs=(anywhere, in_vmem),
    )
    home = within_half(back)
    lag = call(
        functools.partial(lag_kernel, shards, 1.0 / (length * math.sqrt(length))),
        "lags", of(groups, channels, length // groups),
        [vmem(count, channels, 2 * lanes)] * 2,
        own_spec, far_spec, lag_mine, lag_theirs, twist, matrix,
    )
    filter_grad = lag[0]
    for step in range(1, groups):
        members = [(source, (source + step) % groups) for source in range(groups)]
        filter_grad = filter_grad + lax.ppermute(lag[step], "batch", members)
    output, query_grad, key_grad, value_grad = call(
        output_kernel,
        "outputs", (of(*query_gate.shape),) * 4,
        [vmem(4, batch, tokens, all_channels), pltpu.SemaphoreType.DMA((4, batch))],
        query_gate, key_gate, value_input, cotangent, skip_gain.reshape(1, all_channels),
        home,
        out_specs=(anywhere,) * 4,
    )
    return (output, query_grad, key_grad, value_grad, filter_grad)


def solution(mesh):
    in_specs = (
        P("batch", "seq", None),
        P("batch", "seq", None),
        P("batch", "seq", None),
        P("seq", None),
        P(),
        P("batch", "seq", None),
    )
    out_specs = (
        P("batch", "seq", None),
        P("batch", "seq", None),
        P("batch", "seq", None),
        P("batch", "seq", None),
        P("seq", "batch"),
    )
    shards, groups = mesh.shape["seq"], mesh.shape["batch"]

    def whole(*arrays):
        return per_device(*arrays, shards=shards, groups=groups)

    return jax.shard_map(whole, mesh=mesh, in_specs=in_specs, out_specs=out_specs, check_vma=False)
```

```python
import functools
import math

import jax
import jax.numpy as jnp
import ml_dtypes
import numpy as np
from jax import lax
from jax.experimental import pallas as pl
from jax.experimental.pallas import tpu as pltpu
from jax.sharding import PartitionSpec as P

VMEM_BYTES = 48 * 1024 * 1024
ROW_CHUNK = 128


def add(a, b):
    if a is None:
        return b
    if b is None:
        return a
    return a + b


def sub(a, b):
    if b is None:
        return a
    if a is None:
        return -b
    return a - b


def scale(a, factor):
    if a is None or factor == 1.0:
        return a
    if factor == -1.0:
        return -a
    return a * factor


def turn(x, step, period):
    if x is None:
        return None
    re, im = x
    step = step % period
    if (4 * step) % period == 0:
        quarter = 4 * step // period
        if quarter == 0:
            return (re, im)
        if quarter == 1:
            return (im, scale(re, -1.0))
        if quarter == 2:
            return (scale(re, -1.0), scale(im, -1.0))
        return (scale(im, -1.0), re)
    angle = -2.0 * math.pi * step / period
    c, s = math.cos(angle), math.sin(angle)
    if (8 * step) % period == 0:
        root = math.sqrt(0.5)
        total, difference = add(re, im), sub(re, im)
        if c * s > 0:
            return (scale(difference, math.copysign(root, c)), scale(total, math.copysign(root, c)))
        return (scale(total, math.copysign(root, c)), scale(sub(im, re), math.copysign(root, c)))
    return (sub(scale(re, c), scale(im, s)), add(scale(re, s), scale(im, c)))


def complex_add(x, y):
    if x is None:
        return y
    if y is None:
        return x
    return (add(x[0], y[0]), add(x[1], y[1]))


def complex_sub(x, y):
    if y is None:
        return x
    if x is None:
        return (scale(y[0], -1.0), scale(y[1], -1.0))
    return (sub(x[0], y[0]), sub(x[1], y[1]))


def small_dft(values):
    size = len(values)
    if size == 1:
        return list(values)
    even = small_dft(values[0::2])
    odd = small_dft(values[1::2])
    odd = [turn(value, step, size) for step, value in enumerate(odd)]
    return [complex_add(e, o) for e, o in zip(even, odd)] + [
        complex_sub(e, o) for e, o in zip(even, odd)
    ]


def factors_of(size):
    first = 1
    while first * first < size:
        first *= 2
    return (size // first, first)


def across_rows(load, emit, count, kept, store, fetch):
    first, second = factors_of(count)
    for b in range(second):
        values = small_dft([load(second * a + b) for a in range(first)])
        for p, value in enumerate(values):
            store(b, p, turn(value, b * p, count))
    for p in range(first):
        values = small_dft([fetch(b, p) for b in range(second)])
        for q, value in enumerate(values):
            k1 = p + first * q
            if k1 < kept:
                emit(k1, value)


def tables(count, lanes):
    k1 = np.arange(count)[:, None]
    n2 = np.arange(lanes)[None, :]
    phase = -2.0 * np.pi * ((k1 * n2) % (count * lanes)) / (count * lanes)
    twist = np.concatenate([np.cos(phase), np.sin(phase)], axis=1).astype(np.float32)
    j = np.arange(lanes)
    phase = -2.0 * np.pi * ((j[:, None] * j[None, :]) % lanes) / lanes
    c, s = np.cos(phase), np.sin(phase)
    matrix = np.block([[c, s], [-s, c]]).astype(np.float32)
    high = matrix.astype(ml_dtypes.bfloat16)
    low = (matrix - high.astype(np.float32)).astype(ml_dtypes.bfloat16)
    return twist, np.concatenate([high, high, low], axis=0)


def lane_dft(x, matrix):
    high = x.astype(jnp.bfloat16)
    low = (x - high.astype(jnp.float32)).astype(jnp.bfloat16)
    return jnp.dot(
        jnp.concatenate([high, low, high], axis=1), matrix, preferred_element_type=jnp.float32
    )


def is_low(shards):
    return lax.axis_index("seq") < shards // 2


def block_rows(sequence, piece, pieces, channels, part=None):
    first = (sequence * pieces + piece) * 2 * channels
    if part is None:
        return slice(first, first + 2 * channels)
    return slice(first + part * channels, first + (part + 1) * channels)


def gate_kernel(
    query_hbm, key_hbm, value_hbm, cotangent_hbm, sent_hbm, held, sent, sems, out_sems
):
    half, block, lanes = sent.shape
    _, batch, tokens, all_channels = held.shape
    channels, pieces = all_channels // (2 * half), tokens // lanes
    low = is_low(2 * half)
    sources = (key_hbm, value_hbm, cotangent_hbm, query_hbm)

    def copy(b, i):
        return pltpu.make_async_copy(sources[i].at[b], held.at[i, b], sems.at[i, b])

    def send(kind):
        span = pl.ds(kind * (block // 2), block // 2)
        return pltpu.make_async_copy(sent.at[:, span], sent_hbm.at[:, span], out_sems.at[kind])

    def put(kind, b, product):
        columns = jnp.transpose(product).reshape(2, half, channels, tokens)
        for piece in range(pieces):
            for part in range(2):
                at = block_rows(kind * batch + b, piece, pieces, channels, part)
                sent[:, at] = columns[part, :, :, piece * lanes : (piece + 1) * lanes]

    for b in range(batch):
        for i in range(4):
            copy(b, i).start()
    for b in range(batch):
        for i in range(4):
            copy(b, i).wait()
        mixed, upstream = held[0, b] * held[1, b], held[2, b] * held[3, b]
        put(0, b, jnp.where(low, mixed, upstream))
    send(0).start()
    for b in range(batch):
        mixed, upstream = held[0, b] * held[1, b], held[2, b] * held[3, b]
        put(1, b, jnp.where(low, upstream, mixed))
    send(1).start()
    send(0).wait()
    send(1).wait()


def transforms(twist_ref, matrix_ref, middle, turned):
    count, channels, width = turned.shape
    lanes = width // 2
    first, _ = factors_of(count)
    per_chunk = ROW_CHUNK // channels
    chunks = [slice(at, min(at + per_chunk, count)) for at in range(0, count, per_chunk)]

    def store(b, p, value):
        re, im = value
        middle[b * first + p, :, :lanes] = jnp.zeros_like(im) if re is None else re
        middle[b * first + p, :, lanes:] = jnp.zeros_like(re) if im is None else im

    def fetch(b, p):
        return (middle[b * first + p, :, :lanes], middle[b * first + p, :, lanes:])

    def twist(k1, value):
        c, s = twist_ref[k1 : k1 + 1, :lanes], twist_ref[k1 : k1 + 1, lanes:]
        return (value[0] * c - value[1] * s, value[0] * s + value[1] * c)

    def place(k1, value):
        turned[k1, :, :lanes], turned[k1, :, lanes:] = twist(k1, value)

    def forward(load, spec):
        across_rows(load, place, count, count, store, fetch)
        for part in chunks:
            x = turned[part].reshape(-1, width)
            spec[part] = lane_dft(x, matrix_ref[...]).reshape(-1, channels, width)

    def inverse(product, emit, kept):
        for part in chunks:
            re, im = product(part)
            x = jnp.concatenate([re.reshape(-1, lanes), im.reshape(-1, lanes)], axis=1)
            turned[part] = lane_dft(x, matrix_ref[...]).reshape(-1, channels, width)

        def load(k1):
            return twist(k1, (turned[k1, :, :lanes], turned[k1, :, lanes:]))

        across_rows(load, emit, count, kept, store, fetch)

    return forward, inverse


def spectrum_part(ref, part):
    lanes = ref.shape[-1] // 2
    return ref[part, :, :lanes], ref[part, :, lanes:]


def token_blocks(ref, first, sequences, channels, live):
    pieces = ref.shape[1] // (2 * sequences * channels)

    def where(n1, sequence):
        return n1 // pieces, block_rows(first + sequence, n1 % pieces, pieces, channels)

    def load(n1):
        if n1 >= live:
            return None
        return (ref[where(n1, 0)], ref[where(n1, 1)])

    def emit(n1, value):
        ref[where(n1, 0)] = value[0]
        ref[where(n1, 1)] = -value[1]

    return load, emit


def filter_kernel(
    shards, own_ref, other_ref, twist_ref, matrix_ref, near_ref, cross_ref, middle, turned
):
    length = own_ref.shape[1]
    lanes = twist_ref.shape[1] // 2
    low = is_low(shards)
    count = length // lanes
    forward, _ = transforms(twist_ref, matrix_ref, middle, turned)

    def load_half(first):
        def load(n1):
            if n1 >= count // 2:
                return None
            span = slice(first + n1 * lanes, first + (n1 + 1) * lanes)
            own, other = own_ref[:, span], other_ref[:, span]
            taps = jnp.concatenate([jnp.where(low, own, other), jnp.where(low, other, own)], axis=0)
            return (taps * (1.0 / length), None)

        return load

    forward(load_half(0), near_ref)
    forward(load_half(length // 2), cross_ref)
    for k1 in range(count):
        if k1 % 2 == 0:
            cross_ref[k1] += near_ref[k1]
        else:
            cross_ref[k1] -= near_ref[k1]


def near_kernel(
    shards, held_ref, filter_ref, twist_ref, matrix_ref,
    back_hbm, own_spec, other_spec, lag_mine, lag_theirs, back, middles, turneds, sem,
):
    pairs, count, rows, width = own_spec.shape
    channels, lanes, batch = rows // 2, width // 2, 2 * pairs
    low = is_low(shards)
    sign = jnp.where(low, 1.0, -1.0)
    scratch = [transforms(twist_ref, matrix_ref, middles.at[i], turneds.at[i]) for i in range(2)]
    done = pltpu.make_async_copy(back, back_hbm, sem)
    for pair in range(pairs):
        own, other = own_spec.at[pair], other_spec.at[pair]
        load, _ = token_blocks(held_ref, 2 * pair, 2 * batch, channels, count // 2)
        scratch[0][0](load, own)
        load, _ = token_blocks(held_ref, batch + 2 * pair, 2 * batch, channels, count // 2)
        scratch[1][0](load, other)

        def result(part):
            fr, fi = spectrum_part(filter_ref, part)
            ar, ai = spectrum_part(own, part)
            fi = sign * fi
            return (fr * ar - fi * ai, -(fr * ai + fi * ar))

        def lags(part):
            ar, ai = spectrum_part(own, part)
            br, bi = spectrum_part(other, part)
            return (ar * br + ai * bi, sign * (ai * br - ar * bi))

        def emit_lag(n1, value):
            first, second = value[0][:channels], value[0][channels:]
            span = slice(n1 * lanes, (n1 + 1) * lanes)
            mine, theirs = jnp.where(low, first, second), jnp.where(low, second, first)
            if pair == 0:
                lag_mine[:, span] = mine
                lag_theirs[:, span] = theirs
            else:
                lag_mine[:, span] += mine
                lag_theirs[:, span] += theirs

        _, emit = token_blocks(back, 2 * pair, batch, channels, count // 2)
        scratch[0][1](result, emit, count // 2)
        if pair == pairs - 1:
            done.start()
        scratch[1][1](lags, emit_lag, count // 2)
    done.wait()


def cross_kernel(
    shards, far_hbm, other_spec, near_ref, cross_ref, twist_ref, matrix_ref,
    back_hbm, far_spec, far_ref, back, middle, turned, sems,
):
    pairs, count, rows, _ = other_spec.shape
    half = back.shape[0]
    sign = jnp.where(is_low(shards), -1.0, 1.0)
    forward, inverse = transforms(twist_ref, matrix_ref, middle, turned)
    copies = [
        pltpu.make_async_copy(far_hbm.at[i], far_ref.at[i], sems.at[i]) for i in range(half)
    ]
    for copy in copies:
        copy.start()
    for copy in copies:
        copy.wait()
    for pair in range(pairs):
        far, other = far_spec.at[pair], other_spec.at[pair]
        load, _ = token_blocks(far_ref, 2 * pair, 2 * pairs, rows // 2, count // 2)
        forward(load, far)

        def result(part):
            nr, ni = spectrum_part(near_ref, part)
            cr, ci = spectrum_part(cross_ref, part)
            br, bi = spectrum_part(other, part)
            gr, gi = spectrum_part(far, part)
            ni, ci = sign * ni, sign * ci
            return (
                nr * br - ni * bi + (cr * gr - ci * gi),
                -(nr * bi + ni * br + (cr * gi + ci * gr)),
            )

        _, emit = token_blocks(back, 2 * pair, 2 * pairs, rows // 2, count // 2)
        inverse(result, emit, count // 2)
    done = pltpu.make_async_copy(back, back_hbm, sems.at[half])
    done.start()
    done.wait()


def lag_kernel(
    shards, scaling, own_spec, far_spec, mine_ref, theirs_ref, twist_ref, matrix_ref,
    lag_ref, middle, turned,
):
    pairs, count, rows, width = own_spec.shape
    channels, lanes = rows // 2, width // 2
    groups, _, share = lag_ref.shape
    low = is_low(shards)
    sign = jnp.where(low, 1.0, -1.0)
    group = lax.axis_index("batch")
    _, inverse = transforms(twist_ref, matrix_ref, middle, turned)
    for pair in range(pairs):

        def mine(ref, part):
            x = jnp.where(low, ref[pair, part, :channels], ref[pair, part, channels:])
            return x[..., :lanes], x[..., lanes:]

        def lags(part):
            ar, ai = mine(own_spec, part)
            gr, gi = mine(far_spec, part)
            return (ar * gr + ai * gi, sign * (ai * gr - ar * gi))

        def emit(n1, value):
            total = value[0]
            if n1 >= count // 2:
                at = (n1 - count // 2) * lanes
                if pair == 0:
                    total += mine_ref[:, at : at + lanes] + theirs_ref[:, at : at + lanes]
            else:
                at = (n1 + count // 2) * lanes
            slot = lax.rem(at // share - group + groups, groups)
            span = slice(at % share, at % share + lanes)
            if pair == 0:
                lag_ref[slot, :, span] = total * scaling
            else:
                lag_ref[slot, :, span] += total * scaling

        inverse(lags, emit, count)


def output_kernel(
    query_ref, key_ref, value_ref, cotangent_ref, skip_ref, own_ref, other_ref, *refs
):
    *results, ready, out_sems = refs
    half, _, lanes = own_ref.shape
    batch, tokens, all_channels = query_ref.shape
    channels, pieces = all_channels // (2 * half), tokens // lanes
    low = is_low(2 * half)
    skip = skip_ref[...]

    def columns(ref, b):
        pieces_of = []
        for piece in range(pieces):
            parts = []
            for part in range(2):
                at = block_rows(b, piece, pieces, channels, part)
                parts.append(ref[:, at].reshape(half * channels, lanes))
            pieces_of.append(jnp.transpose(jnp.concatenate(parts, axis=0)))
        return jnp.concatenate(pieces_of, axis=0)

    def finish(i, b):
        return pltpu.make_async_copy(ready.at[i, b], results[i].at[b], out_sems.at[i, b])

    for b in range(batch):
        query, key, value, cotangent = query_ref[b], key_ref[b], value_ref[b], cotangent_ref[b]
        own, other = columns(own_ref, b), columns(other_ref, b)
        hidden = jnp.where(low, own, other) + skip * (key * value)
        ready[0, b] = query * hidden
        finish(0, b).start()
        ready[1, b] = cotangent * hidden
        finish(1, b).start()
        mixed_grad = jnp.where(low, other, own) + skip * (cotangent * query)
        ready[2, b] = mixed_grad * value
        finish(2, b).start()
        ready[3, b] = mixed_grad * key
        finish(3, b).start()
    for b in range(batch):
        for i in range(4):
            finish(i, b).wait()


def per_device(query_gate, key_gate, value_input, filters, skip_gain, cotangent, *, shards, groups):
    batch, tokens, all_channels = query_gate.shape
    channels, length = filters.shape
    lanes = 128 if length // 128 <= 64 else tokens
    count, half, pairs = length // lanes, shards // 2, batch // 2
    twist, matrix = tables(count, lanes)
    lane_work = 2 * 3 * count * 2 * channels * (2 * lanes) ** 2

    def of(*shape):
        return jax.ShapeDtypeStruct(shape, jnp.float32)

    def vmem(*shape):
        return pltpu.VMEM(shape, jnp.float32)

    def call(kernel, name, stages, out_shape, scratch, *arrays, **options):
        return pl.pallas_call(
            kernel,
            out_shape=out_shape,
            scratch_shapes=scratch,
            compiler_params=pltpu.CompilerParams(vmem_limit_bytes=VMEM_BYTES),
            cost_estimate=pl.CostEstimate(
                flops=stages * lane_work, bytes_accessed=stages * 4 * batch * channels * length,
                transcendentals=0,
            ),
            name=name,
            **options,
        )(*arrays)

    def within_half(blocks):
        members = [list(range(first, first + half)) for first in (0, half)]
        return lax.all_to_all(
            blocks, "seq", split_axis=0, concat_axis=0, tiled=True, axis_index_groups=members
        )

    def swap_halves(x):
        return lax.ppermute(x, "seq", [(i, (i + half) % shards) for i in range(shards)])

    rows = 2 * batch * channels * tokens // lanes
    blocks = of(half, rows, lanes)
    spectra = of(pairs, count, 2 * channels, 2 * lanes)
    spectrum = of(count, 2 * channels, 2 * lanes)
    work = [vmem(count, 2 * channels, 2 * lanes)] * 2
    anywhere = pl.BlockSpec(memory_space=pl.ANY)
    in_vmem = pl.BlockSpec(memory_space=pltpu.VMEM)

    other_filters = swap_halves(filters)
    sent = call(
        gate_kernel,
        "gate", 1, of(half, 2 * rows, lanes),
        [
            vmem(4, batch, tokens, all_channels),
            vmem(half, 2 * rows, lanes),
            pltpu.SemaphoreType.DMA((4, batch)),
            pltpu.SemaphoreType.DMA((2,)),
        ],
        *(
            pltpu.with_memory_space_constraint(x, pltpu.HBM)
            for x in (query_gate, key_gate, value_input, cotangent)
        ),
        in_specs=[pl.BlockSpec(memory_space=pltpu.HBM)] * 4,
        out_specs=anywhere,
    )
    held = within_half(sent)
    far = swap_halves(held[:, :rows])
    near_filter, cross_filter = call(
        functools.partial(filter_kernel, shards),
        "filter", 4, (spectrum, spectrum), work, filters, other_filters, twist, matrix,
    )
    own_back, own_spec, other_spec, lag_mine, lag_theirs = call(
        functools.partial(near_kernel, shards),
        "near", 8,
        (blocks, spectra, spectra) + (of(channels, length // 2),) * 2,
        [vmem(half, rows, lanes)] + [vmem(2, count, 2 * channels, 2 * lanes)] * 2
        + [pltpu.SemaphoreType.DMA],
        held, near_filter, twist, matrix,
        out_specs=(anywhere,) + (in_vmem,) * 4,
    )
    own_home = within_half(own_back)
    lag_theirs, _ = lax.optimization_barrier((lag_theirs, far))
    lag_theirs = swap_halves(lag_theirs)
    other_back, far_spec = call(
        functools.partial(cross_kernel, shards),
        "cross", 4, (blocks, spectra),
        [vmem(half, rows, lanes)] * 2 + work + [pltpu.SemaphoreType.DMA((half + 1,))],
        far, other_spec, near_filter, cross_filter, twist, matrix,
        in_specs=[anywhere] + [in_vmem] * 5,
        out_specs=(anywhere, in_vmem),
    )
    other_home = within_half(other_back)
    lag = call(
        functools.partial(lag_kernel, shards, 1.0 / (length * math.sqrt(length))),
        "lags", 2, of(groups, channels, length // groups),
        [vmem(count, channels, 2 * lanes)] * 2,
        own_spec, far_spec, lag_mine, lag_theirs, twist, matrix,
    )
    filter_grad = lag[0]
    for step in range(1, groups):
        members = [(source, (source + step) % groups) for source in range(groups)]
        filter_grad = filter_grad + lax.ppermute(lag[step], "batch", members)
    output, query_grad, key_grad, value_grad = call(
        output_kernel,
        "outputs", 2, (of(*query_gate.shape),) * 4,
        [vmem(4, batch, tokens, all_channels), pltpu.SemaphoreType.DMA((4, batch))],
        query_gate, key_gate, value_input, cotangent, skip_gain.reshape(1, all_channels),
        own_home, other_home,
        out_specs=(anywhere,) * 4,
    )
    return (output, query_grad, key_grad, value_grad, filter_grad)


def solution(mesh):
    in_specs = (
        P("batch", "seq", None),
        P("batch", "seq", None),
        P("batch", "seq", None),
        P("seq", None),
        P(),
        P("batch", "seq", None),
    )
    out_specs = (
        P("batch", "seq", None),
        P("batch", "seq", None),
        P("batch", "seq", None),
        P("batch", "seq", None),
        P("seq", "batch"),
    )
    shards, groups = mesh.shape["seq"], mesh.shape["batch"]

    def whole(*arrays):
        return per_device(*arrays, shards=shards, groups=groups)

    return jax.shard_map(whole, mesh=mesh, in_specs=in_specs, out_specs=out_specs, check_vma=False)
```

```python
import functools
import math

import jax
import jax.numpy as jnp
import ml_dtypes
import numpy as np
from jax import lax
from jax.experimental import pallas as pl
from jax.experimental.pallas import tpu as pltpu
from jax.sharding import PartitionSpec as P

VMEM_BYTES = 48 * 1024 * 1024
ROW_CHUNK = 128


def add(a, b):
    if a is None:
        return b
    if b is None:
        return a
    return a + b


def sub(a, b):
    if b is None:
        return a
    if a is None:
        return -b
    return a - b


def scale(a, factor):
    if a is None or factor == 1.0:
        return a
    if factor == -1.0:
        return -a
    return a * factor


def turn(x, step, period):
    if x is None:
        return None
    re, im = x
    step = step % period
    if (4 * step) % period == 0:
        quarter = 4 * step // period
        if quarter == 0:
            return (re, im)
        if quarter == 1:
            return (im, scale(re, -1.0))
        if quarter == 2:
            return (scale(re, -1.0), scale(im, -1.0))
        return (scale(im, -1.0), re)
    angle = -2.0 * math.pi * step / period
    c, s = math.cos(angle), math.sin(angle)
    if (8 * step) % period == 0:
        root = math.sqrt(0.5)
        total, difference = add(re, im), sub(re, im)
        if c * s > 0:
            return (scale(difference, math.copysign(root, c)), scale(total, math.copysign(root, c)))
        return (scale(total, math.copysign(root, c)), scale(sub(im, re), math.copysign(root, c)))
    return (sub(scale(re, c), scale(im, s)), add(scale(re, s), scale(im, c)))


def complex_add(x, y):
    if x is None:
        return y
    if y is None:
        return x
    return (add(x[0], y[0]), add(x[1], y[1]))


def complex_sub(x, y):
    if y is None:
        return x
    if x is None:
        return (scale(y[0], -1.0), scale(y[1], -1.0))
    return (sub(x[0], y[0]), sub(x[1], y[1]))


def small_dft(values):
    size = len(values)
    if size == 1:
        return list(values)
    even = small_dft(values[0::2])
    odd = small_dft(values[1::2])
    odd = [turn(value, step, size) for step, value in enumerate(odd)]
    return [complex_add(e, o) for e, o in zip(even, odd)] + [
        complex_sub(e, o) for e, o in zip(even, odd)
    ]


def factors_of(size):
    first = 1
    while first * first < size:
        first *= 2
    return (size // first, first)


def across_rows(load, emit, count, kept, store, fetch):
    first, second = factors_of(count)
    for b in range(second):
        values = small_dft([load(second * a + b) for a in range(first)])
        for p, value in enumerate(values):
            store(b, p, turn(value, b * p, count))
    for p in range(first):
        values = small_dft([fetch(b, p) for b in range(second)])
        for q, value in enumerate(values):
            k1 = p + first * q
            if k1 < kept:
                emit(k1, value)


def tables(count, lanes):
    k1 = np.arange(count)[:, None]
    n2 = np.arange(lanes)[None, :]
    phase = -2.0 * np.pi * ((k1 * n2) % (count * lanes)) / (count * lanes)
    twist = np.concatenate([np.cos(phase), np.sin(phase)], axis=1).astype(np.float32)
    j = np.arange(lanes)
    phase = -2.0 * np.pi * ((j[:, None] * j[None, :]) % lanes) / lanes
    c, s = np.cos(phase), np.sin(phase)
    matrix = np.block([[c, s], [-s, c]]).astype(np.float32)
    high = matrix.astype(ml_dtypes.bfloat16)
    low = (matrix - high.astype(np.float32)).astype(ml_dtypes.bfloat16)
    return twist, np.concatenate([high, high, low], axis=0)


def lane_dft(x, matrix):
    high = x.astype(jnp.bfloat16)
    low = (x - high.astype(jnp.float32)).astype(jnp.bfloat16)
    return jnp.dot(
        jnp.concatenate([high, low, high], axis=1), matrix, preferred_element_type=jnp.float32
    )


def exchange_order(shards):
    if shards < 8:
        return list(range(shards))
    steps = shards // 4
    uses = np.zeros((shards, shards, 2, steps, 2), np.int32)
    for a in range(shards):
        for b in range(shards):
            (za, ya), (zb, yb) = (a // 4, a // 2 % 2), (b // 4, b // 2 % 2)
            for z in range(min(za, zb), max(za, zb)):
                uses[a, b, ya, z, int(za > zb)] = 1
    uses = uses.reshape(shards, shards, -1)
    place, shift = np.arange(shards)[:, None], np.arange(1, shards)[None, :]

    def load(order):
        total = 0
        for partner in ((place + shift) % shards, place ^ shift):
            total += uses[order[place], order[partner]].sum(axis=0).max(axis=1).sum()
        return int(total)

    draw = np.random.RandomState(0)
    order = 5 * np.arange(shards) % shards
    least = load(order)
    for _ in range(24000 // shards):
        i, j = draw.randint(shards), draw.randint(shards)
        order[[i, j]] = order[[j, i]]
        now = load(order)
        if now <= least:
            least = now
        else:
            order[[i, j]] = order[[j, i]]
    return [int(shard) for shard in order]


def block_rows(kind, sequence, piece, batch, pieces, channels):
    first = ((kind * batch + sequence) * pieces + piece) * channels
    return slice(first, first + channels)


def gate_kernel(order, query_hbm, key_hbm, value_hbm, cotangent_hbm, sent_hbm, held, sent, sems, out_sems):
    shards, rows, lanes = sent.shape
    _, batch, tokens, all_channels = held.shape
    channels, pieces = all_channels // shards, tokens // lanes
    sources = (key_hbm, value_hbm, cotangent_hbm, query_hbm)
    parts = sems.shape[2]

    def copy(b, i, part):
        span = pl.ds(part * (tokens // parts), tokens // parts)
        return pltpu.make_async_copy(
            sources[i].at[b, span], held.at[i, b, span], sems.at[i, b, part]
        )

    def send(kind):
        span = pl.ds(kind * (rows // 2), rows // 2)
        return pltpu.make_async_copy(sent.at[:, span], sent_hbm.at[:, span], out_sems.at[kind])

    for kind in range(2):
        for b in range(batch):
            for part in range(parts):
                copy(b, 2 * kind, part).start()
                copy(b, 2 * kind + 1, part).start()
    for kind in range(2):
        for b in range(batch):
            for part in range(parts):
                copy(b, 2 * kind, part).wait()
                copy(b, 2 * kind + 1, part).wait()
            columns = jnp.transpose(held[2 * kind, b] * held[2 * kind + 1, b])
            columns = columns.reshape(shards, channels, tokens)
            for piece in range(pieces):
                at = block_rows(kind, b, piece, batch, pieces, channels)
                for place, shard in enumerate(order):
                    sent[place, at] = columns[shard, :, piece * lanes : (piece + 1) * lanes]
        send(kind).start()
    for kind in range(2):
        send(kind).wait()


def transforms(twist_ref, matrix_ref, middle, turned):
    count, channels, width = turned.shape
    lanes = width // 2
    first, _ = factors_of(count)
    per_chunk = ROW_CHUNK // channels
    chunks = [slice(at, min(at + per_chunk, count)) for at in range(0, count, per_chunk)]

    def store(b, p, value):
        re, im = value
        middle[b * first + p, :, :lanes] = jnp.zeros_like(im) if re is None else re
        middle[b * first + p, :, lanes:] = jnp.zeros_like(re) if im is None else im

    def fetch(b, p):
        return (middle[b * first + p, :, :lanes], middle[b * first + p, :, lanes:])

    def twist(k1, value):
        c, s = twist_ref[k1 : k1 + 1, :lanes], twist_ref[k1 : k1 + 1, lanes:]
        return (value[0] * c - value[1] * s, value[0] * s + value[1] * c)

    def place(k1, value):
        turned[k1, :, :lanes], turned[k1, :, lanes:] = twist(k1, value)

    def forward(load, spec):
        across_rows(load, place, count, count, store, fetch)
        for part in chunks:
            x = turned[part].reshape(-1, width)
            spec[part] = lane_dft(x, matrix_ref[...]).reshape(-1, channels, width)

    def inverse(left, right, conjugate_left, emit):
        for part in chunks:
            lr, li = left[part, :, :lanes], left[part, :, lanes:]
            rr, ri = right[part, :, :lanes], right[part, :, lanes:]
            if conjugate_left:
                re, im = lr * rr + li * ri, li * rr - lr * ri
            else:
                re, im = lr * rr - li * ri, -(lr * ri + li * rr)
            x = jnp.concatenate([re.reshape(-1, lanes), im.reshape(-1, lanes)], axis=1)
            turned[part] = lane_dft(x, matrix_ref[...]).reshape(-1, channels, width)

        def load(k1):
            return twist(k1, (turned[k1, :, :lanes], turned[k1, :, lanes:]))

        across_rows(load, emit, count, count // 2, store, fetch)

    return forward, inverse


def token_blocks(ref, order, kind, pair, batch, channels, live):
    pieces = ref.shape[1] // (2 * batch * channels)

    def where(n1, sequence):
        at = block_rows(kind, 2 * pair + sequence, n1 % pieces, batch, pieces, channels)
        return order.index(n1 // pieces), at

    def load(n1):
        if n1 >= live:
            return None
        return (ref[where(n1, 0)], ref[where(n1, 1)])

    def emit(n1, value):
        ref[where(n1, 0)] = value[0]
        ref[where(n1, 1)] = -value[1]

    return load, emit


def filter_kernel(filter_ref, twist_ref, matrix_ref, spec_ref, middle, turned):
    length = filter_ref.shape[1]
    lanes = twist_ref.shape[1] // 2
    forward, _ = transforms(twist_ref, matrix_ref, middle, turned)

    def load(n1):
        if n1 * lanes >= length:
            return None
        return (filter_ref[:, n1 * lanes : (n1 + 1) * lanes] * (0.5 / length), None)

    forward(load, spec_ref)


def convolve_kernel(
    order, held_ref, filter_ref, twist_ref, matrix_ref, back_hbm, mixed_ref, upstream_ref,
    back, middles, turneds, out_sems,
):
    pairs, count, channels, _ = mixed_ref.shape
    half = back.shape[1] // 2
    kinds = (mixed_ref, upstream_ref)
    scratch = [
        transforms(twist_ref, matrix_ref, middles.at[kind], turneds.at[kind]) for kind in range(2)
    ]

    def send(kind):
        span = pl.ds(kind * half, half)
        return pltpu.make_async_copy(back.at[:, span], back_hbm.at[:, span], out_sems.at[kind])

    for pair in range(pairs):
        for kind in range(2):
            load, _ = token_blocks(held_ref, order, kind, pair, 2 * pairs, channels, count // 2)
            scratch[kind][0](load, kinds[kind].at[pair])
        for kind in range(2):
            _, emit = token_blocks(back, order, kind, pair, 2 * pairs, channels, count // 2)
            scratch[kind][1](filter_ref, kinds[kind].at[pair], kind == 1, emit)
            if pair == pairs - 1:
                send(kind).start()
    for kind in range(2):
        send(kind).wait()


def lag_kernel(scaling, mixed_ref, upstream_ref, twist_ref, matrix_ref, lag_ref, middle, turned):
    lanes = twist_ref.shape[1] // 2
    groups, _, share = lag_ref.shape
    group = lax.axis_index("batch")
    _, inverse = transforms(twist_ref, matrix_ref, middle, turned)
    for pair in range(mixed_ref.shape[0]):

        def emit(n1, value):
            at = n1 * lanes
            slot = lax.rem(at // share - group + groups, groups)
            span = slice(at % share, at % share + lanes)
            if pair == 0:
                lag_ref[slot, :, span] = value[0] * scaling
            else:
                lag_ref[slot, :, span] += value[0] * scaling

        inverse(mixed_ref.at[pair], upstream_ref.at[pair], True, emit)


def output_kernel(
    order, query_ref, key_ref, value_ref, cotangent_ref, skip_ref, home_ref, *refs
):
    *results, ready, out_sems = refs
    shards, _, lanes = home_ref.shape
    batch, tokens, all_channels = query_ref.shape
    channels, pieces = all_channels // shards, tokens // lanes
    skip = skip_ref[...]

    def columns(kind, b):
        turned = []
        for piece in range(pieces):
            at = block_rows(kind, b, piece, batch, pieces, channels)
            blocks = [home_ref[order.index(shard), at] for shard in range(shards)]
            turned.append(jnp.transpose(jnp.concatenate(blocks, axis=0)))
        return jnp.concatenate(turned, axis=0)

    def finish(i, b):
        return pltpu.make_async_copy(ready.at[i, b], results[i].at[b], out_sems.at[i, b])

    for b in range(batch):
        query, key, value, cotangent = query_ref[b], key_ref[b], value_ref[b], cotangent_ref[b]
        hidden = columns(0, b) + skip * (key * value)
        ready[0, b] = query * hidden
        finish(0, b).start()
        ready[1, b] = cotangent * hidden
        finish(1, b).start()
        mixed_grad = columns(1, b) + skip * (cotangent * query)
        ready[2, b] = mixed_grad * value
        finish(2, b).start()
        ready[3, b] = mixed_grad * key
        finish(3, b).start()
    for b in range(batch):
        for i in range(4):
            finish(i, b).wait()


def per_device(query_gate, key_gate, value_input, filters, skip_gain, cotangent, *, shards, groups):
    batch, tokens, all_channels = query_gate.shape
    channels, length = filters.shape
    lanes = 128 if 2 * length // 128 <= 64 else tokens
    count = 2 * length // lanes
    twist, matrix = tables(count, lanes)
    order = exchange_order(shards)
    lane_work = 2 * 3 * count * channels * (2 * lanes) ** 2

    def of(*shape):
        return jax.ShapeDtypeStruct(shape, jnp.float32)

    def call(kernel, name, stages, out_shape, scratch, *arrays, **options):
        return pl.pallas_call(
            kernel,
            out_shape=out_shape,
            scratch_shapes=scratch,
            compiler_params=pltpu.CompilerParams(vmem_limit_bytes=VMEM_BYTES),
            cost_estimate=pl.CostEstimate(
                flops=stages * lane_work, bytes_accessed=stages * 4 * batch * channels * length,
                transcendentals=0,
            ),
            name=name,
            **options,
        )(*arrays)

    def exchange(blocks):
        return lax.all_to_all(
            blocks, "seq", split_axis=0, concat_axis=0, tiled=True, axis_index_groups=[order]
        )

    rows = 2 * batch * channels * tokens // lanes
    swap = of(shards, rows, lanes)
    anywhere = pl.BlockSpec(memory_space=pl.ANY)
    in_vmem = pl.BlockSpec(memory_space=pltpu.VMEM)
    spectrum = of(batch // 2, count, channels, 2 * lanes)
    work = [pltpu.VMEM((count, channels, 2 * lanes), jnp.float32)] * 2
    sent = call(
        functools.partial(gate_kernel, order),
        "gate", 1, swap,
        [
            pltpu.VMEM((4, batch, tokens, all_channels), jnp.float32),
            pltpu.VMEM((shards, rows, lanes), jnp.float32),
            pltpu.SemaphoreType.DMA((4, batch, 4)),
            pltpu.SemaphoreType.DMA((2,)),
        ],
        *(
            pltpu.with_memory_space_constraint(x, pltpu.HBM)
            for x in (query_gate, key_gate, value_input, cotangent)
        ),
        in_specs=[pl.BlockSpec(memory_space=pltpu.HBM)] * 4,
        out_specs=anywhere,
    )
    held = exchange(sent)
    filter_spec = call(
        filter_kernel, "filter", 2, of(count, channels, 2 * lanes), work, filters, twist, matrix
    )
    back, mixed_spec, upstream_spec = call(
        functools.partial(convolve_kernel, order),
        "convolve", 8, (swap, spectrum, spectrum),
        [
            pltpu.VMEM((shards, rows, lanes), jnp.float32),
            pltpu.VMEM((2, count, channels, 2 * lanes), jnp.float32),
            pltpu.VMEM((2, count, channels, 2 * lanes), jnp.float32),
            pltpu.SemaphoreType.DMA((2,)),
        ],
        held, filter_spec, twist, matrix,
        out_specs=(anywhere, in_vmem, in_vmem),
    )
    home = exchange(back)
    lag = call(
        functools.partial(lag_kernel, 1.0 / (2.0 * length * math.sqrt(length))),
        "lags", 2, of(groups, channels, length // groups), work,
        mixed_spec, upstream_spec, twist, matrix,
    )
    filter_grad = lag[0]
    for step in range(1, groups):
        pairs = [(source, (source + step) % groups) for source in range(groups)]
        filter_grad = filter_grad + lax.ppermute(lag[step], "batch", pairs)
    output, query_grad, key_grad, value_grad = call(
        functools.partial(output_kernel, order),
        "outputs", 2, (of(*query_gate.shape),) * 4,
        [
            pltpu.VMEM((4, batch, tokens, all_channels), jnp.float32),
            pltpu.SemaphoreType.DMA((4, batch)),
        ],
        query_gate, key_gate, value_input, cotangent, skip_gain.reshape(1, all_channels),
        home,
        out_specs=(anywhere,) * 4,
    )
    return (output, query_grad, key_grad, value_grad, filter_grad)


def solution(mesh):
    in_specs = (
        P("batch", "seq", None),
        P("batch", "seq", None),
        P("batch", "seq", None),
        P("seq", None),
        P(),
        P("batch", "seq", None),
    )
    out_specs = (
        P("batch", "seq", None),
        P("batch", "seq", None),
        P("batch", "seq", None),
        P("batch", "seq", None),
        P("seq", "batch"),
    )
    shards, groups = mesh.shape["seq"], mesh.shape["batch"]

    def whole(*arrays):
        return per_device(*arrays, shards=shards, groups=groups)

    return jax.shard_map(whole, mesh=mesh, in_specs=in_specs, out_specs=out_specs, check_vma=False)
```

```python
import itertools
import math

import jax
import jax.numpy as jnp
import ml_dtypes
import numpy as np
from jax import lax
from jax.experimental import pallas as pl
from jax.experimental.pallas import tpu as pltpu
from jax.sharding import PartitionSpec as P

VMEM_BYTES = 48 * 1024 * 1024
ROW_CHUNK = 128


def add(a, b):
    if a is None:
        return b
    if b is None:
        return a
    return a + b


def sub(a, b):
    if b is None:
        return a
    if a is None:
        return -b
    return a - b


def scale(a, factor):
    if a is None or factor == 1.0:
        return a
    if factor == -1.0:
        return -a
    return a * factor


def turn(x, step, period):
    if x is None:
        return None
    re, im = x
    step = step % period
    if (4 * step) % period == 0:
        quarter = 4 * step // period
        if quarter == 0:
            return (re, im)
        if quarter == 1:
            return (im, scale(re, -1.0))
        if quarter == 2:
            return (scale(re, -1.0), scale(im, -1.0))
        return (scale(im, -1.0), re)
    angle = -2.0 * math.pi * step / period
    c, s = math.cos(angle), math.sin(angle)
    if (8 * step) % period == 0:
        root = math.sqrt(0.5)
        total, difference = add(re, im), sub(re, im)
        if c * s > 0:
            return (scale(difference, math.copysign(root, c)), scale(total, math.copysign(root, c)))
        return (scale(total, math.copysign(root, c)), scale(sub(im, re), math.copysign(root, c)))
    return (sub(scale(re, c), scale(im, s)), add(scale(re, s), scale(im, c)))


def complex_add(x, y):
    if x is None:
        return y
    if y is None:
        return x
    return (add(x[0], y[0]), add(x[1], y[1]))


def complex_sub(x, y):
    if y is None:
        return x
    if x is None:
        return (scale(y[0], -1.0), scale(y[1], -1.0))
    return (sub(x[0], y[0]), sub(x[1], y[1]))


def small_dft(values):
    size = len(values)
    if size == 1:
        return list(values)
    even = small_dft(values[0::2])
    odd = small_dft(values[1::2])
    odd = [turn(value, step, size) for step, value in enumerate(odd)]
    return [complex_add(e, o) for e, o in zip(even, odd)] + [
        complex_sub(e, o) for e, o in zip(even, odd)
    ]


def factors_of(size):
    first = 1
    while first * first < size:
        first *= 2
    return (size // first, first)


def across_rows(load, emit, count, kept, store, fetch):
    first, second = factors_of(count)
    for b in range(second):
        values = small_dft([load(second * a + b) for a in range(first)])
        for p, value in enumerate(values):
            store(b, p, turn(value, b * p, count))
    for p in range(first):
        values = small_dft([fetch(b, p) for b in range(second)])
        for q, value in enumerate(values):
            k1 = p + first * q
            if k1 < kept:
                emit(k1, value)


def tables(count, lanes):
    k1 = np.arange(count)[:, None]
    n2 = np.arange(lanes)[None, :]
    phase = -2.0 * np.pi * ((k1 * n2) % (count * lanes)) / (count * lanes)
    twist = np.concatenate([np.cos(phase), np.sin(phase)], axis=1).astype(np.float32)
    j = np.arange(lanes)
    phase = -2.0 * np.pi * ((j[:, None] * j[None, :]) % lanes) / lanes
    c, s = np.cos(phase), np.sin(phase)
    matrix = np.block([[c, s], [-s, c]]).astype(np.float32)
    high = matrix.astype(ml_dtypes.bfloat16)
    low = (matrix - high.astype(np.float32)).astype(ml_dtypes.bfloat16)
    return twist, np.concatenate([high, high, low], axis=0)


def lane_dft(x, matrix):
    high = x.astype(jnp.bfloat16)
    low = (x - high.astype(jnp.float32)).astype(jnp.bfloat16)
    return jnp.dot(
        jnp.concatenate([high, low, high], axis=1), matrix, preferred_element_type=jnp.float32
    )


def gate_kernel(query_hbm, key_hbm, value_hbm, cotangent_hbm, *refs):
    *sent, held, turned, sems = refs
    shards = len(sent)
    _, batch, channels, tokens = sent[0].shape
    me = lax.axis_index("seq")
    sources = (key_hbm, value_hbm, cotangent_hbm, query_hbm)

    def copy(b, i):
        return pltpu.make_async_copy(sources[i].at[b], held.at[i, b], sems.at[i, b])

    for b in range(batch):
        for i in range(4):
            copy(b, i).start()
    for b in range(batch):
        for kind in range(2):
            copy(b, 2 * kind).wait()
            copy(b, 2 * kind + 1).wait()
            product = held[2 * kind, b] * held[2 * kind + 1, b]
            turned[:, kind, b] = jnp.transpose(product).reshape(shards, channels, tokens)
    for step in range(shards):
        sent[step][...] = turned[me ^ step]


def spectral_kernel(
    shards, lag_scale, filter_ref, twist_ref, matrix_ref, *refs
):
    received, refs = refs[:shards], refs[shards:]
    returned, refs = refs[:shards], refs[shards:]
    lag_ref, held_ref, back_ref, middle, turned, filter_spec, mixed_spec, upstream_spec = refs
    _, _, batch, channels, tokens = held_ref.shape
    count, width = twist_ref.shape
    lanes = width // 2
    length = shards * tokens
    live = count // 2
    pieces = tokens // lanes
    groups = lag_ref.shape[0]
    group = lax.axis_index("batch")
    me = lax.axis_index("seq")
    for step in range(shards):
        held_ref[me ^ step] = received[step][...]

    def store(b, p, value):
        first, _ = factors_of(count)
        row = b * first + p
        re, im = value
        middle[row, :, :lanes] = jnp.zeros_like(im) if re is None else re
        middle[row, :, lanes:] = jnp.zeros_like(re) if im is None else im

    def fetch(b, p):
        first, _ = factors_of(count)
        row = b * first + p
        return (middle[row, :, :lanes], middle[row, :, lanes:])

    def place(k1, value):
        c, s = twist_ref[k1 : k1 + 1, :lanes], twist_ref[k1 : k1 + 1, lanes:]
        turned[k1, :, :lanes] = value[0] * c - value[1] * s
        turned[k1, :, lanes:] = value[0] * s + value[1] * c

    per_chunk = ROW_CHUNK // channels

    def chunks():
        for start in range(0, count, per_chunk):
            yield slice(start, min(start + per_chunk, count))

    def flat(x):
        return x.reshape(x.shape[0] * channels, width)

    def forward(load, spec):
        across_rows(load, place, count, count, store, fetch)
        for part in chunks():
            out = lane_dft(flat(turned[part]), matrix_ref[...])
            spec[part] = out.reshape(-1, channels, width)

    def inverse(product, emit):
        for part in chunks():
            re, im = product(part)
            x = jnp.concatenate([flat2(re), flat2(im)], axis=1)
            turned[part] = lane_dft(x, matrix_ref[...]).reshape(-1, channels, width)

        def load(k1):
            c, s = twist_ref[k1 : k1 + 1, :lanes], twist_ref[k1 : k1 + 1, lanes:]
            re, im = turned[k1, :, :lanes], turned[k1, :, lanes:]
            return (re * c - im * s, re * s + im * c)

        across_rows(load, emit, count, live, store, fetch)

    def flat2(x):
        return x.reshape(x.shape[0] * channels, lanes)

    def parts(spec, part):
        return spec[part, :, :lanes], spec[part, :, lanes:]

    def load_filter(n1):
        if n1 >= live:
            return None
        return (filter_ref[:, n1 * lanes : (n1 + 1) * lanes] * (0.5 / length), None)

    forward(load_filter, filter_spec)
    for pair in range(batch // 2):

        def load_kind(kind):
            def load(n1):
                if n1 >= live:
                    return None
                shard, piece = n1 // pieces, n1 % pieces
                span = slice(piece * lanes, (piece + 1) * lanes)
                return (
                    held_ref[shard, kind, 2 * pair, :, span],
                    held_ref[shard, kind, 2 * pair + 1, :, span],
                )

            return load

        def emit_kind(kind):
            def emit(n1, value):
                shard, piece = n1 // pieces, n1 % pieces
                span = slice(piece * lanes, (piece + 1) * lanes)
                back_ref[shard, kind, 2 * pair, :, span] = value[0]
                back_ref[shard, kind, 2 * pair + 1, :, span] = -value[1]

            return emit

        def convolve(part):
            fr, fi = parts(filter_spec, part)
            mr, mi = parts(mixed_spec, part)
            return (fr * mr - fi * mi, -(fr * mi + fi * mr))

        def correlate(part):
            fr, fi = parts(filter_spec, part)
            ur, ui = parts(upstream_spec, part)
            return (fr * ur + fi * ui, fi * ur - fr * ui)

        def lags(part):
            mr, mi = parts(mixed_spec, part)
            ur, ui = parts(upstream_spec, part)
            return (mr * ur + mi * ui, mi * ur - mr * ui)

        def emit_lag(n1, value):
            at = n1 * lanes
            share = length // groups
            slot = lax.rem(at // share - group + groups, groups)
            span = slice(at % share, at % share + lanes)
            if pair == 0:
                lag_ref[slot, :, span] = value[0] * lag_scale
            else:
                lag_ref[slot, :, span] += value[0] * lag_scale

        forward(load_kind(0), mixed_spec)
        inverse(convolve, emit_kind(0))
        forward(load_kind(1), upstream_spec)
        inverse(correlate, emit_kind(1))
        inverse(lags, emit_lag)
    for step in range(shards):
        returned[step][...] = back_ref[me ^ step]


def output_kernel(query_ref, key_ref, value_ref, cotangent_ref, skip_ref, *refs):
    *home, output_ref, query_grad_ref, key_grad_ref, value_grad_ref, turned = refs
    _, batch, channels, tokens = home[0].shape
    me = lax.axis_index("seq")
    for step, block in enumerate(home):
        turned[me ^ step] = block[...]
    skip = skip_ref[...]

    def columns(kind, b):
        return jnp.transpose(turned[:, kind, b].reshape(len(home) * channels, tokens))

    for b in range(batch):
        query, key, value, cotangent = query_ref[b], key_ref[b], value_ref[b], cotangent_ref[b]
        hidden = columns(0, b) + skip * (key * value)
        output_ref[b] = query * hidden
        query_grad_ref[b] = cotangent * hidden
        mixed_grad = columns(1, b) + skip * (cotangent * query)
        key_grad_ref[b] = mixed_grad * value
        value_grad_ref[b] = mixed_grad * key


def exchange(blocks):
    shards = len(blocks)
    received = [blocks[0]] + [None] * (shards - 1)
    far, near = range(shards - 1, shards // 2 - 1, -1), range(shards // 2 - 1, 0, -1)
    steps = [step for both in itertools.zip_longest(far, near) for step in both if step is not None]
    for step in steps:
        pairs = [(source, source ^ step) for source in range(shards)]
        received[step] = lax.ppermute(blocks[step], "seq", pairs)
    return received


def per_device(query_gate, key_gate, value_input, filters, skip_gain, cotangent, *, shards, groups):
    batch, tokens, all_channels = query_gate.shape
    channels, length = filters.shape
    lanes = 128 if 2 * length // 128 <= 64 else tokens
    count = 2 * length // lanes
    twist, matrix = tables(count, lanes)
    params = pltpu.CompilerParams(vmem_limit_bytes=VMEM_BYTES)
    block = jax.ShapeDtypeStruct((2, batch, channels, tokens), jnp.float32)
    swap = pltpu.VMEM((shards, 2, batch, channels, tokens), jnp.float32)
    sent = pl.pallas_call(
        gate_kernel,
        out_shape=(block,) * shards,
        in_specs=[pl.BlockSpec(memory_space=pltpu.HBM)] * 4,
        scratch_shapes=[
            pltpu.VMEM((4, batch, tokens, all_channels), jnp.float32),
            swap,
            pltpu.SemaphoreType.DMA((4, batch)),
        ],
        compiler_params=params,
        name="gate",
    )(*(
        pltpu.with_memory_space_constraint(x, pltpu.HBM)
        for x in (query_gate, key_gate, value_input, cotangent)
    ))
    received = exchange(sent)
    spectrum = pltpu.VMEM((count, channels, 2 * lanes), jnp.float32)

    def body(*refs):
        spectral_kernel(shards, 1.0 / (2.0 * length * math.sqrt(length)), *refs)

    *returned, lag = pl.pallas_call(
        body,
        out_shape=(block,) * shards
        + (jax.ShapeDtypeStruct((groups, channels, length // groups), jnp.float32),),
        scratch_shapes=[swap] * 2 + [spectrum] * 5,
        compiler_params=params,
        name="spectral",
    )(filters, twist, matrix, *received)
    home = exchange(returned)
    filter_grad = lag[0]
    for step in range(1, groups):
        pairs = [(source, (source + step) % groups) for source in range(groups)]
        filter_grad = filter_grad + lax.ppermute(lag[step], "batch", pairs)
    token_out = jax.ShapeDtypeStruct(query_gate.shape, jnp.float32)
    output, query_grad, key_grad, value_grad = pl.pallas_call(
        output_kernel,
        out_shape=(token_out,) * 4,
        scratch_shapes=[swap],
        compiler_params=params,
        name="outputs",
    )(query_gate, key_gate, value_input, cotangent, skip_gain.reshape(1, all_channels), *home)
    return (output, query_grad, key_grad, value_grad, filter_grad)


def solution(mesh):
    in_specs = (
        P("batch", "seq", None),
        P("batch", "seq", None),
        P("batch", "seq", None),
        P("seq", None),
        P(),
        P("batch", "seq", None),
    )
    out_specs = (
        P("batch", "seq", None),
        P("batch", "seq", None),
        P("batch", "seq", None),
        P("batch", "seq", None),
        P("seq", "batch"),
    )
    shards, groups = mesh.shape["seq"], mesh.shape["batch"]

    def whole(*arrays):
        return per_device(*arrays, shards=shards, groups=groups)

    return jax.shard_map(whole, mesh=mesh, in_specs=in_specs, out_specs=out_specs, check_vma=False)
```

```python
import itertools
import math

import jax
import jax.numpy as jnp
import ml_dtypes
import numpy as np
from jax import lax
from jax.experimental import pallas as pl
from jax.experimental.pallas import tpu as pltpu
from jax.sharding import PartitionSpec as P

VMEM_BYTES = 48 * 1024 * 1024
ROW_CHUNK = 128


def add(a, b):
    if a is None:
        return b
    if b is None:
        return a
    return a + b


def sub(a, b):
    if b is None:
        return a
    if a is None:
        return -b
    return a - b


def scale(a, factor):
    if a is None or factor == 1.0:
        return a
    if factor == -1.0:
        return -a
    return a * factor


def turn(x, step, period):
    if x is None:
        return None
    re, im = x
    step = step % period
    if (4 * step) % period == 0:
        quarter = 4 * step // period
        if quarter == 0:
            return (re, im)
        if quarter == 1:
            return (im, scale(re, -1.0))
        if quarter == 2:
            return (scale(re, -1.0), scale(im, -1.0))
        return (scale(im, -1.0), re)
    angle = -2.0 * math.pi * step / period
    c, s = math.cos(angle), math.sin(angle)
    if (8 * step) % period == 0:
        root = math.sqrt(0.5)
        total, difference = add(re, im), sub(re, im)
        if c * s > 0:
            return (scale(difference, math.copysign(root, c)), scale(total, math.copysign(root, c)))
        return (scale(total, math.copysign(root, c)), scale(sub(im, re), math.copysign(root, c)))
    return (sub(scale(re, c), scale(im, s)), add(scale(re, s), scale(im, c)))


def complex_add(x, y):
    if x is None:
        return y
    if y is None:
        return x
    return (add(x[0], y[0]), add(x[1], y[1]))


def complex_sub(x, y):
    if y is None:
        return x
    if x is None:
        return (scale(y[0], -1.0), scale(y[1], -1.0))
    return (sub(x[0], y[0]), sub(x[1], y[1]))


def small_dft(values):
    size = len(values)
    if size == 1:
        return list(values)
    even = small_dft(values[0::2])
    odd = small_dft(values[1::2])
    odd = [turn(value, step, size) for step, value in enumerate(odd)]
    return [complex_add(e, o) for e, o in zip(even, odd)] + [
        complex_sub(e, o) for e, o in zip(even, odd)
    ]


def factors_of(size):
    first = 1
    while first * first < size:
        first *= 2
    return (size // first, first)


def across_rows(load, emit, count, kept, store, fetch):
    first, second = factors_of(count)
    for b in range(second):
        values = small_dft([load(second * a + b) for a in range(first)])
        for p, value in enumerate(values):
            store(b, p, turn(value, b * p, count))
    for p in range(first):
        values = small_dft([fetch(b, p) for b in range(second)])
        for q, value in enumerate(values):
            k1 = p + first * q
            if k1 < kept:
                emit(k1, value)


def tables(count, lanes):
    k1 = np.arange(count)[:, None]
    n2 = np.arange(lanes)[None, :]
    phase = -2.0 * np.pi * ((k1 * n2) % (count * lanes)) / (count * lanes)
    twist = np.concatenate([np.cos(phase), np.sin(phase)], axis=1).astype(np.float32)
    j = np.arange(lanes)
    phase = -2.0 * np.pi * ((j[:, None] * j[None, :]) % lanes) / lanes
    c, s = np.cos(phase), np.sin(phase)
    matrix = np.block([[c, s], [-s, c]]).astype(np.float32)
    high = matrix.astype(ml_dtypes.bfloat16)
    low = (matrix - high.astype(np.float32)).astype(ml_dtypes.bfloat16)
    return twist, np.concatenate([high, high, low], axis=0)


def lane_dft(x, matrix):
    high = x.astype(jnp.bfloat16)
    low = (x - high.astype(jnp.float32)).astype(jnp.bfloat16)
    return jnp.dot(
        jnp.concatenate([high, low, high], axis=1), matrix, preferred_element_type=jnp.float32
    )


def gate_kernel(query_hbm, key_hbm, value_hbm, cotangent_hbm, *refs):
    *sent, held, turned, sems = refs
    shards = len(sent)
    _, batch, channels, tokens = sent[0].shape
    me = lax.axis_index("seq")
    sources = (key_hbm, value_hbm, cotangent_hbm, query_hbm)

    def copy(b, i):
        return pltpu.make_async_copy(sources[i].at[b], held.at[i, b], sems.at[i, b])

    for b in range(batch):
        for i in range(4):
            copy(b, i).start()
    for b in range(batch):
        for kind in range(2):
            copy(b, 2 * kind).wait()
            copy(b, 2 * kind + 1).wait()
            product = held[2 * kind, b] * held[2 * kind + 1, b]
            turned[:, kind, b] = jnp.transpose(product).reshape(shards, channels, tokens)
    for ref, step in zip(sent, exchange_steps(shards)):
        ref[...] = turned[me ^ step]


def spectral_kernel(
    shards, lag_scale, filter_ref, twist_ref, matrix_ref, *refs
):
    received, refs = refs[:shards], refs[shards:]
    returned, refs = refs[:shards], refs[shards:]
    lag_ref, held_ref, back_ref, middle, turned, filter_spec, mixed_spec, upstream_spec = refs
    _, _, batch, channels, tokens = held_ref.shape
    count, width = twist_ref.shape
    lanes = width // 2
    length = shards * tokens
    live = count // 2
    pieces = tokens // lanes
    groups = lag_ref.shape[0]
    group = lax.axis_index("batch")
    me = lax.axis_index("seq")
    for ref, step in zip(received, exchange_steps(shards)):
        held_ref[me ^ step] = ref[...]

    def store(b, p, value):
        first, _ = factors_of(count)
        row = b * first + p
        re, im = value
        middle[row, :, :lanes] = jnp.zeros_like(im) if re is None else re
        middle[row, :, lanes:] = jnp.zeros_like(re) if im is None else im

    def fetch(b, p):
        first, _ = factors_of(count)
        row = b * first + p
        return (middle[row, :, :lanes], middle[row, :, lanes:])

    def place(k1, value):
        c, s = twist_ref[k1 : k1 + 1, :lanes], twist_ref[k1 : k1 + 1, lanes:]
        turned[k1, :, :lanes] = value[0] * c - value[1] * s
        turned[k1, :, lanes:] = value[0] * s + value[1] * c

    per_chunk = ROW_CHUNK // channels

    def chunks():
        for start in range(0, count, per_chunk):
            yield slice(start, min(start + per_chunk, count))

    def flat(x):
        return x.reshape(x.shape[0] * channels, width)

    def forward(load, spec):
        across_rows(load, place, count, count, store, fetch)
        for part in chunks():
            out = lane_dft(flat(turned[part]), matrix_ref[...])
            spec[part] = out.reshape(-1, channels, width)

    def inverse(product, emit):
        for part in chunks():
            re, im = product(part)
            x = jnp.concatenate([flat2(re), flat2(im)], axis=1)
            turned[part] = lane_dft(x, matrix_ref[...]).reshape(-1, channels, width)

        def load(k1):
            c, s = twist_ref[k1 : k1 + 1, :lanes], twist_ref[k1 : k1 + 1, lanes:]
            re, im = turned[k1, :, :lanes], turned[k1, :, lanes:]
            return (re * c - im * s, re * s + im * c)

        across_rows(load, emit, count, live, store, fetch)

    def flat2(x):
        return x.reshape(x.shape[0] * channels, lanes)

    def parts(spec, part):
        return spec[part, :, :lanes], spec[part, :, lanes:]

    def load_filter(n1):
        if n1 >= live:
            return None
        return (filter_ref[:, n1 * lanes : (n1 + 1) * lanes] * (0.5 / length), None)

    forward(load_filter, filter_spec)
    for pair in range(batch // 2):

        def load_kind(kind):
            def load(n1):
                if n1 >= live:
                    return None
                shard, piece = n1 // pieces, n1 % pieces
                span = slice(piece * lanes, (piece + 1) * lanes)
                return (
                    held_ref[shard, kind, 2 * pair, :, span],
                    held_ref[shard, kind, 2 * pair + 1, :, span],
                )

            return load

        def emit_kind(kind):
            def emit(n1, value):
                shard, piece = n1 // pieces, n1 % pieces
                span = slice(piece * lanes, (piece + 1) * lanes)
                back_ref[shard, kind, 2 * pair, :, span] = value[0]
                back_ref[shard, kind, 2 * pair + 1, :, span] = -value[1]

            return emit

        def convolve(part):
            fr, fi = parts(filter_spec, part)
            mr, mi = parts(mixed_spec, part)
            return (fr * mr - fi * mi, -(fr * mi + fi * mr))

        def correlate(part):
            fr, fi = parts(filter_spec, part)
            ur, ui = parts(upstream_spec, part)
            return (fr * ur + fi * ui, fi * ur - fr * ui)

        def lags(part):
            mr, mi = parts(mixed_spec, part)
            ur, ui = parts(upstream_spec, part)
            return (mr * ur + mi * ui, mi * ur - mr * ui)

        def emit_lag(n1, value):
            at = n1 * lanes
            share = length // groups
            slot = lax.rem(at // share - group + groups, groups)
            span = slice(at % share, at % share + lanes)
            if pair == 0:
                lag_ref[slot, :, span] = value[0] * lag_scale
            else:
                lag_ref[slot, :, span] += value[0] * lag_scale

        forward(load_kind(0), mixed_spec)
        inverse(convolve, emit_kind(0))
        forward(load_kind(1), upstream_spec)
        inverse(correlate, emit_kind(1))
        inverse(lags, emit_lag)
    for ref, step in zip(returned, exchange_steps(shards)):
        ref[...] = back_ref[me ^ step]


def output_kernel(query_ref, key_ref, value_ref, cotangent_ref, skip_ref, *refs):
    *home, output_ref, query_grad_ref, key_grad_ref, value_grad_ref, turned = refs
    _, batch, channels, tokens = home[0].shape
    me = lax.axis_index("seq")
    for block, step in zip(home, exchange_steps(len(home))):
        turned[me ^ step] = block[...]
    skip = skip_ref[...]

    def columns(kind, b):
        return jnp.transpose(turned[:, kind, b].reshape(len(home) * channels, tokens))

    for b in range(batch):
        query, key, value, cotangent = query_ref[b], key_ref[b], value_ref[b], cotangent_ref[b]
        hidden = columns(0, b) + skip * (key * value)
        output_ref[b] = query * hidden
        query_grad_ref[b] = cotangent * hidden
        mixed_grad = columns(1, b) + skip * (cotangent * query)
        key_grad_ref[b] = mixed_grad * value
        value_grad_ref[b] = mixed_grad * key


def exchange_steps(shards):
    far, near = range(shards - 1, shards // 2 - 1, -1), range(shards // 2 - 1, 0, -1)
    both = itertools.zip_longest(far, near)
    return [0] + [step for pair in both for step in pair if step is not None]


def exchange(blocks):
    shards = len(blocks)
    received = []
    for block, step in zip(blocks, exchange_steps(shards)):
        pairs = [(source, source ^ step) for source in range(shards)]
        received.append(lax.ppermute(block, "seq", pairs) if step else block)
    return received


def per_device(query_gate, key_gate, value_input, filters, skip_gain, cotangent, *, shards, groups):
    batch, tokens, all_channels = query_gate.shape
    channels, length = filters.shape
    lanes = 128 if 2 * length // 128 <= 64 else tokens
    count = 2 * length // lanes
    twist, matrix = tables(count, lanes)
    params = pltpu.CompilerParams(vmem_limit_bytes=VMEM_BYTES)
    block = jax.ShapeDtypeStruct((2, batch, channels, tokens), jnp.float32)
    swap = pltpu.VMEM((shards, 2, batch, channels, tokens), jnp.float32)
    sent = pl.pallas_call(
        gate_kernel,
        out_shape=(block,) * shards,
        in_specs=[pl.BlockSpec(memory_space=pltpu.HBM)] * 4,
        scratch_shapes=[
            pltpu.VMEM((4, batch, tokens, all_channels), jnp.float32),
            swap,
            pltpu.SemaphoreType.DMA((4, batch)),
        ],
        compiler_params=params,
        name="gate",
    )(*(
        pltpu.with_memory_space_constraint(x, pltpu.HBM)
        for x in (query_gate, key_gate, value_input, cotangent)
    ))
    received = exchange(sent)
    spectrum = pltpu.VMEM((count, channels, 2 * lanes), jnp.float32)

    def body(*refs):
        spectral_kernel(shards, 1.0 / (2.0 * length * math.sqrt(length)), *refs)

    *returned, lag = pl.pallas_call(
        body,
        out_shape=(block,) * shards
        + (jax.ShapeDtypeStruct((groups, channels, length // groups), jnp.float32),),
        scratch_shapes=[swap] * 2 + [spectrum] * 5,
        compiler_params=params,
        name="spectral",
    )(filters, twist, matrix, *received)
    home = exchange(returned)
    filter_grad = lag[0]
    for step in range(1, groups):
        pairs = [(source, (source + step) % groups) for source in range(groups)]
        filter_grad = filter_grad + lax.ppermute(lag[step], "batch", pairs)
    token_out = jax.ShapeDtypeStruct(query_gate.shape, jnp.float32)
    output, query_grad, key_grad, value_grad = pl.pallas_call(
        output_kernel,
        out_shape=(token_out,) * 4,
        scratch_shapes=[swap],
        compiler_params=params,
        name="outputs",
    )(query_gate, key_gate, value_input, cotangent, skip_gain.reshape(1, all_channels), *home)
    return (output, query_grad, key_grad, value_grad, filter_grad)


def solution(mesh):
    in_specs = (
        P("batch", "seq", None),
        P("batch", "seq", None),
        P("batch", "seq", None),
        P("seq", None),
        P(),
        P("batch", "seq", None),
    )
    out_specs = (
        P("batch", "seq", None),
        P("batch", "seq", None),
        P("batch", "seq", None),
        P("batch", "seq", None),
        P("seq", "batch"),
    )
    shards, groups = mesh.shape["seq"], mesh.shape["batch"]

    def whole(*arrays):
        return per_device(*arrays, shards=shards, groups=groups)

    return jax.shard_map(whole, mesh=mesh, in_specs=in_specs, out_specs=out_specs, check_vma=False)
```

```python
import functools
import math

import jax
import jax.numpy as jnp
import ml_dtypes
import numpy as np
from jax import lax
from jax.experimental import pallas as pl
from jax.experimental.pallas import tpu as pltpu
from jax.sharding import PartitionSpec as P

VMEM_BYTES = 48 * 1024 * 1024
ROW_CHUNK = 128


def add(a, b):
    if a is None:
        return b
    if b is None:
        return a
    return a + b


def sub(a, b):
    if b is None:
        return a
    if a is None:
        return -b
    return a - b


def scale(a, factor):
    if a is None or factor == 1.0:
        return a
    if factor == -1.0:
        return -a
    return a * factor


def turn(x, step, period):
    if x is None:
        return None
    re, im = x
    step = step % period
    if (4 * step) % period == 0:
        quarter = 4 * step // period
        if quarter == 0:
            return (re, im)
        if quarter == 1:
            return (im, scale(re, -1.0))
        if quarter == 2:
            return (scale(re, -1.0), scale(im, -1.0))
        return (scale(im, -1.0), re)
    angle = -2.0 * math.pi * step / period
    c, s = math.cos(angle), math.sin(angle)
    if (8 * step) % period == 0:
        root = math.sqrt(0.5)
        total, difference = add(re, im), sub(re, im)
        if c * s > 0:
            return (scale(difference, math.copysign(root, c)), scale(total, math.copysign(root, c)))
        return (scale(total, math.copysign(root, c)), scale(sub(im, re), math.copysign(root, c)))
    return (sub(scale(re, c), scale(im, s)), add(scale(re, s), scale(im, c)))


def complex_add(x, y):
    if x is None:
        return y
    if y is None:
        return x
    return (add(x[0], y[0]), add(x[1], y[1]))


def complex_sub(x, y):
    if y is None:
        return x
    if x is None:
        return (scale(y[0], -1.0), scale(y[1], -1.0))
    return (sub(x[0], y[0]), sub(x[1], y[1]))


def small_dft(values):
    size = len(values)
    if size == 1:
        return list(values)
    even = small_dft(values[0::2])
    odd = small_dft(values[1::2])
    odd = [turn(value, step, size) for step, value in enumerate(odd)]
    return [complex_add(e, o) for e, o in zip(even, odd)] + [
        complex_sub(e, o) for e, o in zip(even, odd)
    ]


def factors_of(size):
    first = 1
    while first * first < size:
        first *= 2
    return (size // first, first)


def across_rows(load, emit, count, kept, store, fetch):
    first, second = factors_of(count)
    for b in range(second):
        values = small_dft([load(second * a + b) for a in range(first)])
        for p, value in enumerate(values):
            store(b, p, turn(value, b * p, count))
    for p in range(first):
        values = small_dft([fetch(b, p) for b in range(second)])
        for q, value in enumerate(values):
            k1 = p + first * q
            if k1 < kept:
                emit(k1, value)


def tables(count, lanes):
    k1 = np.arange(count)[:, None]
    n2 = np.arange(lanes)[None, :]
    phase = -2.0 * np.pi * ((k1 * n2) % (count * lanes)) / (count * lanes)
    twist = np.concatenate([np.cos(phase), np.sin(phase)], axis=1).astype(np.float32)
    j = np.arange(lanes)
    phase = -2.0 * np.pi * ((j[:, None] * j[None, :]) % lanes) / lanes
    c, s = np.cos(phase), np.sin(phase)
    matrix = np.block([[c, s], [-s, c]]).astype(np.float32)
    high = matrix.astype(ml_dtypes.bfloat16)
    low = (matrix - high.astype(np.float32)).astype(ml_dtypes.bfloat16)
    return twist, np.concatenate([high, high, low], axis=0)


def lane_dft(x, matrix):
    high = x.astype(jnp.bfloat16)
    low = (x - high.astype(jnp.float32)).astype(jnp.bfloat16)
    return jnp.dot(
        jnp.concatenate([high, low, high], axis=1), matrix, preferred_element_type=jnp.float32
    )


def exchange_order(shards):
    if shards < 8:
        return list(range(shards))
    steps = shards // 4
    uses = np.zeros((shards, shards, 2, steps, 2), np.int32)
    for a in range(shards):
        for b in range(shards):
            (za, ya), (zb, yb) = (a // 4, a // 2 % 2), (b // 4, b // 2 % 2)
            for z in range(min(za, zb), max(za, zb)):
                uses[a, b, ya, z, int(za > zb)] = 1
    uses = uses.reshape(shards, shards, -1)
    place, shift = np.arange(shards)[:, None], np.arange(1, shards)[None, :]

    def load(order):
        total = 0
        for partner in ((place + shift) % shards, place ^ shift):
            total += uses[order[place], order[partner]].sum(axis=0).max(axis=1).sum()
        return int(total)

    draw = np.random.RandomState(0)
    order = 5 * np.arange(shards) % shards
    least = load(order)
    for _ in range(24000 // shards):
        i, j = draw.randint(shards), draw.randint(shards)
        order[[i, j]] = order[[j, i]]
        now = load(order)
        if now <= least:
            least = now
        else:
            order[[i, j]] = order[[j, i]]
    return [int(shard) for shard in order]


def block_rows(kind, sequence, piece, batch, pieces, channels):
    first = ((kind * batch + sequence) * pieces + piece) * channels
    return slice(first, first + channels)


def gate_kernel(order, query_hbm, key_hbm, value_hbm, cotangent_hbm, sent_hbm, held, sent, sems, out_sems):
    shards, rows, lanes = sent.shape
    _, batch, tokens, all_channels = held.shape
    channels, pieces = all_channels // shards, tokens // lanes
    sources = (key_hbm, value_hbm, cotangent_hbm, query_hbm)

    def copy(b, i):
        return pltpu.make_async_copy(sources[i].at[b], held.at[i, b], sems.at[i, b])

    def send(kind, b):
        first = block_rows(kind, b, 0, batch, pieces, channels).start
        span = pl.ds(first, pieces * channels)
        return pltpu.make_async_copy(sent.at[:, span], sent_hbm.at[:, span], out_sems.at[kind, b])

    parts = [(kind, b) for kind in range(2) for b in range(batch)]
    for kind, b in parts:
        copy(b, 2 * kind).start()
        copy(b, 2 * kind + 1).start()
    for kind, b in parts:
        copy(b, 2 * kind).wait()
        copy(b, 2 * kind + 1).wait()
        columns = jnp.transpose(held[2 * kind, b] * held[2 * kind + 1, b])
        columns = columns.reshape(shards, channels, tokens)
        for piece in range(pieces):
            at = block_rows(kind, b, piece, batch, pieces, channels)
            for place, shard in enumerate(order):
                sent[place, at] = columns[shard, :, piece * lanes : (piece + 1) * lanes]
        send(kind, b).start()
    for kind, b in parts:
        send(kind, b).wait()


def transforms(twist_ref, matrix_ref, middle, turned):
    count, channels, width = turned.shape
    lanes = width // 2
    first, _ = factors_of(count)
    per_chunk = ROW_CHUNK // channels
    chunks = [slice(at, min(at + per_chunk, count)) for at in range(0, count, per_chunk)]

    def store(b, p, value):
        re, im = value
        middle[b * first + p, :, :lanes] = jnp.zeros_like(im) if re is None else re
        middle[b * first + p, :, lanes:] = jnp.zeros_like(re) if im is None else im

    def fetch(b, p):
        return (middle[b * first + p, :, :lanes], middle[b * first + p, :, lanes:])

    def twist(k1, value):
        c, s = twist_ref[k1 : k1 + 1, :lanes], twist_ref[k1 : k1 + 1, lanes:]
        return (value[0] * c - value[1] * s, value[0] * s + value[1] * c)

    def place(k1, value):
        turned[k1, :, :lanes], turned[k1, :, lanes:] = twist(k1, value)

    def forward(load, spec):
        across_rows(load, place, count, count, store, fetch)
        for part in chunks:
            x = turned[part].reshape(-1, width)
            spec[part] = lane_dft(x, matrix_ref[...]).reshape(-1, channels, width)

    def inverse(left, right, conjugate_left, emit):
        for part in chunks:
            lr, li = left[part, :, :lanes], left[part, :, lanes:]
            rr, ri = right[part, :, :lanes], right[part, :, lanes:]
            if conjugate_left:
                re, im = lr * rr + li * ri, li * rr - lr * ri
            else:
                re, im = lr * rr - li * ri, -(lr * ri + li * rr)
            x = jnp.concatenate([re.reshape(-1, lanes), im.reshape(-1, lanes)], axis=1)
            turned[part] = lane_dft(x, matrix_ref[...]).reshape(-1, channels, width)

        def load(k1):
            return twist(k1, (turned[k1, :, :lanes], turned[k1, :, lanes:]))

        across_rows(load, emit, count, count // 2, store, fetch)

    return forward, inverse


def token_blocks(ref, order, kind, pair, batch, channels, live):
    pieces = ref.shape[1] // (2 * batch * channels)

    def where(n1, sequence):
        at = block_rows(kind, 2 * pair + sequence, n1 % pieces, batch, pieces, channels)
        return order.index(n1 // pieces), at

    def load(n1):
        if n1 >= live:
            return None
        return (ref[where(n1, 0)], ref[where(n1, 1)])

    def emit(n1, value):
        ref[where(n1, 0)] = value[0]
        ref[where(n1, 1)] = -value[1]

    return load, emit


def filter_kernel(filter_ref, twist_ref, matrix_ref, spec_ref, middle, turned):
    length = filter_ref.shape[1]
    lanes = twist_ref.shape[1] // 2
    forward, _ = transforms(twist_ref, matrix_ref, middle, turned)

    def load(n1):
        if n1 * lanes >= length:
            return None
        return (filter_ref[:, n1 * lanes : (n1 + 1) * lanes] * (0.5 / length), None)

    forward(load, spec_ref)


def convolve_kernel(
    order, held_ref, filter_ref, twist_ref, matrix_ref, back_hbm, mixed_ref, upstream_ref,
    back, middles, turneds, out_sems,
):
    pairs, count, channels, _ = mixed_ref.shape
    half = back.shape[1] // 2
    kinds = (mixed_ref, upstream_ref)
    scratch = [
        transforms(twist_ref, matrix_ref, middles.at[kind], turneds.at[kind]) for kind in range(2)
    ]

    def send(kind, place):
        span = pl.ds(kind * half, half)
        return pltpu.make_async_copy(
            back.at[place, span], back_hbm.at[place, span], out_sems.at[kind, place]
        )

    def sending(kind, emit):
        pieces = count // 2 // len(order)
        left = [pieces] * len(order)

        def emit_and_send(n1, value):
            emit(n1, value)
            shard = n1 // pieces
            left[shard] -= 1
            if left[shard] == 0:
                send(kind, order.index(shard)).start()

        return emit_and_send

    for pair in range(pairs):
        for kind in range(2):
            load, _ = token_blocks(held_ref, order, kind, pair, 2 * pairs, channels, count // 2)
            scratch[kind][0](load, kinds[kind].at[pair])
        for kind in range(2):
            _, emit = token_blocks(back, order, kind, pair, 2 * pairs, channels, count // 2)
            if pair == pairs - 1:
                emit = sending(kind, emit)
            scratch[kind][1](filter_ref, kinds[kind].at[pair], kind == 1, emit)
    for kind in range(2):
        for place in range(len(order)):
            send(kind, place).wait()


def lag_kernel(scaling, mixed_ref, upstream_ref, twist_ref, matrix_ref, lag_ref, middle, turned):
    lanes = twist_ref.shape[1] // 2
    groups, _, share = lag_ref.shape
    group = lax.axis_index("batch")
    _, inverse = transforms(twist_ref, matrix_ref, middle, turned)
    for pair in range(mixed_ref.shape[0]):

        def emit(n1, value):
            at = n1 * lanes
            slot = lax.rem(at // share - group + groups, groups)
            span = slice(at % share, at % share + lanes)
            if pair == 0:
                lag_ref[slot, :, span] = value[0] * scaling
            else:
                lag_ref[slot, :, span] += value[0] * scaling

        inverse(mixed_ref.at[pair], upstream_ref.at[pair], True, emit)


def output_kernel(
    order, query_ref, key_ref, value_ref, cotangent_ref, skip_ref, home_ref, *refs
):
    *results, ready, out_sems = refs
    shards, _, lanes = home_ref.shape
    batch, tokens, all_channels = query_ref.shape
    channels, pieces = all_channels // shards, tokens // lanes
    skip = skip_ref[...]

    def columns(kind, b):
        turned = []
        for piece in range(pieces):
            at = block_rows(kind, b, piece, batch, pieces, channels)
            blocks = [home_ref[order.index(shard), at] for shard in range(shards)]
            turned.append(jnp.transpose(jnp.concatenate(blocks, axis=0)))
        return jnp.concatenate(turned, axis=0)

    def finish(i, b):
        return pltpu.make_async_copy(ready.at[i, b], results[i].at[b], out_sems.at[i, b])

    for b in range(batch):
        query, key, value, cotangent = query_ref[b], key_ref[b], value_ref[b], cotangent_ref[b]
        hidden = columns(0, b) + skip * (key * value)
        ready[0, b] = query * hidden
        finish(0, b).start()
        ready[1, b] = cotangent * hidden
        finish(1, b).start()
        mixed_grad = columns(1, b) + skip * (cotangent * query)
        ready[2, b] = mixed_grad * value
        finish(2, b).start()
        ready[3, b] = mixed_grad * key
        finish(3, b).start()
    for b in range(batch):
        for i in range(4):
            finish(i, b).wait()


def per_device(query_gate, key_gate, value_input, filters, skip_gain, cotangent, *, shards, groups):
    batch, tokens, all_channels = query_gate.shape
    channels, length = filters.shape
    lanes = 128 if 2 * length // 128 <= 64 else tokens
    count = 2 * length // lanes
    twist, matrix = tables(count, lanes)
    order = exchange_order(shards)
    lane_work = 2 * 3 * count * channels * (2 * lanes) ** 2

    def of(*shape):
        return jax.ShapeDtypeStruct(shape, jnp.float32)

    def call(kernel, name, stages, out_shape, scratch, *arrays, **options):
        return pl.pallas_call(
            kernel,
            out_shape=out_shape,
            scratch_shapes=scratch,
            compiler_params=pltpu.CompilerParams(vmem_limit_bytes=VMEM_BYTES),
            cost_estimate=pl.CostEstimate(
                flops=stages * lane_work, bytes_accessed=stages * 4 * batch * channels * length,
                transcendentals=0,
            ),
            name=name,
            **options,
        )(*arrays)

    def exchange(blocks):
        return lax.all_to_all(
            blocks, "seq", split_axis=0, concat_axis=0, tiled=True, axis_index_groups=[order]
        )

    rows = 2 * batch * channels * tokens // lanes
    swap = of(shards, rows, lanes)
    anywhere = pl.BlockSpec(memory_space=pl.ANY)
    in_vmem = pl.BlockSpec(memory_space=pltpu.VMEM)
    spectrum = of(batch // 2, count, channels, 2 * lanes)
    work = [pltpu.VMEM((count, channels, 2 * lanes), jnp.float32)] * 2
    sent = call(
        functools.partial(gate_kernel, order),
        "gate", 1, swap,
        [
            pltpu.VMEM((4, batch, tokens, all_channels), jnp.float32),
            pltpu.VMEM((shards, rows, lanes), jnp.float32),
            pltpu.SemaphoreType.DMA((4, batch)),
            pltpu.SemaphoreType.DMA((2, batch)),
        ],
        *(
            pltpu.with_memory_space_constraint(x, pltpu.HBM)
            for x in (query_gate, key_gate, value_input, cotangent)
        ),
        in_specs=[pl.BlockSpec(memory_space=pltpu.HBM)] * 4,
        out_specs=anywhere,
    )
    held = exchange(sent)
    filter_spec = call(
        filter_kernel, "filter", 2, of(count, channels, 2 * lanes), work, filters, twist, matrix
    )
    back, mixed_spec, upstream_spec = call(
        functools.partial(convolve_kernel, order),
        "convolve", 8, (swap, spectrum, spectrum),
        [
            pltpu.VMEM((shards, rows, lanes), jnp.float32),
            pltpu.VMEM((2, count, channels, 2 * lanes), jnp.float32),
            pltpu.VMEM((2, count, channels, 2 * lanes), jnp.float32),
            pltpu.SemaphoreType.DMA((2, shards)),
        ],
        held, filter_spec, twist, matrix,
        out_specs=(anywhere, in_vmem, in_vmem),
    )
    home = exchange(back)
    lag = call(
        functools.partial(lag_kernel, 1.0 / (2.0 * length * math.sqrt(length))),
        "lags", 2, of(groups, channels, length // groups), work,
        mixed_spec, upstream_spec, twist, matrix,
    )
    filter_grad = lag[0]
    for step in range(1, groups):
        pairs = [(source, (source + step) % groups) for source in range(groups)]
        filter_grad = filter_grad + lax.ppermute(lag[step], "batch", pairs)
    output, query_grad, key_grad, value_grad = call(
        functools.partial(output_kernel, order),
        "outputs", 2, (of(*query_gate.shape),) * 4,
        [
            pltpu.VMEM((4, batch, tokens, all_channels), jnp.float32),
            pltpu.SemaphoreType.DMA((4, batch)),
        ],
        query_gate, key_gate, value_input, cotangent, skip_gain.reshape(1, all_channels),
        home,
        out_specs=(anywhere,) * 4,
    )
    return (output, query_grad, key_grad, value_grad, filter_grad)


def solution(mesh):
    in_specs = (
        P("batch", "seq", None),
        P("batch", "seq", None),
        P("batch", "seq", None),
        P("seq", None),
        P(),
        P("batch", "seq", None),
    )
    out_specs = (
        P("batch", "seq", None),
        P("batch", "seq", None),
        P("batch", "seq", None),
        P("batch", "seq", None),
        P("seq", "batch"),
    )
    shards, groups = mesh.shape["seq"], mesh.shape["batch"]

    def whole(*arrays):
        return per_device(*arrays, shards=shards, groups=groups)

    return jax.shard_map(whole, mesh=mesh, in_specs=in_specs, out_specs=out_specs, check_vma=False)
```

```python
import functools
import math

import jax
import jax.numpy as jnp
import ml_dtypes
import numpy as np
from jax import lax
from jax.experimental import pallas as pl
from jax.experimental.pallas import tpu as pltpu
from jax.sharding import PartitionSpec as P

VMEM_BYTES = 48 * 1024 * 1024
ROW_CHUNK = 512


def add(a, b):
    if a is None:
        return b
    if b is None:
        return a
    return a + b


def sub(a, b):
    if b is None:
        return a
    if a is None:
        return -b
    return a - b


def scale(a, factor):
    if a is None or factor == 1.0:
        return a
    if factor == -1.0:
        return -a
    return a * factor


def turn(x, step, period):
    if x is None:
        return None
    re, im = x
    step = step % period
    if (4 * step) % period == 0:
        quarter = 4 * step // period
        if quarter == 0:
            return (re, im)
        if quarter == 1:
            return (im, scale(re, -1.0))
        if quarter == 2:
            return (scale(re, -1.0), scale(im, -1.0))
        return (scale(im, -1.0), re)
    angle = -2.0 * math.pi * step / period
    c, s = math.cos(angle), math.sin(angle)
    if (8 * step) % period == 0:
        root = math.sqrt(0.5)
        total, difference = add(re, im), sub(re, im)
        if c * s > 0:
            return (scale(difference, math.copysign(root, c)), scale(total, math.copysign(root, c)))
        return (scale(total, math.copysign(root, c)), scale(sub(im, re), math.copysign(root, c)))
    return (sub(scale(re, c), scale(im, s)), add(scale(re, s), scale(im, c)))


def complex_add(x, y):
    if x is None:
        return y
    if y is None:
        return x
    return (add(x[0], y[0]), add(x[1], y[1]))


def complex_sub(x, y):
    if y is None:
        return x
    if x is None:
        return (scale(y[0], -1.0), scale(y[1], -1.0))
    return (sub(x[0], y[0]), sub(x[1], y[1]))


def small_dft(values):
    size = len(values)
    if size == 1:
        return list(values)
    even = small_dft(values[0::2])
    odd = small_dft(values[1::2])
    odd = [turn(value, step, size) for step, value in enumerate(odd)]
    return [complex_add(e, o) for e, o in zip(even, odd)] + [
        complex_sub(e, o) for e, o in zip(even, odd)
    ]


def factors_of(size):
    first = 1
    while first * first < size:
        first *= 2
    return (size // first, first)


def across_rows(load, emit, count, kept, store, fetch):
    first, second = factors_of(count)
    for b in range(second):
        values = small_dft([load(second * a + b) for a in range(first)])
        for p, value in enumerate(values):
            store(b, p, turn(value, b * p, count))
    for p in range(first):
        values = small_dft([fetch(b, p) for b in range(second)])
        for q, value in enumerate(values):
            k1 = p + first * q
            if k1 < kept:
                emit(k1, value)


def tables(count, lanes):
    k1 = np.arange(count)[:, None]
    n2 = np.arange(lanes)[None, :]
    phase = -2.0 * np.pi * ((k1 * n2) % (count * lanes)) / (count * lanes)
    twist = np.concatenate([np.cos(phase), np.sin(phase)], axis=1).astype(np.float32)
    j = np.arange(lanes)
    phase = -2.0 * np.pi * ((j[:, None] * j[None, :]) % lanes) / lanes
    c, s = np.cos(phase), np.sin(phase)
    matrix = np.block([[c, s], [-s, c]]).astype(np.float32)
    high = matrix.astype(ml_dtypes.bfloat16)
    low = (matrix - high.astype(np.float32)).astype(ml_dtypes.bfloat16)
    return twist, np.concatenate([high, high, low], axis=0)


def lane_dft(x, matrix):
    high = x.astype(jnp.bfloat16)
    low = (x - high.astype(jnp.float32)).astype(jnp.bfloat16)
    return jnp.dot(
        jnp.concatenate([high, low, high], axis=1), matrix, preferred_element_type=jnp.float32
    )


def exchange_order(shards):
    if shards < 8:
        return list(range(shards))
    steps = shards // 4
    uses = np.zeros((shards, shards, 2, steps, 2), np.int32)
    for a in range(shards):
        for b in range(shards):
            (za, ya), (zb, yb) = (a // 4, a // 2 % 2), (b // 4, b // 2 % 2)
            for z in range(min(za, zb), max(za, zb)):
                uses[a, b, ya, z, int(za > zb)] = 1
    uses = uses.reshape(shards, shards, -1)
    place, shift = np.arange(shards)[:, None], np.arange(1, shards)[None, :]

    def load(order):
        total = 0
        for partner in ((place + shift) % shards, place ^ shift):
            total += uses[order[place], order[partner]].sum(axis=0).max(axis=1).sum()
        return int(total)

    draw = np.random.RandomState(0)
    order = 5 * np.arange(shards) % shards
    least = load(order)
    for _ in range(24000 // shards):
        i, j = draw.randint(shards), draw.randint(shards)
        order[[i, j]] = order[[j, i]]
        now = load(order)
        if now <= least:
            least = now
        else:
            order[[i, j]] = order[[j, i]]
    return [int(shard) for shard in order]


def block_rows(kind, sequence, piece, batch, pieces, channels):
    first = ((kind * batch + sequence) * pieces + piece) * channels
    return slice(first, first + channels)


def gate_kernel(order, query_hbm, key_hbm, value_hbm, cotangent_hbm, sent_hbm, held, sent, sems, out_sems):
    shards, rows, lanes = sent.shape
    _, batch, tokens, all_channels = held.shape
    channels, pieces = all_channels // shards, tokens // lanes
    sources = (key_hbm, value_hbm, cotangent_hbm, query_hbm)

    def copy(b, i):
        return pltpu.make_async_copy(sources[i].at[b], held.at[i, b], sems.at[i, b])

    def send(kind, b):
        first = block_rows(kind, b, 0, batch, pieces, channels).start
        span = pl.ds(first, pieces * channels)
        return pltpu.make_async_copy(sent.at[:, span], sent_hbm.at[:, span], out_sems.at[kind, b])

    parts = [(kind, b) for kind in range(2) for b in range(batch)]
    for kind, b in parts:
        copy(b, 2 * kind).start()
        copy(b, 2 * kind + 1).start()
    for kind, b in parts:
        copy(b, 2 * kind).wait()
        copy(b, 2 * kind + 1).wait()
        columns = jnp.transpose(held[2 * kind, b] * held[2 * kind + 1, b])
        columns = columns.reshape(shards, channels, tokens)
        for piece in range(pieces):
            at = block_rows(kind, b, piece, batch, pieces, channels)
            for place, shard in enumerate(order):
                sent[place, at] = columns[shard, :, piece * lanes : (piece + 1) * lanes]
        send(kind, b).start()
    for kind, b in parts:
        send(kind, b).wait()


def transforms(twist_ref, matrix_ref, middle, turned):
    count, channels, width = turned.shape
    lanes = width // 2
    first, _ = factors_of(count)
    per_chunk = ROW_CHUNK // channels
    chunks = [slice(at, min(at + per_chunk, count)) for at in range(0, count, per_chunk)]

    def store(b, p, value):
        re, im = value
        middle[b * first + p, :, :lanes] = jnp.zeros_like(im) if re is None else re
        middle[b * first + p, :, lanes:] = jnp.zeros_like(re) if im is None else im

    def fetch(b, p):
        return (middle[b * first + p, :, :lanes], middle[b * first + p, :, lanes:])

    def twist(k1, value):
        c, s = twist_ref[k1 : k1 + 1, :lanes], twist_ref[k1 : k1 + 1, lanes:]
        return (value[0] * c - value[1] * s, value[0] * s + value[1] * c)

    def place(k1, value):
        turned[k1, :, :lanes], turned[k1, :, lanes:] = twist(k1, value)

    def forward(load, spec):
        across_rows(load, place, count, count, store, fetch)
        for part in chunks:
            x = turned[part].reshape(-1, width)
            spec[part] = lane_dft(x, matrix_ref[...]).reshape(-1, channels, width)

    def inverse(left, right, conjugate_left, emit):
        for part in chunks:
            lr, li = left[part, :, :lanes], left[part, :, lanes:]
            rr, ri = right[part, :, :lanes], right[part, :, lanes:]
            if conjugate_left:
                re, im = lr * rr + li * ri, li * rr - lr * ri
            else:
                re, im = lr * rr - li * ri, -(lr * ri + li * rr)
            x = jnp.concatenate([re.reshape(-1, lanes), im.reshape(-1, lanes)], axis=1)
            turned[part] = lane_dft(x, matrix_ref[...]).reshape(-1, channels, width)

        def load(k1):
            return twist(k1, (turned[k1, :, :lanes], turned[k1, :, lanes:]))

        across_rows(load, emit, count, count // 2, store, fetch)

    return forward, inverse


def token_blocks(ref, order, kind, pair, batch, channels, live):
    pieces = ref.shape[1] // (2 * batch * channels)

    def where(n1, sequence):
        at = block_rows(kind, 2 * pair + sequence, n1 % pieces, batch, pieces, channels)
        return order.index(n1 // pieces), at

    def load(n1):
        if n1 >= live:
            return None
        return (ref[where(n1, 0)], ref[where(n1, 1)])

    def emit(n1, value):
        ref[where(n1, 0)] = value[0]
        ref[where(n1, 1)] = -value[1]

    return load, emit


def filter_kernel(filter_ref, twist_ref, matrix_ref, spec_ref, middle, turned):
    length = filter_ref.shape[1]
    lanes = twist_ref.shape[1] // 2
    forward, _ = transforms(twist_ref, matrix_ref, middle, turned)

    def load(n1):
        if n1 * lanes >= length:
            return None
        return (filter_ref[:, n1 * lanes : (n1 + 1) * lanes] * (0.5 / length), None)

    forward(load, spec_ref)


def convolve_kernel(
    order, held_ref, filter_ref, twist_ref, matrix_ref, back_hbm, mixed_ref, upstream_ref,
    back, middles, turneds, out_sems,
):
    pairs, count, channels, _ = mixed_ref.shape
    half = back.shape[1] // 2
    kinds = (mixed_ref, upstream_ref)
    scratch = [
        transforms(twist_ref, matrix_ref, middles.at[kind], turneds.at[kind]) for kind in range(2)
    ]

    def send(kind):
        span = pl.ds(kind * half, half)
        return pltpu.make_async_copy(back.at[:, span], back_hbm.at[:, span], out_sems.at[kind])

    for pair in range(pairs):
        for kind in range(2):
            load, _ = token_blocks(held_ref, order, kind, pair, 2 * pairs, channels, count // 2)
            scratch[kind][0](load, kinds[kind].at[pair])
        for kind in range(2):
            _, emit = token_blocks(back, order, kind, pair, 2 * pairs, channels, count // 2)
            scratch[kind][1](filter_ref, kinds[kind].at[pair], kind == 1, emit)
            if pair == pairs - 1:
                send(kind).start()
    for kind in range(2):
        send(kind).wait()


def lag_kernel(scaling, mixed_ref, upstream_ref, twist_ref, matrix_ref, lag_ref, middle, turned):
    lanes = twist_ref.shape[1] // 2
    groups, _, share = lag_ref.shape
    group = lax.axis_index("batch")
    _, inverse = transforms(twist_ref, matrix_ref, middle, turned)
    for pair in range(mixed_ref.shape[0]):

        def emit(n1, value):
            at = n1 * lanes
            slot = lax.rem(at // share - group + groups, groups)
            span = slice(at % share, at % share + lanes)
            if pair == 0:
                lag_ref[slot, :, span] = value[0] * scaling
            else:
                lag_ref[slot, :, span] += value[0] * scaling

        inverse(mixed_ref.at[pair], upstream_ref.at[pair], True, emit)


def output_kernel(
    order, query_ref, key_ref, value_ref, cotangent_ref, skip_ref, home_ref, *refs
):
    *results, ready, out_sems = refs
    shards, _, lanes = home_ref.shape
    batch, tokens, all_channels = query_ref.shape
    channels, pieces = all_channels // shards, tokens // lanes
    skip = skip_ref[...]

    def columns(kind, b):
        turned = []
        for piece in range(pieces):
            at = block_rows(kind, b, piece, batch, pieces, channels)
            blocks = [home_ref[order.index(shard), at] for shard in range(shards)]
            turned.append(jnp.transpose(jnp.concatenate(blocks, axis=0)))
        return jnp.concatenate(turned, axis=0)

    def finish(i, b):
        return pltpu.make_async_copy(ready.at[i, b], results[i].at[b], out_sems.at[i, b])

    for b in range(batch):
        query, key, value, cotangent = query_ref[b], key_ref[b], value_ref[b], cotangent_ref[b]
        hidden = columns(0, b) + skip * (key * value)
        ready[0, b] = query * hidden
        finish(0, b).start()
        ready[1, b] = cotangent * hidden
        finish(1, b).start()
        mixed_grad = columns(1, b) + skip * (cotangent * query)
        ready[2, b] = mixed_grad * value
        finish(2, b).start()
        ready[3, b] = mixed_grad * key
        finish(3, b).start()
    for b in range(batch):
        for i in range(4):
            finish(i, b).wait()


def per_device(query_gate, key_gate, value_input, filters, skip_gain, cotangent, *, shards, groups):
    batch, tokens, all_channels = query_gate.shape
    channels, length = filters.shape
    lanes = 128 if 2 * length // 128 <= 64 else tokens
    count = 2 * length // lanes
    twist, matrix = tables(count, lanes)
    order = exchange_order(shards)
    lane_work = 2 * 3 * count * channels * (2 * lanes) ** 2

    def of(*shape):
        return jax.ShapeDtypeStruct(shape, jnp.float32)

    def call(kernel, name, stages, out_shape, scratch, *arrays, **options):
        return pl.pallas_call(
            kernel,
            out_shape=out_shape,
            scratch_shapes=scratch,
            compiler_params=pltpu.CompilerParams(vmem_limit_bytes=VMEM_BYTES),
            cost_estimate=pl.CostEstimate(
                flops=stages * lane_work, bytes_accessed=stages * 4 * batch * channels * length,
                transcendentals=0,
            ),
            name=name,
            **options,
        )(*arrays)

    def exchange(blocks):
        return lax.all_to_all(
            blocks, "seq", split_axis=0, concat_axis=0, tiled=True, axis_index_groups=[order]
        )

    rows = 2 * batch * channels * tokens // lanes
    swap = of(shards, rows, lanes)
    anywhere = pl.BlockSpec(memory_space=pl.ANY)
    in_vmem = pl.BlockSpec(memory_space=pltpu.VMEM)
    spectrum = of(batch // 2, count, channels, 2 * lanes)
    work = [pltpu.VMEM((count, channels, 2 * lanes), jnp.float32)] * 2
    sent = call(
        functools.partial(gate_kernel, order),
        "gate", 1, swap,
        [
            pltpu.VMEM((4, batch, tokens, all_channels), jnp.float32),
            pltpu.VMEM((shards, rows, lanes), jnp.float32),
            pltpu.SemaphoreType.DMA((4, batch)),
            pltpu.SemaphoreType.DMA((2, batch)),
        ],
        *(
            pltpu.with_memory_space_constraint(x, pltpu.HBM)
            for x in (query_gate, key_gate, value_input, cotangent)
        ),
        in_specs=[pl.BlockSpec(memory_space=pltpu.HBM)] * 4,
        out_specs=anywhere,
    )
    held = exchange(sent)
    filter_spec = call(
        filter_kernel, "filter", 2, of(count, channels, 2 * lanes), work, filters, twist, matrix
    )
    back, mixed_spec, upstream_spec = call(
        functools.partial(convolve_kernel, order),
        "convolve", 8, (swap, spectrum, spectrum),
        [
            pltpu.VMEM((shards, rows, lanes), jnp.float32),
            pltpu.VMEM((2, count, channels, 2 * lanes), jnp.float32),
            pltpu.VMEM((2, count, channels, 2 * lanes), jnp.float32),
            pltpu.SemaphoreType.DMA((2,)),
        ],
        held, filter_spec, twist, matrix,
        out_specs=(anywhere, in_vmem, in_vmem),
    )
    home = exchange(back)
    lag = call(
        functools.partial(lag_kernel, 1.0 / (2.0 * length * math.sqrt(length))),
        "lags", 2, of(groups, channels, length // groups), work,
        mixed_spec, upstream_spec, twist, matrix,
    )
    filter_grad = lag[0]
    for step in range(1, groups):
        pairs = [(source, (source + step) % groups) for source in range(groups)]
        filter_grad = filter_grad + lax.ppermute(lag[step], "batch", pairs)
    output, query_grad, key_grad, value_grad = call(
        functools.partial(output_kernel, order),
        "outputs", 2, (of(*query_gate.shape),) * 4,
        [
            pltpu.VMEM((4, batch, tokens, all_channels), jnp.float32),
            pltpu.SemaphoreType.DMA((4, batch)),
        ],
        query_gate, key_gate, value_input, cotangent, skip_gain.reshape(1, all_channels),
        home,
        out_specs=(anywhere,) * 4,
    )
    return (output, query_grad, key_grad, value_grad, filter_grad)


def solution(mesh):
    in_specs = (
        P("batch", "seq", None),
        P("batch", "seq", None),
        P("batch", "seq", None),
        P("seq", None),
        P(),
        P("batch", "seq", None),
    )
    out_specs = (
        P("batch", "seq", None),
        P("batch", "seq", None),
        P("batch", "seq", None),
        P("batch", "seq", None),
        P("seq", "batch"),
    )
    shards, groups = mesh.shape["seq"], mesh.shape["batch"]

    def whole(*arrays):
        return per_device(*arrays, shards=shards, groups=groups)

    return jax.shard_map(whole, mesh=mesh, in_specs=in_specs, out_specs=out_specs, check_vma=False)
```

```python
import functools
import math

import jax
import jax.numpy as jnp
import ml_dtypes
import numpy as np
from jax import lax
from jax.experimental import pallas as pl
from jax.experimental.pallas import tpu as pltpu
from jax.sharding import PartitionSpec as P

VMEM_BYTES = 48 * 1024 * 1024
ROW_CHUNK = 128


def add(a, b):
    if a is None:
        return b
    if b is None:
        return a
    return a + b


def sub(a, b):
    if b is None:
        return a
    if a is None:
        return -b
    return a - b


def scale(a, factor):
    if a is None or factor == 1.0:
        return a
    if factor == -1.0:
        return -a
    return a * factor


def turn(x, step, period):
    if x is None:
        return None
    re, im = x
    step = step % period
    if (4 * step) % period == 0:
        quarter = 4 * step // period
        if quarter == 0:
            return (re, im)
        if quarter == 1:
            return (im, scale(re, -1.0))
        if quarter == 2:
            return (scale(re, -1.0), scale(im, -1.0))
        return (scale(im, -1.0), re)
    angle = -2.0 * math.pi * step / period
    c, s = math.cos(angle), math.sin(angle)
    if (8 * step) % period == 0:
        root = math.sqrt(0.5)
        total, difference = add(re, im), sub(re, im)
        if c * s > 0:
            return (scale(difference, math.copysign(root, c)), scale(total, math.copysign(root, c)))
        return (scale(total, math.copysign(root, c)), scale(sub(im, re), math.copysign(root, c)))
    return (sub(scale(re, c), scale(im, s)), add(scale(re, s), scale(im, c)))


def complex_add(x, y):
    if x is None:
        return y
    if y is None:
        return x
    return (add(x[0], y[0]), add(x[1], y[1]))


def complex_sub(x, y):
    if y is None:
        return x
    if x is None:
        return (scale(y[0], -1.0), scale(y[1], -1.0))
    return (sub(x[0], y[0]), sub(x[1], y[1]))


def small_dft(values):
    size = len(values)
    if size == 1:
        return list(values)
    even = small_dft(values[0::2])
    odd = small_dft(values[1::2])
    odd = [turn(value, step, size) for step, value in enumerate(odd)]
    return [complex_add(e, o) for e, o in zip(even, odd)] + [
        complex_sub(e, o) for e, o in zip(even, odd)
    ]


def factors_of(size):
    first = 1
    while first * first < size:
        first *= 2
    return (size // first, first)


def across_rows(load, emit, count, kept, store, fetch):
    first, second = factors_of(count)
    for b in range(second):
        values = small_dft([load(second * a + b) for a in range(first)])
        for p, value in enumerate(values):
            store(b, p, turn(value, b * p, count))
    for p in range(first):
        values = small_dft([fetch(b, p) for b in range(second)])
        for q, value in enumerate(values):
            k1 = p + first * q
            if k1 < kept:
                emit(k1, value)


def tables(count, channels, lanes):
    k1 = np.arange(count)[:, None]
    n2 = np.arange(lanes)[None, :]
    phase = -2.0 * np.pi * ((k1 * n2) % (count * lanes)) / (count * lanes)
    twist = np.concatenate([np.cos(phase), np.sin(phase)], axis=1).astype(np.float32)
    twist = np.repeat(twist[:, None], channels, axis=1)
    j = np.arange(lanes)
    phase = -2.0 * np.pi * ((j[:, None] * j[None, :]) % lanes) / lanes
    c, s = np.cos(phase), np.sin(phase)
    matrix = np.block([[c, s], [-s, c]]).astype(np.float32)
    high = matrix.astype(ml_dtypes.bfloat16)
    low = (matrix - high.astype(np.float32)).astype(ml_dtypes.bfloat16)
    return twist, np.concatenate([high, high, low], axis=0)


def lane_dft(x, matrix):
    high = x.astype(jnp.bfloat16)
    low = (x - high.astype(jnp.float32)).astype(jnp.bfloat16)
    return jnp.dot(
        jnp.concatenate([high, low, high], axis=1), matrix, preferred_element_type=jnp.float32
    )


def exchange_order(shards):
    if shards < 8:
        return list(range(shards))
    steps = shards // 4
    uses = np.zeros((shards, shards, 2, steps, 2), np.int32)
    for a in range(shards):
        for b in range(shards):
            (za, ya), (zb, yb) = (a // 4, a // 2 % 2), (b // 4, b // 2 % 2)
            for z in range(min(za, zb), max(za, zb)):
                uses[a, b, ya, z, int(za > zb)] = 1
    uses = uses.reshape(shards, shards, -1)
    place, shift = np.arange(shards)[:, None], np.arange(1, shards)[None, :]

    def load(order):
        total = 0
        for partner in ((place + shift) % shards, place ^ shift):
            total += uses[order[place], order[partner]].sum(axis=0).max(axis=1).sum()
        return int(total)

    draw = np.random.RandomState(0)
    order = 5 * np.arange(shards) % shards
    least = load(order)
    for _ in range(24000 // shards):
        i, j = draw.randint(shards), draw.randint(shards)
        order[[i, j]] = order[[j, i]]
        now = load(order)
        if now <= least:
            least = now
        else:
            order[[i, j]] = order[[j, i]]
    return [int(shard) for shard in order]


def block_rows(kind, sequence, piece, batch, pieces, channels):
    first = ((kind * batch + sequence) * pieces + piece) * channels
    return slice(first, first + channels)


def gate_kernel(order, query_hbm, key_hbm, value_hbm, cotangent_hbm, sent_hbm, held, sent, sems, out_sems):
    shards, rows, lanes = sent.shape
    _, batch, tokens, all_channels = held.shape
    channels, pieces = all_channels // shards, tokens // lanes
    sources = (key_hbm, value_hbm, cotangent_hbm, query_hbm)

    def copy(b, i):
        return pltpu.make_async_copy(sources[i].at[b], held.at[i, b], sems.at[i, b])

    def send(kind, b):
        first = block_rows(kind, b, 0, batch, pieces, channels).start
        span = pl.ds(first, pieces * channels)
        return pltpu.make_async_copy(sent.at[:, span], sent_hbm.at[:, span], out_sems.at[kind, b])

    parts = [(kind, b) for kind in range(2) for b in range(batch)]
    for kind, b in parts:
        copy(b, 2 * kind).start()
        copy(b, 2 * kind + 1).start()
    for kind, b in parts:
        copy(b, 2 * kind).wait()
        copy(b, 2 * kind + 1).wait()
        columns = jnp.transpose(held[2 * kind, b] * held[2 * kind + 1, b])
        columns = columns.reshape(shards, channels, tokens)
        for piece in range(pieces):
            at = block_rows(kind, b, piece, batch, pieces, channels)
            for place, shard in enumerate(order):
                sent[place, at] = columns[shard, :, piece * lanes : (piece + 1) * lanes]
        send(kind, b).start()
    for kind, b in parts:
        send(kind, b).wait()


def transforms(twist_ref, matrix_ref, middle, turned):
    count, channels, width = turned.shape
    lanes = width // 2
    first, _ = factors_of(count)
    per_chunk = ROW_CHUNK // channels
    chunks = [slice(at, min(at + per_chunk, count)) for at in range(0, count, per_chunk)]

    def store(b, p, value):
        re, im = value
        middle[b * first + p, :, :lanes] = jnp.zeros_like(im) if re is None else re
        middle[b * first + p, :, lanes:] = jnp.zeros_like(re) if im is None else im

    def fetch(b, p):
        return (middle[b * first + p, :, :lanes], middle[b * first + p, :, lanes:])

    def twist(k1, value):
        c, s = twist_ref[k1, :, :lanes], twist_ref[k1, :, lanes:]
        return (value[0] * c - value[1] * s, value[0] * s + value[1] * c)

    def place(k1, value):
        turned[k1, :, :lanes], turned[k1, :, lanes:] = twist(k1, value)

    def forward(load, spec):
        across_rows(load, place, count, count, store, fetch)
        for part in chunks:
            x = turned[part].reshape(-1, width)
            spec[part] = lane_dft(x, matrix_ref[...]).reshape(-1, channels, width)

    def inverse(left, right, conjugate_left, emit):
        for part in chunks:
            lr, li = left[part, :, :lanes], left[part, :, lanes:]
            rr, ri = right[part, :, :lanes], right[part, :, lanes:]
            if conjugate_left:
                re, im = lr * rr + li * ri, li * rr - lr * ri
            else:
                re, im = lr * rr - li * ri, -(lr * ri + li * rr)
            x = jnp.concatenate([re.reshape(-1, lanes), im.reshape(-1, lanes)], axis=1)
            turned[part] = lane_dft(x, matrix_ref[...]).reshape(-1, channels, width)

        def load(k1):
            return twist(k1, (turned[k1, :, :lanes], turned[k1, :, lanes:]))

        across_rows(load, emit, count, count // 2, store, fetch)

    return forward, inverse


def token_blocks(ref, order, kind, pair, batch, channels, live):
    pieces = ref.shape[1] // (2 * batch * channels)

    def where(n1, sequence):
        at = block_rows(kind, 2 * pair + sequence, n1 % pieces, batch, pieces, channels)
        return order.index(n1 // pieces), at

    def load(n1):
        if n1 >= live:
            return None
        return (ref[where(n1, 0)], ref[where(n1, 1)])

    def emit(n1, value):
        ref[where(n1, 0)] = value[0]
        ref[where(n1, 1)] = -value[1]

    return load, emit


def filter_kernel(filter_ref, twist_ref, matrix_ref, spec_ref, middle, turned):
    length = filter_ref.shape[1]
    lanes = twist_ref.shape[2] // 2
    forward, _ = transforms(twist_ref, matrix_ref, middle, turned)

    def load(n1):
        if n1 * lanes >= length:
            return None
        return (filter_ref[:, n1 * lanes : (n1 + 1) * lanes] * (0.5 / length), None)

    forward(load, spec_ref)


def convolve_kernel(
    order, held_ref, filter_ref, twist_ref, matrix_ref, back_hbm, mixed_ref, upstream_ref,
    back, middles, turneds, out_sems,
):
    pairs, count, channels, _ = mixed_ref.shape
    half = back.shape[1] // 2
    kinds = (mixed_ref, upstream_ref)
    scratch = [
        transforms(twist_ref, matrix_ref, middles.at[kind], turneds.at[kind]) for kind in range(2)
    ]

    def send(kind):
        span = pl.ds(kind * half, half)
        return pltpu.make_async_copy(back.at[:, span], back_hbm.at[:, span], out_sems.at[kind])

    for pair in range(pairs):
        for kind in range(2):
            load, _ = token_blocks(held_ref, order, kind, pair, 2 * pairs, channels, count // 2)
            scratch[kind][0](load, kinds[kind].at[pair])
        for kind in range(2):
            _, emit = token_blocks(back, order, kind, pair, 2 * pairs, channels, count // 2)
            scratch[kind][1](filter_ref, kinds[kind].at[pair], kind == 1, emit)
            if pair == pairs - 1:
                send(kind).start()
    for kind in range(2):
        send(kind).wait()


def lag_kernel(scaling, mixed_ref, upstream_ref, twist_ref, matrix_ref, lag_ref, middle, turned):
    lanes = twist_ref.shape[2] // 2
    groups, _, share = lag_ref.shape
    group = lax.axis_index("batch")
    _, inverse = transforms(twist_ref, matrix_ref, middle, turned)
    for pair in range(mixed_ref.shape[0]):

        def emit(n1, value):
            at = n1 * lanes
            slot = lax.rem(at // share - group + groups, groups)
            span = slice(at % share, at % share + lanes)
            if pair == 0:
                lag_ref[slot, :, span] = value[0] * scaling
            else:
                lag_ref[slot, :, span] += value[0] * scaling

        inverse(mixed_ref.at[pair], upstream_ref.at[pair], True, emit)


def output_kernel(
    order, query_ref, key_ref, value_ref, cotangent_ref, skip_ref, home_ref, *refs
):
    *results, ready, out_sems = refs
    shards, _, lanes = home_ref.shape
    batch, tokens, all_channels = query_ref.shape
    channels, pieces = all_channels // shards, tokens // lanes
    skip = skip_ref[...]

    def columns(kind, b):
        turned = []
        for piece in range(pieces):
            at = block_rows(kind, b, piece, batch, pieces, channels)
            blocks = [home_ref[order.index(shard), at] for shard in range(shards)]
            turned.append(jnp.transpose(jnp.concatenate(blocks, axis=0)))
        return jnp.concatenate(turned, axis=0)

    def finish(i, b):
        return pltpu.make_async_copy(ready.at[i, b], results[i].at[b], out_sems.at[i, b])

    for b in range(batch):
        query, key, value, cotangent = query_ref[b], key_ref[b], value_ref[b], cotangent_ref[b]
        hidden = columns(0, b) + skip * (key * value)
        ready[0, b] = query * hidden
        finish(0, b).start()
        ready[1, b] = cotangent * hidden
        finish(1, b).start()
        mixed_grad = columns(1, b) + skip * (cotangent * query)
        ready[2, b] = mixed_grad * value
        finish(2, b).start()
        ready[3, b] = mixed_grad * key
        finish(3, b).start()
    for b in range(batch):
        for i in range(4):
            finish(i, b).wait()


def per_device(query_gate, key_gate, value_input, filters, skip_gain, cotangent, *, shards, groups):
    batch, tokens, all_channels = query_gate.shape
    channels, length = filters.shape
    lanes = 128 if 2 * length // 128 <= 64 else tokens
    count = 2 * length // lanes
    twist, matrix = tables(count, channels, lanes)
    order = exchange_order(shards)
    lane_work = 2 * 3 * count * channels * (2 * lanes) ** 2

    def of(*shape):
        return jax.ShapeDtypeStruct(shape, jnp.float32)

    def call(kernel, name, stages, out_shape, scratch, *arrays, **options):
        return pl.pallas_call(
            kernel,
            out_shape=out_shape,
            scratch_shapes=scratch,
            compiler_params=pltpu.CompilerParams(vmem_limit_bytes=VMEM_BYTES),
            cost_estimate=pl.CostEstimate(
                flops=stages * lane_work, bytes_accessed=stages * 4 * batch * channels * length,
                transcendentals=0,
            ),
            name=name,
            **options,
        )(*arrays)

    def exchange(blocks):
        return lax.all_to_all(
            blocks, "seq", split_axis=0, concat_axis=0, tiled=True, axis_index_groups=[order]
        )

    rows = 2 * batch * channels * tokens // lanes
    swap = of(shards, rows, lanes)
    anywhere = pl.BlockSpec(memory_space=pl.ANY)
    in_vmem = pl.BlockSpec(memory_space=pltpu.VMEM)
    spectrum = of(batch // 2, count, channels, 2 * lanes)
    work = [pltpu.VMEM((count, channels, 2 * lanes), jnp.float32)] * 2
    sent = call(
        functools.partial(gate_kernel, order),
        "gate", 1, swap,
        [
            pltpu.VMEM((4, batch, tokens, all_channels), jnp.float32),
            pltpu.VMEM((shards, rows, lanes), jnp.float32),
            pltpu.SemaphoreType.DMA((4, batch)),
            pltpu.SemaphoreType.DMA((2, batch)),
        ],
        *(
            pltpu.with_memory_space_constraint(x, pltpu.HBM)
            for x in (query_gate, key_gate, value_input, cotangent)
        ),
        in_specs=[pl.BlockSpec(memory_space=pltpu.HBM)] * 4,
        out_specs=anywhere,
    )
    held = exchange(sent)
    filter_spec = call(
        filter_kernel, "filter", 2, of(count, channels, 2 * lanes), work, filters, twist, matrix
    )
    back, mixed_spec, upstream_spec = call(
        functools.partial(convolve_kernel, order),
        "convolve", 8, (swap, spectrum, spectrum),
        [
            pltpu.VMEM((shards, rows, lanes), jnp.float32),
            pltpu.VMEM((2, count, channels, 2 * lanes), jnp.float32),
            pltpu.VMEM((2, count, channels, 2 * lanes), jnp.float32),
            pltpu.SemaphoreType.DMA((2,)),
        ],
        held, filter_spec, twist, matrix,
        out_specs=(anywhere, in_vmem, in_vmem),
    )
    home = exchange(back)
    lag = call(
        functools.partial(lag_kernel, 1.0 / (2.0 * length * math.sqrt(length))),
        "lags", 2, of(groups, channels, length // groups), work,
        mixed_spec, upstream_spec, twist, matrix,
    )
    filter_grad = lag[0]
    for step in range(1, groups):
        pairs = [(source, (source + step) % groups) for source in range(groups)]
        filter_grad = filter_grad + lax.ppermute(lag[step], "batch", pairs)
    output, query_grad, key_grad, value_grad = call(
        functools.partial(output_kernel, order),
        "outputs", 2, (of(*query_gate.shape),) * 4,
        [
            pltpu.VMEM((4, batch, tokens, all_channels), jnp.float32),
            pltpu.SemaphoreType.DMA((4, batch)),
        ],
        query_gate, key_gate, value_input, cotangent, skip_gain.reshape(1, all_channels),
        home,
        out_specs=(anywhere,) * 4,
    )
    return (output, query_grad, key_grad, value_grad, filter_grad)


def solution(mesh):
    in_specs = (
        P("batch", "seq", None),
        P("batch", "seq", None),
        P("batch", "seq", None),
        P("seq", None),
        P(),
        P("batch", "seq", None),
    )
    out_specs = (
        P("batch", "seq", None),
        P("batch", "seq", None),
        P("batch", "seq", None),
        P("batch", "seq", None),
        P("seq", "batch"),
    )
    shards, groups = mesh.shape["seq"], mesh.shape["batch"]

    def whole(*arrays):
        return per_device(*arrays, shards=shards, groups=groups)

    return jax.shard_map(whole, mesh=mesh, in_specs=in_specs, out_specs=out_specs, check_vma=False)
```

```python
import functools
import math

import jax
import jax.numpy as jnp
import ml_dtypes
import numpy as np
from jax import lax
from jax.experimental import pallas as pl
from jax.experimental.pallas import tpu as pltpu
from jax.sharding import PartitionSpec as P

VMEM_BYTES = 48 * 1024 * 1024
ROW_CHUNK = 256


def add(a, b):
    if a is None:
        return b
    if b is None:
        return a
    return a + b


def sub(a, b):
    if b is None:
        return a
    if a is None:
        return -b
    return a - b


def scale(a, factor):
    if a is None or factor == 1.0:
        return a
    if factor == -1.0:
        return -a
    return a * factor


def turn(x, step, period):
    if x is None:
        return None
    re, im = x
    step = step % period
    if (4 * step) % period == 0:
        quarter = 4 * step // period
        if quarter == 0:
            return (re, im)
        if quarter == 1:
            return (im, scale(re, -1.0))
        if quarter == 2:
            return (scale(re, -1.0), scale(im, -1.0))
        return (scale(im, -1.0), re)
    angle = -2.0 * math.pi * step / period
    c, s = math.cos(angle), math.sin(angle)
    if (8 * step) % period == 0:
        root = math.sqrt(0.5)
        total, difference = add(re, im), sub(re, im)
        if c * s > 0:
            return (scale(difference, math.copysign(root, c)), scale(total, math.copysign(root, c)))
        return (scale(total, math.copysign(root, c)), scale(sub(im, re), math.copysign(root, c)))
    return (sub(scale(re, c), scale(im, s)), add(scale(re, s), scale(im, c)))


def complex_add(x, y):
    if x is None:
        return y
    if y is None:
        return x
    return (add(x[0], y[0]), add(x[1], y[1]))


def complex_sub(x, y):
    if y is None:
        return x
    if x is None:
        return (scale(y[0], -1.0), scale(y[1], -1.0))
    return (sub(x[0], y[0]), sub(x[1], y[1]))


def small_dft(values):
    size = len(values)
    if size == 1:
        return list(values)
    even = small_dft(values[0::2])
    odd = small_dft(values[1::2])
    odd = [turn(value, step, size) for step, value in enumerate(odd)]
    return [complex_add(e, o) for e, o in zip(even, odd)] + [
        complex_sub(e, o) for e, o in zip(even, odd)
    ]


def factors_of(size):
    first = 1
    while first * first < size:
        first *= 2
    return (size // first, first)


def across_rows(load, emit, count, kept, store, fetch):
    first, second = factors_of(count)
    for b in range(second):
        values = small_dft([load(second * a + b) for a in range(first)])
        for p, value in enumerate(values):
            store(b, p, turn(value, b * p, count))
    for p in range(first):
        values = small_dft([fetch(b, p) for b in range(second)])
        for q, value in enumerate(values):
            k1 = p + first * q
            if k1 < kept:
                emit(k1, value)


def tables(count, lanes):
    k1 = np.arange(count)[:, None]
    n2 = np.arange(lanes)[None, :]
    phase = -2.0 * np.pi * ((k1 * n2) % (count * lanes)) / (count * lanes)
    twist = np.concatenate([np.cos(phase), np.sin(phase)], axis=1).astype(np.float32)
    j = np.arange(lanes)
    phase = -2.0 * np.pi * ((j[:, None] * j[None, :]) % lanes) / lanes
    c, s = np.cos(phase), np.sin(phase)
    matrix = np.block([[c, s], [-s, c]]).astype(np.float32)
    high = matrix.astype(ml_dtypes.bfloat16)
    low = (matrix - high.astype(np.float32)).astype(ml_dtypes.bfloat16)
    return twist, np.concatenate([high, high, low], axis=0)


def lane_dft(x, matrix):
    high = x.astype(jnp.bfloat16)
    low = (x - high.astype(jnp.float32)).astype(jnp.bfloat16)
    return jnp.dot(
        jnp.concatenate([high, low, high], axis=1), matrix, preferred_element_type=jnp.float32
    )


def exchange_order(shards):
    if shards < 8:
        return list(range(shards))
    steps = shards // 4
    uses = np.zeros((shards, shards, 2, steps, 2), np.int32)
    for a in range(shards):
        for b in range(shards):
            (za, ya), (zb, yb) = (a // 4, a // 2 % 2), (b // 4, b // 2 % 2)
            for z in range(min(za, zb), max(za, zb)):
                uses[a, b, ya, z, int(za > zb)] = 1
    uses = uses.reshape(shards, shards, -1)
    place, shift = np.arange(shards)[:, None], np.arange(1, shards)[None, :]

    def load(order):
        total = 0
        for partner in ((place + shift) % shards, place ^ shift):
            total += uses[order[place], order[partner]].sum(axis=0).max(axis=1).sum()
        return int(total)

    draw = np.random.RandomState(0)
    order = 5 * np.arange(shards) % shards
    least = load(order)
    for _ in range(24000 // shards):
        i, j = draw.randint(shards), draw.randint(shards)
        order[[i, j]] = order[[j, i]]
        now = load(order)
        if now <= least:
            least = now
        else:
            order[[i, j]] = order[[j, i]]
    return [int(shard) for shard in order]


def block_rows(kind, sequence, piece, batch, pieces, channels):
    first = ((kind * batch + sequence) * pieces + piece) * channels
    return slice(first, first + channels)


def gate_kernel(order, query_hbm, key_hbm, value_hbm, cotangent_hbm, sent_hbm, held, sent, sems, out_sems):
    shards, rows, lanes = sent.shape
    _, batch, tokens, all_channels = held.shape
    channels, pieces = all_channels // shards, tokens // lanes
    sources = (key_hbm, value_hbm, cotangent_hbm, query_hbm)

    def copy(b, i):
        return pltpu.make_async_copy(sources[i].at[b], held.at[i, b], sems.at[i, b])

    def send(kind, b):
        first = block_rows(kind, b, 0, batch, pieces, channels).start
        span = pl.ds(first, pieces * channels)
        return pltpu.make_async_copy(sent.at[:, span], sent_hbm.at[:, span], out_sems.at[kind, b])

    parts = [(kind, b) for kind in range(2) for b in range(batch)]
    for kind, b in parts:
        copy(b, 2 * kind).start()
        copy(b, 2 * kind + 1).start()
    for kind, b in parts:
        copy(b, 2 * kind).wait()
        copy(b, 2 * kind + 1).wait()
        columns = jnp.transpose(held[2 * kind, b] * held[2 * kind + 1, b])
        columns = columns.reshape(shards, channels, tokens)
        for piece in range(pieces):
            at = block_rows(kind, b, piece, batch, pieces, channels)
            for place, shard in enumerate(order):
                sent[place, at] = columns[shard, :, piece * lanes : (piece + 1) * lanes]
        send(kind, b).start()
    for kind, b in parts:
        send(kind, b).wait()


def transforms(twist_ref, matrix_ref, middle, turned):
    count, channels, width = turned.shape
    lanes = width // 2
    first, _ = factors_of(count)
    per_chunk = ROW_CHUNK // channels
    chunks = [slice(at, min(at + per_chunk, count)) for at in range(0, count, per_chunk)]

    def store(b, p, value):
        re, im = value
        middle[b * first + p, :, :lanes] = jnp.zeros_like(im) if re is None else re
        middle[b * first + p, :, lanes:] = jnp.zeros_like(re) if im is None else im

    def fetch(b, p):
        return (middle[b * first + p, :, :lanes], middle[b * first + p, :, lanes:])

    def twist(k1, value):
        c, s = twist_ref[k1 : k1 + 1, :lanes], twist_ref[k1 : k1 + 1, lanes:]
        return (value[0] * c - value[1] * s, value[0] * s + value[1] * c)

    def place(k1, value):
        turned[k1, :, :lanes], turned[k1, :, lanes:] = twist(k1, value)

    def forward(load, spec):
        across_rows(load, place, count, count, store, fetch)
        for part in chunks:
            x = turned[part].reshape(-1, width)
            spec[part] = lane_dft(x, matrix_ref[...]).reshape(-1, channels, width)

    def inverse(left, right, conjugate_left, emit):
        for part in chunks:
            lr, li = left[part, :, :lanes], left[part, :, lanes:]
            rr, ri = right[part, :, :lanes], right[part, :, lanes:]
            if conjugate_left:
                re, im = lr * rr + li * ri, li * rr - lr * ri
            else:
                re, im = lr * rr - li * ri, -(lr * ri + li * rr)
            x = jnp.concatenate([re.reshape(-1, lanes), im.reshape(-1, lanes)], axis=1)
            turned[part] = lane_dft(x, matrix_ref[...]).reshape(-1, channels, width)

        def load(k1):
            return twist(k1, (turned[k1, :, :lanes], turned[k1, :, lanes:]))

        across_rows(load, emit, count, count // 2, store, fetch)

    return forward, inverse


def token_blocks(ref, order, kind, pair, batch, channels, live):
    pieces = ref.shape[1] // (2 * batch * channels)

    def where(n1, sequence):
        at = block_rows(kind, 2 * pair + sequence, n1 % pieces, batch, pieces, channels)
        return order.index(n1 // pieces), at

    def load(n1):
        if n1 >= live:
            return None
        return (ref[where(n1, 0)], ref[where(n1, 1)])

    def emit(n1, value):
        ref[where(n1, 0)] = value[0]
        ref[where(n1, 1)] = -value[1]

    return load, emit


def filter_kernel(filter_ref, twist_ref, matrix_ref, spec_ref, middle, turned):
    length = filter_ref.shape[1]
    lanes = twist_ref.shape[1] // 2
    forward, _ = transforms(twist_ref, matrix_ref, middle, turned)

    def load(n1):
        if n1 * lanes >= length:
            return None
        return (filter_ref[:, n1 * lanes : (n1 + 1) * lanes] * (0.5 / length), None)

    forward(load, spec_ref)


def convolve_kernel(
    order, held_ref, filter_ref, twist_ref, matrix_ref, back_hbm, mixed_ref, upstream_ref,
    back, middles, turneds, out_sems,
):
    pairs, count, channels, _ = mixed_ref.shape
    half = back.shape[1] // 2
    kinds = (mixed_ref, upstream_ref)
    scratch = [
        transforms(twist_ref, matrix_ref, middles.at[kind], turneds.at[kind]) for kind in range(2)
    ]

    def send(kind):
        span = pl.ds(kind * half, half)
        return pltpu.make_async_copy(back.at[:, span], back_hbm.at[:, span], out_sems.at[kind])

    for pair in range(pairs):
        for kind in range(2):
            load, _ = token_blocks(held_ref, order, kind, pair, 2 * pairs, channels, count // 2)
            scratch[kind][0](load, kinds[kind].at[pair])
        for kind in range(2):
            _, emit = token_blocks(back, order, kind, pair, 2 * pairs, channels, count // 2)
            scratch[kind][1](filter_ref, kinds[kind].at[pair], kind == 1, emit)
            if pair == pairs - 1:
                send(kind).start()
    for kind in range(2):
        send(kind).wait()


def lag_kernel(scaling, mixed_ref, upstream_ref, twist_ref, matrix_ref, lag_ref, middle, turned):
    lanes = twist_ref.shape[1] // 2
    groups, _, share = lag_ref.shape
    group = lax.axis_index("batch")
    _, inverse = transforms(twist_ref, matrix_ref, middle, turned)
    for pair in range(mixed_ref.shape[0]):

        def emit(n1, value):
            at = n1 * lanes
            slot = lax.rem(at // share - group + groups, groups)
            span = slice(at % share, at % share + lanes)
            if pair == 0:
                lag_ref[slot, :, span] = value[0] * scaling
            else:
                lag_ref[slot, :, span] += value[0] * scaling

        inverse(mixed_ref.at[pair], upstream_ref.at[pair], True, emit)


def output_kernel(
    order, query_ref, key_ref, value_ref, cotangent_ref, skip_ref, home_ref, *refs
):
    *results, ready, out_sems = refs
    shards, _, lanes = home_ref.shape
    batch, tokens, all_channels = query_ref.shape
    channels, pieces = all_channels // shards, tokens // lanes
    skip = skip_ref[...]

    def columns(kind, b):
        turned = []
        for piece in range(pieces):
            at = block_rows(kind, b, piece, batch, pieces, channels)
            blocks = [home_ref[order.index(shard), at] for shard in range(shards)]
            turned.append(jnp.transpose(jnp.concatenate(blocks, axis=0)))
        return jnp.concatenate(turned, axis=0)

    def finish(i, b):
        return pltpu.make_async_copy(ready.at[i, b], results[i].at[b], out_sems.at[i, b])

    for b in range(batch):
        query, key, value, cotangent = query_ref[b], key_ref[b], value_ref[b], cotangent_ref[b]
        hidden = columns(0, b) + skip * (key * value)
        ready[0, b] = query * hidden
        finish(0, b).start()
        ready[1, b] = cotangent * hidden
        finish(1, b).start()
        mixed_grad = columns(1, b) + skip * (cotangent * query)
        ready[2, b] = mixed_grad * value
        finish(2, b).start()
        ready[3, b] = mixed_grad * key
        finish(3, b).start()
    for b in range(batch):
        for i in range(4):
            finish(i, b).wait()


def per_device(query_gate, key_gate, value_input, filters, skip_gain, cotangent, *, shards, groups):
    batch, tokens, all_channels = query_gate.shape
    channels, length = filters.shape
    lanes, count = tokens, 2 * shards
    twist, matrix = tables(count, lanes)
    order = exchange_order(shards)
    lane_work = 2 * 3 * count * channels * (2 * lanes) ** 2

    def of(*shape):
        return jax.ShapeDtypeStruct(shape, jnp.float32)

    def call(kernel, name, stages, out_shape, scratch, *arrays, **options):
        return pl.pallas_call(
            kernel,
            out_shape=out_shape,
            scratch_shapes=scratch,
            compiler_params=pltpu.CompilerParams(vmem_limit_bytes=VMEM_BYTES),
            cost_estimate=pl.CostEstimate(
                flops=stages * lane_work, bytes_accessed=stages * 4 * batch * channels * length,
                transcendentals=0,
            ),
            name=name,
            **options,
        )(*arrays)

    def exchange(blocks):
        return lax.all_to_all(
            blocks, "seq", split_axis=0, concat_axis=0, tiled=True, axis_index_groups=[order]
        )

    rows = 2 * batch * channels * tokens // lanes
    swap = of(shards, rows, lanes)
    anywhere = pl.BlockSpec(memory_space=pl.ANY)
    in_vmem = pl.BlockSpec(memory_space=pltpu.VMEM)
    spectrum = of(batch // 2, count, channels, 2 * lanes)
    work = [pltpu.VMEM((count, channels, 2 * lanes), jnp.float32)] * 2
    sent = call(
        functools.partial(gate_kernel, order),
        "gate", 1, swap,
        [
            pltpu.VMEM((4, batch, tokens, all_channels), jnp.float32),
            pltpu.VMEM((shards, rows, lanes), jnp.float32),
            pltpu.SemaphoreType.DMA((4, batch)),
            pltpu.SemaphoreType.DMA((2, batch)),
        ],
        *(
            pltpu.with_memory_space_constraint(x, pltpu.HBM)
            for x in (query_gate, key_gate, value_input, cotangent)
        ),
        in_specs=[pl.BlockSpec(memory_space=pltpu.HBM)] * 4,
        out_specs=anywhere,
    )
    held = exchange(sent)
    filter_spec = call(
        filter_kernel, "filter", 2, of(count, channels, 2 * lanes), work, filters, twist, matrix
    )
    back, mixed_spec, upstream_spec = call(
        functools.partial(convolve_kernel, order),
        "convolve", 8, (swap, spectrum, spectrum),
        [
            pltpu.VMEM((shards, rows, lanes), jnp.float32),
            pltpu.VMEM((2, count, channels, 2 * lanes), jnp.float32),
            pltpu.VMEM((2, count, channels, 2 * lanes), jnp.float32),
            pltpu.SemaphoreType.DMA((2,)),
        ],
        held, filter_spec, twist, matrix,
        out_specs=(anywhere, in_vmem, in_vmem),
    )
    home = exchange(back)
    lag = call(
        functools.partial(lag_kernel, 1.0 / (2.0 * length * math.sqrt(length))),
        "lags", 2, of(groups, channels, length // groups), work,
        mixed_spec, upstream_spec, twist, matrix,
    )
    filter_grad = lag[0]
    for step in range(1, groups):
        pairs = [(source, (source + step) % groups) for source in range(groups)]
        filter_grad = filter_grad + lax.ppermute(lag[step], "batch", pairs)
    output, query_grad, key_grad, value_grad = call(
        functools.partial(output_kernel, order),
        "outputs", 2, (of(*query_gate.shape),) * 4,
        [
            pltpu.VMEM((4, batch, tokens, all_channels), jnp.float32),
            pltpu.SemaphoreType.DMA((4, batch)),
        ],
        query_gate, key_gate, value_input, cotangent, skip_gain.reshape(1, all_channels),
        home,
        out_specs=(anywhere,) * 4,
    )
    return (output, query_grad, key_grad, value_grad, filter_grad)


def solution(mesh):
    in_specs = (
        P("batch", "seq", None),
        P("batch", "seq", None),
        P("batch", "seq", None),
        P("seq", None),
        P(),
        P("batch", "seq", None),
    )
    out_specs = (
        P("batch", "seq", None),
        P("batch", "seq", None),
        P("batch", "seq", None),
        P("batch", "seq", None),
        P("seq", "batch"),
    )
    shards, groups = mesh.shape["seq"], mesh.shape["batch"]

    def whole(*arrays):
        return per_device(*arrays, shards=shards, groups=groups)

    return jax.shard_map(whole, mesh=mesh, in_specs=in_specs, out_specs=out_specs, check_vma=False)
```

```python
import functools
import math

import jax
import jax.numpy as jnp
import ml_dtypes
import numpy as np
from jax import lax
from jax.experimental import pallas as pl
from jax.experimental.pallas import tpu as pltpu
from jax.sharding import PartitionSpec as P

VMEM_BYTES = 48 * 1024 * 1024
ROW_CHUNK = 128


def add(a, b):
    if a is None:
        return b
    if b is None:
        return a
    return a + b


def sub(a, b):
    if b is None:
        return a
    if a is None:
        return -b
    return a - b


def scale(a, factor):
    if a is None or factor == 1.0:
        return a
    if factor == -1.0:
        return -a
    return a * factor


def turn(x, step, period):
    if x is None:
        return None
    re, im = x
    step = step % period
    if (4 * step) % period == 0:
        quarter = 4 * step // period
        if quarter == 0:
            return (re, im)
        if quarter == 1:
            return (im, scale(re, -1.0))
        if quarter == 2:
            return (scale(re, -1.0), scale(im, -1.0))
        return (scale(im, -1.0), re)
    angle = -2.0 * math.pi * step / period
    c, s = math.cos(angle), math.sin(angle)
    if (8 * step) % period == 0:
        root = math.sqrt(0.5)
        total, difference = add(re, im), sub(re, im)
        if c * s > 0:
            return (scale(difference, math.copysign(root, c)), scale(total, math.copysign(root, c)))
        return (scale(total, math.copysign(root, c)), scale(sub(im, re), math.copysign(root, c)))
    return (sub(scale(re, c), scale(im, s)), add(scale(re, s), scale(im, c)))


def complex_add(x, y):
    if x is None:
        return y
    if y is None:
        return x
    return (add(x[0], y[0]), add(x[1], y[1]))


def complex_sub(x, y):
    if y is None:
        return x
    if x is None:
        return (scale(y[0], -1.0), scale(y[1], -1.0))
    return (sub(x[0], y[0]), sub(x[1], y[1]))


def small_dft(values):
    size = len(values)
    if size == 1:
        return list(values)
    even = small_dft(values[0::2])
    odd = small_dft(values[1::2])
    odd = [turn(value, step, size) for step, value in enumerate(odd)]
    return [complex_add(e, o) for e, o in zip(even, odd)] + [
        complex_sub(e, o) for e, o in zip(even, odd)
    ]


def factors_of(size):
    first = 1
    while first * first < size:
        first *= 2
    return (size // first, first)


def tables(count, lanes):
    k1 = np.arange(count)[:, None]
    n2 = np.arange(lanes)[None, :]
    phase = -2.0 * np.pi * ((k1 * n2) % (count * lanes)) / (count * lanes)
    twist = np.concatenate([np.cos(phase), np.sin(phase)], axis=1).astype(np.float32)
    j = np.arange(lanes)
    phase = -2.0 * np.pi * ((j[:, None] * j[None, :]) % lanes) / lanes
    c, s = np.cos(phase), np.sin(phase)
    matrix = np.block([[c, s], [-s, c]]).astype(np.float32)
    high = matrix.astype(ml_dtypes.bfloat16)
    low = (matrix - high.astype(np.float32)).astype(ml_dtypes.bfloat16)
    return twist, np.concatenate([high, high, low], axis=0)


def lane_dft(x, matrix):
    high = x.astype(jnp.bfloat16)
    low = (x - high.astype(jnp.float32)).astype(jnp.bfloat16)
    return jnp.dot(
        jnp.concatenate([high, low, high], axis=1), matrix, preferred_element_type=jnp.float32
    )


def exchange_order(shards):
    if shards < 8:
        return list(range(shards))
    steps = shards // 4
    uses = np.zeros((shards, shards, 2, steps, 2), np.int32)
    for a in range(shards):
        for b in range(shards):
            (za, ya), (zb, yb) = (a // 4, a // 2 % 2), (b // 4, b // 2 % 2)
            for z in range(min(za, zb), max(za, zb)):
                uses[a, b, ya, z, int(za > zb)] = 1
    uses = uses.reshape(shards, shards, -1)
    place, shift = np.arange(shards)[:, None], np.arange(1, shards)[None, :]

    def load(order):
        total = 0
        for partner in ((place + shift) % shards, place ^ shift):
            total += uses[order[place], order[partner]].sum(axis=0).max(axis=1).sum()
        return int(total)

    draw = np.random.RandomState(0)
    order = 5 * np.arange(shards) % shards
    least = load(order)
    for _ in range(24000 // shards):
        i, j = draw.randint(shards), draw.randint(shards)
        order[[i, j]] = order[[j, i]]
        now = load(order)
        if now <= least:
            least = now
        else:
            order[[i, j]] = order[[j, i]]
    return [int(shard) for shard in order]


def block_rows(kind, sequence, piece, batch, pieces, channels):
    first = ((kind * batch + sequence) * pieces + piece) * channels
    return slice(first, first + channels)


def gate_kernel(order, query_hbm, key_hbm, value_hbm, cotangent_hbm, sent_hbm, held, sent, sems, out_sems):
    shards, rows, lanes = sent.shape
    _, batch, tokens, all_channels = held.shape
    channels, pieces = all_channels // shards, tokens // lanes
    sources = (key_hbm, value_hbm, cotangent_hbm, query_hbm)

    def copy(b, i):
        return pltpu.make_async_copy(sources[i].at[b], held.at[i, b], sems.at[i, b])

    def send(kind, b):
        first = block_rows(kind, b, 0, batch, pieces, channels).start
        span = pl.ds(first, pieces * channels)
        return pltpu.make_async_copy(sent.at[:, span], sent_hbm.at[:, span], out_sems.at[kind, b])

    parts = [(kind, b) for kind in range(2) for b in range(batch)]
    for kind, b in parts:
        copy(b, 2 * kind).start()
        copy(b, 2 * kind + 1).start()
    for kind, b in parts:
        copy(b, 2 * kind).wait()
        copy(b, 2 * kind + 1).wait()
        columns = jnp.transpose(held[2 * kind, b] * held[2 * kind + 1, b])
        columns = columns.reshape(shards, channels, tokens)
        for piece in range(pieces):
            at = block_rows(kind, b, piece, batch, pieces, channels)
            for place, shard in enumerate(order):
                sent[place, at] = columns[shard, :, piece * lanes : (piece + 1) * lanes]
        send(kind, b).start()
    for kind, b in parts:
        send(kind, b).wait()


def transforms(twist_ref, matrix_ref, middle, turned):
    count, channels, width = turned.shape
    lanes = width // 2
    first, second = factors_of(count)
    in_chunk = max(1, ROW_CHUNK // channels // second)
    chunks = [range(p, min(p + in_chunk, first)) for p in range(0, first, in_chunk)]

    def store(row, value):
        re, im = value
        middle[row, :, :lanes] = jnp.zeros_like(im) if re is None else re
        middle[row, :, lanes:] = jnp.zeros_like(re) if im is None else im

    def fetch(row):
        return (middle[row, :, :lanes], middle[row, :, lanes:])

    def twist(k1, value):
        c, s = twist_ref[k1 : k1 + 1, :lanes], twist_ref[k1 : k1 + 1, lanes:]
        return (value[0] * c - value[1] * s, value[0] * s + value[1] * c)

    def places(chunk):
        return slice(chunk[0] * second, (chunk[-1] + 1) * second)

    def forward(load, spec):
        for b in range(second):
            values = small_dft([load(second * a + b) for a in range(first)])
            for p, value in enumerate(values):
                store(b * first + p, turn(value, b * p, count))
        for chunk in chunks:
            for p in chunk:
                values = small_dft([fetch(b * first + p) for b in range(second)])
                for q, value in enumerate(values):
                    place = p * second + q
                    turned[place, :, :lanes], turned[place, :, lanes:] = twist(p + first * q, value)
            x = turned[places(chunk)].reshape(-1, width)
            spec[places(chunk)] = lane_dft(x, matrix_ref[...]).reshape(-1, channels, width)

    def inverse(left, right, conjugate_left, emit):
        def along_lanes(chunk):
            part = places(chunk)
            lr, li = left[part, :, :lanes], left[part, :, lanes:]
            rr, ri = right[part, :, :lanes], right[part, :, lanes:]
            if conjugate_left:
                re, im = lr * rr + li * ri, li * rr - lr * ri
            else:
                re, im = lr * rr - li * ri, -(lr * ri + li * rr)
            x = jnp.concatenate([re.reshape(-1, lanes), im.reshape(-1, lanes)], axis=1)
            turned[part] = lane_dft(x, matrix_ref[...]).reshape(-1, channels, width)

        def along_rows(chunk):
            for p in chunk:
                values = []
                for q in range(second):
                    place = p * second + q
                    value = (turned[place, :, :lanes], turned[place, :, lanes:])
                    values.append(twist(p + first * q, value))
                for r, value in enumerate(small_dft(values)):
                    store(p * second + r, turn(value, p * r, count))

        along_lanes(chunks[0])
        for before, chunk in zip(chunks, chunks[1:]):
            along_lanes(chunk)
            along_rows(before)
        along_rows(chunks[-1])
        for r in range(second):
            values = small_dft([fetch(p * second + r) for p in range(first)])
            for t, value in enumerate(values):
                n1 = r + second * t
                if n1 < count // 2:
                    emit(n1, value)

    return forward, inverse


def token_blocks(ref, order, kind, pair, batch, channels, live):
    pieces = ref.shape[1] // (2 * batch * channels)

    def where(n1, sequence):
        at = block_rows(kind, 2 * pair + sequence, n1 % pieces, batch, pieces, channels)
        return order.index(n1 // pieces), at

    def load(n1):
        if n1 >= live:
            return None
        return (ref[where(n1, 0)], ref[where(n1, 1)])

    def emit(n1, value):
        ref[where(n1, 0)] = value[0]
        ref[where(n1, 1)] = -value[1]

    return load, emit


def filter_kernel(filter_ref, twist_ref, matrix_ref, spec_ref, middle, turned):
    length = filter_ref.shape[1]
    lanes = twist_ref.shape[1] // 2
    forward, _ = transforms(twist_ref, matrix_ref, middle, turned)

    def load(n1):
        if n1 * lanes >= length:
            return None
        return (filter_ref[:, n1 * lanes : (n1 + 1) * lanes] * (0.5 / length), None)

    forward(load, spec_ref)


def convolve_kernel(
    order, held_ref, filter_ref, twist_ref, matrix_ref, back_hbm, mixed_ref, upstream_ref,
    back, middles, turneds, out_sems,
):
    pairs, count, channels, _ = mixed_ref.shape
    half = back.shape[1] // 2
    kinds = (mixed_ref, upstream_ref)
    scratch = [
        transforms(twist_ref, matrix_ref, middles.at[kind], turneds.at[kind]) for kind in range(2)
    ]

    def send(kind):
        span = pl.ds(kind * half, half)
        return pltpu.make_async_copy(back.at[:, span], back_hbm.at[:, span], out_sems.at[kind])

    for pair in range(pairs):
        for kind in range(2):
            load, _ = token_blocks(held_ref, order, kind, pair, 2 * pairs, channels, count // 2)
            scratch[kind][0](load, kinds[kind].at[pair])
        for kind in range(2):
            _, emit = token_blocks(back, order, kind, pair, 2 * pairs, channels, count // 2)
            scratch[kind][1](filter_ref, kinds[kind].at[pair], kind == 1, emit)
            if pair == pairs - 1:
                send(kind).start()
    for kind in range(2):
        send(kind).wait()


def lag_kernel(scaling, mixed_ref, upstream_ref, twist_ref, matrix_ref, lag_ref, middle, turned):
    lanes = twist_ref.shape[1] // 2
    groups, _, share = lag_ref.shape
    group = lax.axis_index("batch")
    _, inverse = transforms(twist_ref, matrix_ref, middle, turned)
    for pair in range(mixed_ref.shape[0]):

        def emit(n1, value):
            at = n1 * lanes
            slot = lax.rem(at // share - group + groups, groups)
            span = slice(at % share, at % share + lanes)
            if pair == 0:
                lag_ref[slot, :, span] = value[0] * scaling
            else:
                lag_ref[slot, :, span] += value[0] * scaling

        inverse(mixed_ref.at[pair], upstream_ref.at[pair], True, emit)


def output_kernel(
    order, query_ref, key_ref, value_ref, cotangent_ref, skip_ref, home_ref, *refs
):
    *results, ready, out_sems = refs
    shards, _, lanes = home_ref.shape
    batch, tokens, all_channels = query_ref.shape
    channels, pieces = all_channels // shards, tokens // lanes
    skip = skip_ref[...]

    def columns(kind, b):
        turned = []
        for piece in range(pieces):
            at = block_rows(kind, b, piece, batch, pieces, channels)
            blocks = [home_ref[order.index(shard), at] for shard in range(shards)]
            turned.append(jnp.transpose(jnp.concatenate(blocks, axis=0)))
        return jnp.concatenate(turned, axis=0)

    def finish(i, b):
        return pltpu.make_async_copy(ready.at[i, b], results[i].at[b], out_sems.at[i, b])

    for b in range(batch):
        query, key, value, cotangent = query_ref[b], key_ref[b], value_ref[b], cotangent_ref[b]
        hidden = columns(0, b) + skip * (key * value)
        ready[0, b] = query * hidden
        finish(0, b).start()
        ready[1, b] = cotangent * hidden
        finish(1, b).start()
        mixed_grad = columns(1, b) + skip * (cotangent * query)
        ready[2, b] = mixed_grad * value
        finish(2, b).start()
        ready[3, b] = mixed_grad * key
        finish(3, b).start()
    for b in range(batch):
        for i in range(4):
            finish(i, b).wait()


def per_device(query_gate, key_gate, value_input, filters, skip_gain, cotangent, *, shards, groups):
    batch, tokens, all_channels = query_gate.shape
    channels, length = filters.shape
    lanes = 128 if 2 * length // 128 <= 64 else tokens
    count = 2 * length // lanes
    twist, matrix = tables(count, lanes)
    order = exchange_order(shards)
    lane_work = 2 * 3 * count * channels * (2 * lanes) ** 2

    def of(*shape):
        return jax.ShapeDtypeStruct(shape, jnp.float32)

    def call(kernel, name, stages, out_shape, scratch, *arrays, **options):
        return pl.pallas_call(
            kernel,
            out_shape=out_shape,
            scratch_shapes=scratch,
            compiler_params=pltpu.CompilerParams(vmem_limit_bytes=VMEM_BYTES),
            cost_estimate=pl.CostEstimate(
                flops=stages * lane_work, bytes_accessed=stages * 4 * batch * channels * length,
                transcendentals=0,
            ),
            name=name,
            **options,
        )(*arrays)

    def exchange(blocks):
        return lax.all_to_all(
            blocks, "seq", split_axis=0, concat_axis=0, tiled=True, axis_index_groups=[order]
        )

    rows = 2 * batch * channels * tokens // lanes
    swap = of(shards, rows, lanes)
    anywhere = pl.BlockSpec(memory_space=pl.ANY)
    in_vmem = pl.BlockSpec(memory_space=pltpu.VMEM)
    spectrum = of(batch // 2, count, channels, 2 * lanes)
    work = [pltpu.VMEM((count, channels, 2 * lanes), jnp.float32)] * 2
    sent = call(
        functools.partial(gate_kernel, order),
        "gate", 1, swap,
        [
            pltpu.VMEM((4, batch, tokens, all_channels), jnp.float32),
            pltpu.VMEM((shards, rows, lanes), jnp.float32),
            pltpu.SemaphoreType.DMA((4, batch)),
            pltpu.SemaphoreType.DMA((2, batch)),
        ],
        *(
            pltpu.with_memory_space_constraint(x, pltpu.HBM)
            for x in (query_gate, key_gate, value_input, cotangent)
        ),
        in_specs=[pl.BlockSpec(memory_space=pltpu.HBM)] * 4,
        out_specs=anywhere,
    )
    held = exchange(sent)
    filter_spec = call(
        filter_kernel, "filter", 2, of(count, channels, 2 * lanes), work, filters, twist, matrix
    )
    back, mixed_spec, upstream_spec = call(
        functools.partial(convolve_kernel, order),
        "convolve", 8, (swap, spectrum, spectrum),
        [
            pltpu.VMEM((shards, rows, lanes), jnp.float32),
            pltpu.VMEM((2, count, channels, 2 * lanes), jnp.float32),
            pltpu.VMEM((2, count, channels, 2 * lanes), jnp.float32),
            pltpu.SemaphoreType.DMA((2,)),
        ],
        held, filter_spec, twist, matrix,
        out_specs=(anywhere, in_vmem, in_vmem),
    )
    home = exchange(back)
    lag = call(
        functools.partial(lag_kernel, 1.0 / (2.0 * length * math.sqrt(length))),
        "lags", 2, of(groups, channels, length // groups), work,
        mixed_spec, upstream_spec, twist, matrix,
    )
    filter_grad = lag[0]
    for step in range(1, groups):
        pairs = [(source, (source + step) % groups) for source in range(groups)]
        filter_grad = filter_grad + lax.ppermute(lag[step], "batch", pairs)
    output, query_grad, key_grad, value_grad = call(
        functools.partial(output_kernel, order),
        "outputs", 2, (of(*query_gate.shape),) * 4,
        [
            pltpu.VMEM((4, batch, tokens, all_channels), jnp.float32),
            pltpu.SemaphoreType.DMA((4, batch)),
        ],
        query_gate, key_gate, value_input, cotangent, skip_gain.reshape(1, all_channels),
        home,
        out_specs=(anywhere,) * 4,
    )
    return (output, query_grad, key_grad, value_grad, filter_grad)


def solution(mesh):
    in_specs = (
        P("batch", "seq", None),
        P("batch", "seq", None),
        P("batch", "seq", None),
        P("seq", None),
        P(),
        P("batch", "seq", None),
    )
    out_specs = (
        P("batch", "seq", None),
        P("batch", "seq", None),
        P("batch", "seq", None),
        P("batch", "seq", None),
        P("seq", "batch"),
    )
    shards, groups = mesh.shape["seq"], mesh.shape["batch"]

    def whole(*arrays):
        return per_device(*arrays, shards=shards, groups=groups)

    return jax.shard_map(whole, mesh=mesh, in_specs=in_specs, out_specs=out_specs, check_vma=False)
```

```python
import functools
import math

import jax
import jax.numpy as jnp
import ml_dtypes
import numpy as np
from jax import lax
from jax.experimental import pallas as pl
from jax.experimental.pallas import tpu as pltpu
from jax.sharding import PartitionSpec as P

VMEM_BYTES = 48 * 1024 * 1024
ROW_CHUNK = 128


def add(a, b):
    if a is None:
        return b
    if b is None:
        return a
    return a + b


def sub(a, b):
    if b is None:
        return a
    if a is None:
        return -b
    return a - b


def scale(a, factor):
    if a is None or factor == 1.0:
        return a
    if factor == -1.0:
        return -a
    return a * factor


def turn(x, step, period):
    if x is None:
        return None
    re, im = x
    step = step % period
    if (4 * step) % period == 0:
        quarter = 4 * step // period
        if quarter == 0:
            return (re, im)
        if quarter == 1:
            return (im, scale(re, -1.0))
        if quarter == 2:
            return (scale(re, -1.0), scale(im, -1.0))
        return (scale(im, -1.0), re)
    angle = -2.0 * math.pi * step / period
    c, s = math.cos(angle), math.sin(angle)
    if (8 * step) % period == 0:
        root = math.sqrt(0.5)
        total, difference = add(re, im), sub(re, im)
        if c * s > 0:
            return (scale(difference, math.copysign(root, c)), scale(total, math.copysign(root, c)))
        return (scale(total, math.copysign(root, c)), scale(sub(im, re), math.copysign(root, c)))
    return (sub(scale(re, c), scale(im, s)), add(scale(re, s), scale(im, c)))


def complex_add(x, y):
    if x is None:
        return y
    if y is None:
        return x
    return (add(x[0], y[0]), add(x[1], y[1]))


def complex_sub(x, y):
    if y is None:
        return x
    if x is None:
        return (scale(y[0], -1.0), scale(y[1], -1.0))
    return (sub(x[0], y[0]), sub(x[1], y[1]))


def small_dft(values):
    size = len(values)
    if size == 1:
        return list(values)
    even = small_dft(values[0::2])
    odd = small_dft(values[1::2])
    odd = [turn(value, step, size) for step, value in enumerate(odd)]
    return [complex_add(e, o) for e, o in zip(even, odd)] + [
        complex_sub(e, o) for e, o in zip(even, odd)
    ]


def factors_of(size):
    first = 1
    while first * first < size:
        first *= 2
    return (size // first, first)


def tables(count, lanes):
    k1 = np.arange(count)[:, None]
    n2 = np.arange(lanes)[None, :]
    phase = -2.0 * np.pi * ((k1 * n2) % (count * lanes)) / (count * lanes)
    twist = np.concatenate([np.cos(phase), np.sin(phase)], axis=1).astype(np.float32)
    j = np.arange(lanes)
    phase = -2.0 * np.pi * ((j[:, None] * j[None, :]) % lanes) / lanes
    c, s = np.cos(phase), np.sin(phase)
    matrix = np.block([[c, s], [-s, c]]).astype(np.float32)
    high = matrix.astype(ml_dtypes.bfloat16)
    low = (matrix - high.astype(np.float32)).astype(ml_dtypes.bfloat16)
    return twist, np.concatenate([high, high, low], axis=0)


def lane_dft(x, matrix):
    high = x.astype(jnp.bfloat16)
    low = (x - high.astype(jnp.float32)).astype(jnp.bfloat16)
    return jnp.dot(
        jnp.concatenate([high, low, high], axis=1), matrix, preferred_element_type=jnp.float32
    )


def exchange_order(shards):
    if shards < 8:
        return list(range(shards))
    steps = shards // 4
    uses = np.zeros((shards, shards, 2, steps, 2), np.int32)
    for a in range(shards):
        for b in range(shards):
            (za, ya), (zb, yb) = (a // 4, a // 2 % 2), (b // 4, b // 2 % 2)
            for z in range(min(za, zb), max(za, zb)):
                uses[a, b, ya, z, int(za > zb)] = 1
    uses = uses.reshape(shards, shards, -1)
    place, shift = np.arange(shards)[:, None], np.arange(1, shards)[None, :]

    def load(order):
        total = 0
        for partner in ((place + shift) % shards, place ^ shift):
            total += uses[order[place], order[partner]].sum(axis=0).max(axis=1).sum()
        return int(total)

    draw = np.random.RandomState(0)
    order = 5 * np.arange(shards) % shards
    least = load(order)
    for _ in range(24000 // shards):
        i, j = draw.randint(shards), draw.randint(shards)
        order[[i, j]] = order[[j, i]]
        now = load(order)
        if now <= least:
            least = now
        else:
            order[[i, j]] = order[[j, i]]
    return [int(shard) for shard in order]


def block_rows(kind, sequence, piece, batch, pieces, channels):
    first = ((kind * batch + sequence) * pieces + piece) * channels
    return slice(first, first + channels)


def gate_kernel(order, query_hbm, key_hbm, value_hbm, cotangent_hbm, sent_hbm, held, sent, sems, out_sems):
    shards, rows, lanes = sent.shape
    _, batch, tokens, all_channels = held.shape
    channels, pieces = all_channels // shards, tokens // lanes
    sources = (key_hbm, value_hbm, cotangent_hbm, query_hbm)

    def copy(b, i):
        return pltpu.make_async_copy(sources[i].at[b], held.at[i, b], sems.at[i, b])

    def send(kind, b):
        first = block_rows(kind, b, 0, batch, pieces, channels).start
        span = pl.ds(first, pieces * channels)
        return pltpu.make_async_copy(sent.at[:, span], sent_hbm.at[:, span], out_sems.at[kind, b])

    parts = [(kind, b) for kind in range(2) for b in range(batch)]
    for kind, b in parts:
        copy(b, 2 * kind).start()
        copy(b, 2 * kind + 1).start()
    for kind, b in parts:
        copy(b, 2 * kind).wait()
        copy(b, 2 * kind + 1).wait()
        columns = jnp.transpose(held[2 * kind, b] * held[2 * kind + 1, b])
        columns = columns.reshape(shards, channels, tokens)
        for piece in range(pieces):
            at = block_rows(kind, b, piece, batch, pieces, channels)
            for place, shard in enumerate(order):
                sent[place, at] = columns[shard, :, piece * lanes : (piece + 1) * lanes]
        send(kind, b).start()
    for kind, b in parts:
        send(kind, b).wait()


def transforms(twist_ref, matrix_ref, middle, turned):
    count, channels, width = turned.shape
    lanes = width // 2
    first, second = factors_of(count)
    in_chunk = max(1, ROW_CHUNK // channels // second)
    chunks = [range(p, min(p + in_chunk, first)) for p in range(0, first, in_chunk)]

    def store(row, value):
        re, im = value
        middle[row, :, :lanes] = jnp.zeros_like(im) if re is None else re
        middle[row, :, lanes:] = jnp.zeros_like(re) if im is None else im

    def fetch(row):
        return (middle[row, :, :lanes], middle[row, :, lanes:])

    def twist(k1, value):
        c, s = twist_ref[k1 : k1 + 1, :lanes], twist_ref[k1 : k1 + 1, lanes:]
        return (value[0] * c - value[1] * s, value[0] * s + value[1] * c)

    def places(chunk):
        return slice(chunk[0] * second, (chunk[-1] + 1) * second)

    def forward(load, spec):
        for b in range(second):
            values = small_dft([load(second * a + b) for a in range(first)])
            for p, value in enumerate(values):
                store(b * first + p, turn(value, b * p, count))
        for chunk in chunks:
            for p in chunk:
                values = small_dft([fetch(b * first + p) for b in range(second)])
                for q, value in enumerate(values):
                    place = p * second + q
                    turned[place, :, :lanes], turned[place, :, lanes:] = twist(p + first * q, value)
            x = turned[places(chunk)].reshape(-1, width)
            spec[places(chunk)] = lane_dft(x, matrix_ref[...]).reshape(-1, channels, width)

    def inverse(left, right, conjugate_left, emit):
        def along_lanes(chunk):
            part = places(chunk)
            lr, li = left[part, :, :lanes], left[part, :, lanes:]
            rr, ri = right[part, :, :lanes], right[part, :, lanes:]
            if conjugate_left:
                re, im = lr * rr + li * ri, li * rr - lr * ri
            else:
                re, im = lr * rr - li * ri, -(lr * ri + li * rr)
            x = jnp.concatenate([re.reshape(-1, lanes), im.reshape(-1, lanes)], axis=1)
            turned[part] = lane_dft(x, matrix_ref[...]).reshape(-1, channels, width)

        def along_rows(chunk):
            for p in chunk:
                values = []
                for q in range(second):
                    place = p * second + q
                    value = (turned[place, :, :lanes], turned[place, :, lanes:])
                    values.append(twist(p + first * q, value))
                for r, value in enumerate(small_dft(values)):
                    store(p * second + r, turn(value, p * r, count))

        along_lanes(chunks[0])
        for before, chunk in zip(chunks, chunks[1:]):
            along_lanes(chunk)
            along_rows(before)
        along_rows(chunks[-1])
        for r in range(second):
            values = small_dft([fetch(p * second + r) for p in range(first)])
            for t, value in enumerate(values):
                n1 = r + second * t
                if n1 < count // 2:
                    emit(n1, value)

    return forward, inverse


def token_blocks(ref, order, kind, pair, batch, channels, live):
    pieces = ref.shape[1] // (2 * batch * channels)

    def where(n1, sequence):
        at = block_rows(kind, 2 * pair + sequence, n1 % pieces, batch, pieces, channels)
        return order.index(n1 // pieces), at

    def load(n1):
        if n1 >= live:
            return None
        return (ref[where(n1, 0)], ref[where(n1, 1)])

    def emit(n1, value):
        ref[where(n1, 0)] = value[0]
        ref[where(n1, 1)] = -value[1]

    return load, emit


def filter_kernel(filter_ref, twist_ref, matrix_ref, spec_ref, middle, turned):
    length = filter_ref.shape[1]
    lanes = twist_ref.shape[1] // 2
    forward, _ = transforms(twist_ref, matrix_ref, middle, turned)

    def load(n1):
        if n1 * lanes >= length:
            return None
        return (filter_ref[:, n1 * lanes : (n1 + 1) * lanes] * (0.5 / length), None)

    forward(load, spec_ref)


def convolve_kernel(
    order, held_ref, filter_ref, twist_ref, matrix_ref, back_hbm, mixed_ref, upstream_ref,
    back, middles, turneds, out_sems,
):
    pairs, count, channels, _ = mixed_ref.shape
    half = back.shape[1] // 2
    kinds = (mixed_ref, upstream_ref)
    scratch = [
        transforms(twist_ref, matrix_ref, middles.at[kind], turneds.at[kind]) for kind in range(2)
    ]

    copies = out_sems.shape[1]
    share = back.shape[0] // copies

    def send(kind, i):
        blocks, span = pl.ds(i * share, share), pl.ds(kind * half, half)
        return pltpu.make_async_copy(
            back.at[blocks, span], back_hbm.at[blocks, span], out_sems.at[kind, i]
        )

    for pair in range(pairs):
        for kind in range(2):
            load, _ = token_blocks(held_ref, order, kind, pair, 2 * pairs, channels, count // 2)
            scratch[kind][0](load, kinds[kind].at[pair])
        for kind in range(2):
            _, emit = token_blocks(back, order, kind, pair, 2 * pairs, channels, count // 2)
            scratch[kind][1](filter_ref, kinds[kind].at[pair], kind == 1, emit)
            if pair == pairs - 1:
                for i in range(copies):
                    send(kind, i).start()
    for kind in range(2):
        for i in range(copies):
            send(kind, i).wait()


def lag_kernel(scaling, mixed_ref, upstream_ref, twist_ref, matrix_ref, lag_ref, middle, turned):
    lanes = twist_ref.shape[1] // 2
    groups, _, share = lag_ref.shape
    group = lax.axis_index("batch")
    _, inverse = transforms(twist_ref, matrix_ref, middle, turned)
    for pair in range(mixed_ref.shape[0]):

        def emit(n1, value):
            at = n1 * lanes
            slot = lax.rem(at // share - group + groups, groups)
            span = slice(at % share, at % share + lanes)
            if pair == 0:
                lag_ref[slot, :, span] = value[0] * scaling
            else:
                lag_ref[slot, :, span] += value[0] * scaling

        inverse(mixed_ref.at[pair], upstream_ref.at[pair], True, emit)


def output_kernel(
    order, query_ref, key_ref, value_ref, cotangent_ref, skip_ref, home_ref, *refs
):
    *results, ready, out_sems = refs
    shards, _, lanes = home_ref.shape
    batch, tokens, all_channels = query_ref.shape
    channels, pieces = all_channels // shards, tokens // lanes
    skip = skip_ref[...]

    def columns(kind, b):
        turned = []
        for piece in range(pieces):
            at = block_rows(kind, b, piece, batch, pieces, channels)
            blocks = [home_ref[order.index(shard), at] for shard in range(shards)]
            turned.append(jnp.transpose(jnp.concatenate(blocks, axis=0)))
        return jnp.concatenate(turned, axis=0)

    def finish(i, b):
        return pltpu.make_async_copy(ready.at[i, b], results[i].at[b], out_sems.at[i, b])

    for b in range(batch):
        query, key, value, cotangent = query_ref[b], key_ref[b], value_ref[b], cotangent_ref[b]
        hidden = columns(0, b) + skip * (key * value)
        ready[0, b] = query * hidden
        finish(0, b).start()
        ready[1, b] = cotangent * hidden
        finish(1, b).start()
        mixed_grad = columns(1, b) + skip * (cotangent * query)
        ready[2, b] = mixed_grad * value
        finish(2, b).start()
        ready[3, b] = mixed_grad * key
        finish(3, b).start()
    for b in range(batch):
        for i in range(4):
            finish(i, b).wait()


def per_device(query_gate, key_gate, value_input, filters, skip_gain, cotangent, *, shards, groups):
    batch, tokens, all_channels = query_gate.shape
    channels, length = filters.shape
    lanes = 128 if 2 * length // 128 <= 64 else tokens
    count = 2 * length // lanes
    twist, matrix = tables(count, lanes)
    order = exchange_order(shards)
    lane_work = 2 * 3 * count * channels * (2 * lanes) ** 2

    def of(*shape):
        return jax.ShapeDtypeStruct(shape, jnp.float32)

    def call(kernel, name, stages, out_shape, scratch, *arrays, **options):
        return pl.pallas_call(
            kernel,
            out_shape=out_shape,
            scratch_shapes=scratch,
            compiler_params=pltpu.CompilerParams(vmem_limit_bytes=VMEM_BYTES),
            cost_estimate=pl.CostEstimate(
                flops=stages * lane_work, bytes_accessed=stages * 4 * batch * channels * length,
                transcendentals=0,
            ),
            name=name,
            **options,
        )(*arrays)

    def exchange(blocks):
        return lax.all_to_all(
            blocks, "seq", split_axis=0, concat_axis=0, tiled=True, axis_index_groups=[order]
        )

    rows = 2 * batch * channels * tokens // lanes
    swap = of(shards, rows, lanes)
    anywhere = pl.BlockSpec(memory_space=pl.ANY)
    in_vmem = pl.BlockSpec(memory_space=pltpu.VMEM)
    spectrum = of(batch // 2, count, channels, 2 * lanes)
    work = [pltpu.VMEM((count, channels, 2 * lanes), jnp.float32)] * 2
    sent = call(
        functools.partial(gate_kernel, order),
        "gate", 1, swap,
        [
            pltpu.VMEM((4, batch, tokens, all_channels), jnp.float32),
            pltpu.VMEM((shards, rows, lanes), jnp.float32),
            pltpu.SemaphoreType.DMA((4, batch)),
            pltpu.SemaphoreType.DMA((2, batch)),
        ],
        *(
            pltpu.with_memory_space_constraint(x, pltpu.HBM)
            for x in (query_gate, key_gate, value_input, cotangent)
        ),
        in_specs=[pl.BlockSpec(memory_space=pltpu.HBM)] * 4,
        out_specs=anywhere,
    )
    held = exchange(sent)
    filter_spec = call(
        filter_kernel, "filter", 2, of(count, channels, 2 * lanes), work, filters, twist, matrix
    )
    back, mixed_spec, upstream_spec = call(
        functools.partial(convolve_kernel, order),
        "convolve", 8, (swap, spectrum, spectrum),
        [
            pltpu.VMEM((shards, rows, lanes), jnp.float32),
            pltpu.VMEM((2, count, channels, 2 * lanes), jnp.float32),
            pltpu.VMEM((2, count, channels, 2 * lanes), jnp.float32),
            pltpu.SemaphoreType.DMA((2, math.gcd(shards, 8))),
        ],
        held, filter_spec, twist, matrix,
        out_specs=(anywhere, in_vmem, in_vmem),
    )
    home = exchange(back)
    lag = call(
        functools.partial(lag_kernel, 1.0 / (2.0 * length * math.sqrt(length))),
        "lags", 2, of(groups, channels, length // groups), work,
        mixed_spec, upstream_spec, twist, matrix,
    )
    filter_grad = lag[0]
    for step in range(1, groups):
        pairs = [(source, (source + step) % groups) for source in range(groups)]
        filter_grad = filter_grad + lax.ppermute(lag[step], "batch", pairs)
    output, query_grad, key_grad, value_grad = call(
        functools.partial(output_kernel, order),
        "outputs", 2, (of(*query_gate.shape),) * 4,
        [
            pltpu.VMEM((4, batch, tokens, all_channels), jnp.float32),
            pltpu.SemaphoreType.DMA((4, batch)),
        ],
        query_gate, key_gate, value_input, cotangent, skip_gain.reshape(1, all_channels),
        home,
        out_specs=(anywhere,) * 4,
    )
    return (output, query_grad, key_grad, value_grad, filter_grad)


def solution(mesh):
    in_specs = (
        P("batch", "seq", None),
        P("batch", "seq", None),
        P("batch", "seq", None),
        P("seq", None),
        P(),
        P("batch", "seq", None),
    )
    out_specs = (
        P("batch", "seq", None),
        P("batch", "seq", None),
        P("batch", "seq", None),
        P("batch", "seq", None),
        P("seq", "batch"),
    )
    shards, groups = mesh.shape["seq"], mesh.shape["batch"]

    def whole(*arrays):
        return per_device(*arrays, shards=shards, groups=groups)

    return jax.shard_map(whole, mesh=mesh, in_specs=in_specs, out_specs=out_specs, check_vma=False)
```

```python
import functools
import itertools
import math

import jax
import jax.numpy as jnp
import ml_dtypes
import numpy as np
from jax import lax
from jax.experimental import pallas as pl
from jax.experimental.pallas import tpu as pltpu
from jax.sharding import PartitionSpec as P

VMEM_BYTES = 48 * 1024 * 1024
ROW_CHUNK = 128


def add(a, b):
    if a is None:
        return b
    if b is None:
        return a
    return a + b


def sub(a, b):
    if b is None:
        return a
    if a is None:
        return -b
    return a - b


def scale(a, factor):
    if a is None or factor == 1.0:
        return a
    if factor == -1.0:
        return -a
    return a * factor


def turn(x, step, period):
    if x is None:
        return None
    re, im = x
    step = step % period
    if (4 * step) % period == 0:
        quarter = 4 * step // period
        if quarter == 0:
            return (re, im)
        if quarter == 1:
            return (im, scale(re, -1.0))
        if quarter == 2:
            return (scale(re, -1.0), scale(im, -1.0))
        return (scale(im, -1.0), re)
    angle = -2.0 * math.pi * step / period
    c, s = math.cos(angle), math.sin(angle)
    if (8 * step) % period == 0:
        root = math.sqrt(0.5)
        total, difference = add(re, im), sub(re, im)
        if c * s > 0:
            return (scale(difference, math.copysign(root, c)), scale(total, math.copysign(root, c)))
        return (scale(total, math.copysign(root, c)), scale(sub(im, re), math.copysign(root, c)))
    return (sub(scale(re, c), scale(im, s)), add(scale(re, s), scale(im, c)))


def complex_add(x, y):
    if x is None:
        return y
    if y is None:
        return x
    return (add(x[0], y[0]), add(x[1], y[1]))


def complex_sub(x, y):
    if y is None:
        return x
    if x is None:
        return (scale(y[0], -1.0), scale(y[1], -1.0))
    return (sub(x[0], y[0]), sub(x[1], y[1]))


def small_dft(values):
    size = len(values)
    if size == 1:
        return list(values)
    even = small_dft(values[0::2])
    odd = small_dft(values[1::2])
    odd = [turn(value, step, size) for step, value in enumerate(odd)]
    return [complex_add(e, o) for e, o in zip(even, odd)] + [
        complex_sub(e, o) for e, o in zip(even, odd)
    ]


def factors_of(size):
    first = 1
    while first * first < size:
        first *= 2
    return (size // first, first)


def tables(count, lanes):
    k1 = np.arange(count)[:, None]
    n2 = np.arange(lanes)[None, :]
    phase = -2.0 * np.pi * ((k1 * n2) % (count * lanes)) / (count * lanes)
    twist = np.concatenate([np.cos(phase), np.sin(phase)], axis=1).astype(np.float32)
    j = np.arange(lanes)
    phase = -2.0 * np.pi * ((j[:, None] * j[None, :]) % lanes) / lanes
    c, s = np.cos(phase), np.sin(phase)
    matrix = np.block([[c, s], [-s, c]]).astype(np.float32)
    high = matrix.astype(ml_dtypes.bfloat16)
    low = (matrix - high.astype(np.float32)).astype(ml_dtypes.bfloat16)
    return twist, np.concatenate([high, high, low], axis=0)


def lane_dft(x, matrix):
    high = x.astype(jnp.bfloat16)
    low = (x - high.astype(jnp.float32)).astype(jnp.bfloat16)
    return jnp.dot(
        jnp.concatenate([high, low, high], axis=1), matrix, preferred_element_type=jnp.float32
    )


def exchange_order(shards):
    if shards < 8:
        return list(range(shards))
    steps = shards // 4
    uses = np.zeros((shards, shards, 2, steps, 2), np.int32)
    for a in range(shards):
        for b in range(shards):
            (za, ya), (zb, yb) = (a // 4, a // 2 % 2), (b // 4, b // 2 % 2)
            for z in range(min(za, zb), max(za, zb)):
                uses[a, b, ya, z, int(za > zb)] = 1
    uses = uses.reshape(shards, shards, -1)
    place, shift = np.arange(shards)[:, None], np.arange(1, shards)[None, :]

    def load(order):
        total = 0
        for partner in ((place + shift) % shards, place ^ shift):
            total += uses[order[place], order[partner]].sum(axis=0).max(axis=1).sum()
        return int(total)

    draw = np.random.RandomState(0)
    order = 5 * np.arange(shards) % shards
    least = load(order)
    for _ in range(24000 // shards):
        i, j = draw.randint(shards), draw.randint(shards)
        order[[i, j]] = order[[j, i]]
        now = load(order)
        if now <= least:
            least = now
        else:
            order[[i, j]] = order[[j, i]]
    return [int(shard) for shard in order]


def block_rows(kind, sequence, piece, batch, pieces, channels):
    first = ((kind * batch + sequence) * pieces + piece) * channels
    return slice(first, first + channels)


def gate_kernel(order, query_hbm, key_hbm, value_hbm, cotangent_hbm, sent_hbm, held, sent, sems, out_sems):
    shards, rows, lanes = sent.shape
    _, batch, tokens, all_channels = held.shape
    channels, pieces = all_channels // shards, tokens // lanes
    sources = (key_hbm, value_hbm, cotangent_hbm, query_hbm)

    def copy(b, i):
        return pltpu.make_async_copy(sources[i].at[b], held.at[i, b], sems.at[i, b])

    def send(kind, b):
        first = block_rows(kind, b, 0, batch, pieces, channels).start
        span = pl.ds(first, pieces * channels)
        return pltpu.make_async_copy(sent.at[:, span], sent_hbm.at[:, span], out_sems.at[kind, b])

    parts = [(kind, b) for kind in range(2) for b in range(batch)]
    for kind, b in parts:
        copy(b, 2 * kind).start()
        copy(b, 2 * kind + 1).start()
    for kind, b in parts:
        copy(b, 2 * kind).wait()
        copy(b, 2 * kind + 1).wait()
        columns = jnp.transpose(held[2 * kind, b] * held[2 * kind + 1, b])
        columns = columns.reshape(shards, channels, tokens)
        for piece in range(pieces):
            at = block_rows(kind, b, piece, batch, pieces, channels)
            for place, shard in enumerate(order):
                sent[place, at] = columns[shard, :, piece * lanes : (piece + 1) * lanes]
        send(kind, b).start()
    for kind, b in parts:
        send(kind, b).wait()


def transforms(twist_ref, matrix_ref, middle, turned):
    count, channels, width = turned.shape
    lanes = width // 2
    first, second = factors_of(count)
    in_chunk = max(1, ROW_CHUNK // channels // second)
    chunks = [range(p, min(p + in_chunk, first)) for p in range(0, first, in_chunk)]

    def store(row, value):
        re, im = value
        middle[row, :, :lanes] = jnp.zeros_like(im) if re is None else re
        middle[row, :, lanes:] = jnp.zeros_like(re) if im is None else im

    def fetch(row):
        return (middle[row, :, :lanes], middle[row, :, lanes:])

    def twist(k1, value):
        c, s = twist_ref[k1 : k1 + 1, :lanes], twist_ref[k1 : k1 + 1, lanes:]
        return (value[0] * c - value[1] * s, value[0] * s + value[1] * c)

    def places(chunk):
        return slice(chunk[0] * second, (chunk[-1] + 1) * second)

    def forward(load, spec):
        for b in range(second):
            values = small_dft([load(second * a + b) for a in range(first)])
            for p, value in enumerate(values):
                store(b * first + p, turn(value, b * p, count))
            yield
        for chunk in chunks:
            for p in chunk:
                values = small_dft([fetch(b * first + p) for b in range(second)])
                for q, value in enumerate(values):
                    place = p * second + q
                    turned[place, :, :lanes], turned[place, :, lanes:] = twist(p + first * q, value)
            x = turned[places(chunk)].reshape(-1, width)
            spec[places(chunk)] = lane_dft(x, matrix_ref[...]).reshape(-1, channels, width)
            yield

    def inverse(left, right, conjugate_left, emit):
        def along_lanes(chunk):
            part = places(chunk)
            lr, li = left[part, :, :lanes], left[part, :, lanes:]
            rr, ri = right[part, :, :lanes], right[part, :, lanes:]
            if conjugate_left:
                re, im = lr * rr + li * ri, li * rr - lr * ri
            else:
                re, im = lr * rr - li * ri, -(lr * ri + li * rr)
            x = jnp.concatenate([re.reshape(-1, lanes), im.reshape(-1, lanes)], axis=1)
            turned[part] = lane_dft(x, matrix_ref[...]).reshape(-1, channels, width)

        def along_rows(chunk):
            for p in chunk:
                values = []
                for q in range(second):
                    place = p * second + q
                    value = (turned[place, :, :lanes], turned[place, :, lanes:])
                    values.append(twist(p + first * q, value))
                for r, value in enumerate(small_dft(values)):
                    store(p * second + r, turn(value, p * r, count))

        along_lanes(chunks[0])
        yield
        for before, chunk in zip(chunks, chunks[1:]):
            along_lanes(chunk)
            yield
            along_rows(before)
            yield
        along_rows(chunks[-1])
        yield
        for r in range(second):
            values = small_dft([fetch(p * second + r) for p in range(first)])
            for t, value in enumerate(values):
                n1 = r + second * t
                if n1 < count // 2:
                    emit(n1, value)
            yield

    return forward, inverse


def in_turn(*streams):
    for _ in itertools.zip_longest(*streams):
        pass


def token_blocks(ref, order, kind, pair, batch, channels, live):
    pieces = ref.shape[1] // (2 * batch * channels)

    def where(n1, sequence):
        at = block_rows(kind, 2 * pair + sequence, n1 % pieces, batch, pieces, channels)
        return order.index(n1 // pieces), at

    def load(n1):
        if n1 >= live:
            return None
        return (ref[where(n1, 0)], ref[where(n1, 1)])

    def emit(n1, value):
        ref[where(n1, 0)] = value[0]
        ref[where(n1, 1)] = -value[1]

    return load, emit


def filter_kernel(filter_ref, twist_ref, matrix_ref, spec_ref, middle, turned):
    length = filter_ref.shape[1]
    lanes = twist_ref.shape[1] // 2
    forward, _ = transforms(twist_ref, matrix_ref, middle, turned)

    def load(n1):
        if n1 * lanes >= length:
            return None
        return (filter_ref[:, n1 * lanes : (n1 + 1) * lanes] * (0.5 / length), None)

    in_turn(forward(load, spec_ref))


def convolve_kernel(
    order, held_ref, filter_ref, twist_ref, matrix_ref, back_hbm, mixed_ref, upstream_ref,
    back, middles, turneds, out_sems,
):
    pairs, count, channels, _ = mixed_ref.shape
    half = back.shape[1] // 2
    kinds = (mixed_ref, upstream_ref)
    scratch = [
        transforms(twist_ref, matrix_ref, middles.at[kind], turneds.at[kind]) for kind in range(2)
    ]

    def send(kind):
        span = pl.ds(kind * half, half)
        return pltpu.make_async_copy(back.at[:, span], back_hbm.at[:, span], out_sems.at[kind])

    for pair in range(pairs):

        def forward(kind):
            load, _ = token_blocks(held_ref, order, kind, pair, 2 * pairs, channels, count // 2)
            return scratch[kind][0](load, kinds[kind].at[pair])

        def inverse(kind):
            _, emit = token_blocks(back, order, kind, pair, 2 * pairs, channels, count // 2)
            return scratch[kind][1](filter_ref, kinds[kind].at[pair], kind == 1, emit)

        in_turn(forward(0))
        in_turn(inverse(0), forward(1))
        if pair == pairs - 1:
            send(0).start()
        in_turn(inverse(1))
    send(1).start()
    for kind in range(2):
        send(kind).wait()


def lag_kernel(scaling, mixed_ref, upstream_ref, twist_ref, matrix_ref, lag_ref, middle, turned):
    lanes = twist_ref.shape[1] // 2
    groups, _, share = lag_ref.shape
    group = lax.axis_index("batch")
    _, inverse = transforms(twist_ref, matrix_ref, middle, turned)
    for pair in range(mixed_ref.shape[0]):

        def emit(n1, value):
            at = n1 * lanes
            slot = lax.rem(at // share - group + groups, groups)
            span = slice(at % share, at % share + lanes)
            if pair == 0:
                lag_ref[slot, :, span] = value[0] * scaling
            else:
                lag_ref[slot, :, span] += value[0] * scaling

        in_turn(inverse(mixed_ref.at[pair], upstream_ref.at[pair], True, emit))


def output_kernel(
    order, query_ref, key_ref, value_ref, cotangent_ref, skip_ref, home_ref, *refs
):
    *results, ready, out_sems = refs
    shards, _, lanes = home_ref.shape
    batch, tokens, all_channels = query_ref.shape
    channels, pieces = all_channels // shards, tokens // lanes
    skip = skip_ref[...]

    def columns(kind, b):
        turned = []
        for piece in range(pieces):
            at = block_rows(kind, b, piece, batch, pieces, channels)
            blocks = [home_ref[order.index(shard), at] for shard in range(shards)]
            turned.append(jnp.transpose(jnp.concatenate(blocks, axis=0)))
        return jnp.concatenate(turned, axis=0)

    def finish(i, b):
        return pltpu.make_async_copy(ready.at[i, b], results[i].at[b], out_sems.at[i, b])

    for b in range(batch):
        query, key, value, cotangent = query_ref[b], key_ref[b], value_ref[b], cotangent_ref[b]
        hidden = columns(0, b) + skip * (key * value)
        ready[0, b] = query * hidden
        finish(0, b).start()
        ready[1, b] = cotangent * hidden
        finish(1, b).start()
        mixed_grad = columns(1, b) + skip * (cotangent * query)
        ready[2, b] = mixed_grad * value
        finish(2, b).start()
        ready[3, b] = mixed_grad * key
        finish(3, b).start()
    for b in range(batch):
        for i in range(4):
            finish(i, b).wait()


def per_device(query_gate, key_gate, value_input, filters, skip_gain, cotangent, *, shards, groups):
    batch, tokens, all_channels = query_gate.shape
    channels, length = filters.shape
    lanes = 128 if 2 * length // 128 <= 64 else tokens
    count = 2 * length // lanes
    twist, matrix = tables(count, lanes)
    order = exchange_order(shards)
    lane_work = 2 * 3 * count * channels * (2 * lanes) ** 2

    def of(*shape):
        return jax.ShapeDtypeStruct(shape, jnp.float32)

    def call(kernel, name, stages, out_shape, scratch, *arrays, **options):
        return pl.pallas_call(
            kernel,
            out_shape=out_shape,
            scratch_shapes=scratch,
            compiler_params=pltpu.CompilerParams(vmem_limit_bytes=VMEM_BYTES),
            cost_estimate=pl.CostEstimate(
                flops=stages * lane_work, bytes_accessed=stages * 4 * batch * channels * length,
                transcendentals=0,
            ),
            name=name,
            **options,
        )(*arrays)

    def exchange(blocks):
        return lax.all_to_all(
            blocks, "seq", split_axis=0, concat_axis=0, tiled=True, axis_index_groups=[order]
        )

    rows = 2 * batch * channels * tokens // lanes
    swap = of(shards, rows, lanes)
    anywhere = pl.BlockSpec(memory_space=pl.ANY)
    in_vmem = pl.BlockSpec(memory_space=pltpu.VMEM)
    spectrum = of(batch // 2, count, channels, 2 * lanes)
    work = [pltpu.VMEM((count, channels, 2 * lanes), jnp.float32)] * 2
    sent = call(
        functools.partial(gate_kernel, order),
        "gate", 1, swap,
        [
            pltpu.VMEM((4, batch, tokens, all_channels), jnp.float32),
            pltpu.VMEM((shards, rows, lanes), jnp.float32),
            pltpu.SemaphoreType.DMA((4, batch)),
            pltpu.SemaphoreType.DMA((2, batch)),
        ],
        *(
            pltpu.with_memory_space_constraint(x, pltpu.HBM)
            for x in (query_gate, key_gate, value_input, cotangent)
        ),
        in_specs=[pl.BlockSpec(memory_space=pltpu.HBM)] * 4,
        out_specs=anywhere,
    )
    held = exchange(sent)
    filter_spec = call(
        filter_kernel, "filter", 2, of(count, channels, 2 * lanes), work, filters, twist, matrix
    )
    back, mixed_spec, upstream_spec = call(
        functools.partial(convolve_kernel, order),
        "convolve", 8, (swap, spectrum, spectrum),
        [
            pltpu.VMEM((shards, rows, lanes), jnp.float32),
            pltpu.VMEM((2, count, channels, 2 * lanes), jnp.float32),
            pltpu.VMEM((2, count, channels, 2 * lanes), jnp.float32),
            pltpu.SemaphoreType.DMA((2,)),
        ],
        held, filter_spec, twist, matrix,
        out_specs=(anywhere, in_vmem, in_vmem),
    )
    home = exchange(back)
    lag = call(
        functools.partial(lag_kernel, 1.0 / (2.0 * length * math.sqrt(length))),
        "lags", 2, of(groups, channels, length // groups), work,
        mixed_spec, upstream_spec, twist, matrix,
    )
    filter_grad = lag[0]
    for step in range(1, groups):
        pairs = [(source, (source + step) % groups) for source in range(groups)]
        filter_grad = filter_grad + lax.ppermute(lag[step], "batch", pairs)
    output, query_grad, key_grad, value_grad = call(
        functools.partial(output_kernel, order),
        "outputs", 2, (of(*query_gate.shape),) * 4,
        [
            pltpu.VMEM((4, batch, tokens, all_channels), jnp.float32),
            pltpu.SemaphoreType.DMA((4, batch)),
        ],
        query_gate, key_gate, value_input, cotangent, skip_gain.reshape(1, all_channels),
        home,
        out_specs=(anywhere,) * 4,
    )
    return (output, query_grad, key_grad, value_grad, filter_grad)


def solution(mesh):
    in_specs = (
        P("batch", "seq", None),
        P("batch", "seq", None),
        P("batch", "seq", None),
        P("seq", None),
        P(),
        P("batch", "seq", None),
    )
    out_specs = (
        P("batch", "seq", None),
        P("batch", "seq", None),
        P("batch", "seq", None),
        P("batch", "seq", None),
        P("seq", "batch"),
    )
    shards, groups = mesh.shape["seq"], mesh.shape["batch"]

    def whole(*arrays):
        return per_device(*arrays, shards=shards, groups=groups)

    return jax.shard_map(whole, mesh=mesh, in_specs=in_specs, out_specs=out_specs, check_vma=False)
```

```python
import functools
import math

import jax
import jax.numpy as jnp
import ml_dtypes
import numpy as np
from jax import lax
from jax.experimental import pallas as pl
from jax.experimental.pallas import tpu as pltpu
from jax.sharding import PartitionSpec as P

VMEM_BYTES = 48 * 1024 * 1024
ROW_CHUNK = 128


def add(a, b):
    if a is None:
        return b
    if b is None:
        return a
    return a + b


def sub(a, b):
    if b is None:
        return a
    if a is None:
        return -b
    return a - b


def scale(a, factor):
    if a is None or factor == 1.0:
        return a
    if factor == -1.0:
        return -a
    return a * factor


def turn(x, step, period):
    if x is None:
        return None
    re, im = x
    step = step % period
    if (4 * step) % period == 0:
        quarter = 4 * step // period
        if quarter == 0:
            return (re, im)
        if quarter == 1:
            return (im, scale(re, -1.0))
        if quarter == 2:
            return (scale(re, -1.0), scale(im, -1.0))
        return (scale(im, -1.0), re)
    angle = -2.0 * math.pi * step / period
    c, s = math.cos(angle), math.sin(angle)
    if (8 * step) % period == 0:
        root = math.sqrt(0.5)
        total, difference = add(re, im), sub(re, im)
        if c * s > 0:
            return (scale(difference, math.copysign(root, c)), scale(total, math.copysign(root, c)))
        return (scale(total, math.copysign(root, c)), scale(sub(im, re), math.copysign(root, c)))
    return (sub(scale(re, c), scale(im, s)), add(scale(re, s), scale(im, c)))


def complex_add(x, y):
    if x is None:
        return y
    if y is None:
        return x
    return (add(x[0], y[0]), add(x[1], y[1]))


def complex_sub(x, y):
    if y is None:
        return x
    if x is None:
        return (scale(y[0], -1.0), scale(y[1], -1.0))
    return (sub(x[0], y[0]), sub(x[1], y[1]))


def small_dft(values):
    size = len(values)
    if size == 1:
        return list(values)
    even = small_dft(values[0::2])
    odd = small_dft(values[1::2])
    odd = [turn(value, step, size) for step, value in enumerate(odd)]
    return [complex_add(e, o) for e, o in zip(even, odd)] + [
        complex_sub(e, o) for e, o in zip(even, odd)
    ]


def factors_of(size):
    first = 1
    while first * first < size:
        first *= 2
    return (size // first, first)


def tables(count, lanes):
    k1 = np.arange(count)[:, None]
    n2 = np.arange(lanes)[None, :]
    phase = -2.0 * np.pi * ((k1 * n2) % (count * lanes)) / (count * lanes)
    twist = np.concatenate([np.cos(phase), np.sin(phase)], axis=1).astype(np.float32)
    j = np.arange(lanes)
    phase = -2.0 * np.pi * ((j[:, None] * j[None, :]) % lanes) / lanes
    c, s = np.cos(phase), np.sin(phase)
    matrix = np.block([[c, s], [-s, c]]).astype(np.float32)
    high = matrix.astype(ml_dtypes.bfloat16)
    low = (matrix - high.astype(np.float32)).astype(ml_dtypes.bfloat16)
    return twist, np.concatenate([high, high, low], axis=0)


def lane_dft(x, matrix):
    high = x.astype(jnp.bfloat16)
    low = (x - high.astype(jnp.float32)).astype(jnp.bfloat16)
    return jnp.dot(
        jnp.concatenate([high, low, high], axis=1), matrix, preferred_element_type=jnp.float32
    )


def exchange_order(shards):
    if shards < 8:
        return list(range(shards))
    steps = shards // 4
    uses = np.zeros((shards, shards, 2, steps, 2), np.int32)
    for a in range(shards):
        for b in range(shards):
            (za, ya), (zb, yb) = (a // 4, a // 2 % 2), (b // 4, b // 2 % 2)
            for z in range(min(za, zb), max(za, zb)):
                uses[a, b, ya, z, int(za > zb)] = 1
    uses = uses.reshape(shards, shards, -1)
    place, shift = np.arange(shards)[:, None], np.arange(1, shards)[None, :]

    def load(order):
        total = 0
        for partner in ((place + shift) % shards, place ^ shift):
            total += uses[order[place], order[partner]].sum(axis=0).max(axis=1).sum()
        return int(total)

    draw = np.random.RandomState(0)
    order = 5 * np.arange(shards) % shards
    least = load(order)
    for _ in range(24000 // shards):
        i, j = draw.randint(shards), draw.randint(shards)
        order[[i, j]] = order[[j, i]]
        now = load(order)
        if now <= least:
            least = now
        else:
            order[[i, j]] = order[[j, i]]
    return [int(shard) for shard in order]


def block_rows(kind, sequence, piece, batch, pieces, channels):
    first = ((kind * pieces + piece) * batch + sequence) * channels
    return slice(first, first + channels)


def gate_kernel(order, query_hbm, key_hbm, value_hbm, cotangent_hbm, sent_hbm, held, sent, sems, out_sems):
    shards, rows, lanes = sent.shape
    _, batch, tokens, all_channels = held.shape
    channels, pieces = all_channels // shards, tokens // lanes
    sources = (key_hbm, value_hbm, cotangent_hbm, query_hbm)

    def copy(b, i):
        return pltpu.make_async_copy(sources[i].at[b], held.at[i, b], sems.at[i, b])

    def send(kind):
        span = pl.ds(kind * (rows // 2), rows // 2)
        return pltpu.make_async_copy(sent.at[:, span], sent_hbm.at[:, span], out_sems.at[kind])

    parts = [(kind, b) for kind in range(2) for b in range(batch)]
    for kind, b in parts:
        copy(b, 2 * kind).start()
        copy(b, 2 * kind + 1).start()
    for kind, b in parts:
        copy(b, 2 * kind).wait()
        copy(b, 2 * kind + 1).wait()
        columns = jnp.transpose(held[2 * kind, b] * held[2 * kind + 1, b])
        columns = columns.reshape(shards, channels, tokens)
        for piece in range(pieces):
            at = block_rows(kind, b, piece, batch, pieces, channels)
            for place, shard in enumerate(order):
                sent[place, at] = columns[shard, :, piece * lanes : (piece + 1) * lanes]
        if b == batch - 1:
            send(kind).start()
    for kind in range(2):
        send(kind).wait()


def transforms(twist_ref, matrix_ref, middle, turned):
    count, channels, width = turned.shape
    lanes = width // 2
    first, second = factors_of(count)
    in_chunk = max(1, ROW_CHUNK // channels // second)
    chunks = [range(p, min(p + in_chunk, first)) for p in range(0, first, in_chunk)]

    def store(row, value):
        re, im = value
        middle[row, :, :lanes] = jnp.zeros_like(im) if re is None else re
        middle[row, :, lanes:] = jnp.zeros_like(re) if im is None else im

    def fetch(row):
        return (middle[row, :, :lanes], middle[row, :, lanes:])

    def twist(k1, value):
        c, s = twist_ref[k1 : k1 + 1, :lanes], twist_ref[k1 : k1 + 1, lanes:]
        return (value[0] * c - value[1] * s, value[0] * s + value[1] * c)

    def places(chunk):
        return slice(chunk[0] * second, (chunk[-1] + 1) * second)

    def forward(load, spec):
        for b in range(second):
            values = small_dft([load(second * a + b) for a in range(first)])
            for p, value in enumerate(values):
                store(b * first + p, turn(value, b * p, count))
        for chunk in chunks:
            for p in chunk:
                values = small_dft([fetch(b * first + p) for b in range(second)])
                for q, value in enumerate(values):
                    place = p * second + q
                    turned[place, :, :lanes], turned[place, :, lanes:] = twist(p + first * q, value)
            x = turned[places(chunk)].reshape(-1, width)
            spec[places(chunk)] = lane_dft(x, matrix_ref[...]).reshape(-1, channels, width)

    def inverse(left, right, conjugate_left, emit, pieces=1):
        def along_lanes(chunk):
            part = places(chunk)
            lr, li = left[part, :, :lanes], left[part, :, lanes:]
            rr, ri = right[part, :, :lanes], right[part, :, lanes:]
            if conjugate_left:
                re, im = lr * rr + li * ri, li * rr - lr * ri
            else:
                re, im = lr * rr - li * ri, -(lr * ri + li * rr)
            x = jnp.concatenate([re.reshape(-1, lanes), im.reshape(-1, lanes)], axis=1)
            turned[part] = lane_dft(x, matrix_ref[...]).reshape(-1, channels, width)

        def along_rows(chunk):
            for p in chunk:
                values = []
                for q in range(second):
                    place = p * second + q
                    value = (turned[place, :, :lanes], turned[place, :, lanes:])
                    values.append(twist(p + first * q, value))
                for r, value in enumerate(small_dft(values)):
                    store(p * second + r, turn(value, p * r, count))

        along_lanes(chunks[0])
        for before, chunk in zip(chunks, chunks[1:]):
            along_lanes(chunk)
            along_rows(before)
        along_rows(chunks[-1])
        for r in sorted(range(second), key=lambda r: r % pieces):
            values = small_dft([fetch(p * second + r) for p in range(first)])
            for t, value in enumerate(values):
                n1 = r + second * t
                if n1 < count // 2:
                    emit(n1, value)

    return forward, inverse


def token_blocks(ref, order, kind, pair, batch, channels, live):
    pieces = ref.shape[1] // (2 * batch * channels)

    def where(n1, sequence):
        at = block_rows(kind, 2 * pair + sequence, n1 % pieces, batch, pieces, channels)
        return order.index(n1 // pieces), at

    def load(n1):
        if n1 >= live:
            return None
        return (ref[where(n1, 0)], ref[where(n1, 1)])

    def emit(n1, value):
        ref[where(n1, 0)] = value[0]
        ref[where(n1, 1)] = -value[1]

    return load, emit


def filter_kernel(filter_ref, twist_ref, matrix_ref, spec_ref, middle, turned):
    length = filter_ref.shape[1]
    lanes = twist_ref.shape[1] // 2
    forward, _ = transforms(twist_ref, matrix_ref, middle, turned)

    def load(n1):
        if n1 * lanes >= length:
            return None
        return (filter_ref[:, n1 * lanes : (n1 + 1) * lanes] * (0.5 / length), None)

    forward(load, spec_ref)


def convolve_kernel(
    order, held_ref, filter_ref, twist_ref, matrix_ref, back_hbm, mixed_ref, upstream_ref,
    back, middles, turneds, out_sems,
):
    pairs, count, channels, _ = mixed_ref.shape
    half = back.shape[1] // 2
    kinds = (mixed_ref, upstream_ref)
    scratch = [
        transforms(twist_ref, matrix_ref, middles.at[kind], turneds.at[kind]) for kind in range(2)
    ]

    pieces = count // 2 // len(order)
    share = half // pieces

    def send(kind, piece):
        span = pl.ds(kind * half + piece * share, share)
        return pltpu.make_async_copy(
            back.at[:, span], back_hbm.at[:, span], out_sems.at[kind, piece]
        )

    def sending(kind, emit):
        left = [len(order)] * pieces

        def emit_and_send(n1, value):
            emit(n1, value)
            left[n1 % pieces] -= 1
            if left[n1 % pieces] == 0:
                send(kind, n1 % pieces).start()

        return emit_and_send

    for pair in range(pairs):
        for kind in range(2):
            load, _ = token_blocks(held_ref, order, kind, pair, 2 * pairs, channels, count // 2)
            scratch[kind][0](load, kinds[kind].at[pair])
        for kind in range(2):
            _, emit = token_blocks(back, order, kind, pair, 2 * pairs, channels, count // 2)
            if pair == pairs - 1:
                emit = sending(kind, emit)
            scratch[kind][1](filter_ref, kinds[kind].at[pair], kind == 1, emit, pieces)
    for kind in range(2):
        for piece in range(pieces):
            send(kind, piece).wait()


def lag_kernel(scaling, mixed_ref, upstream_ref, twist_ref, matrix_ref, lag_ref, middle, turned):
    lanes = twist_ref.shape[1] // 2
    groups, _, share = lag_ref.shape
    group = lax.axis_index("batch")
    _, inverse = transforms(twist_ref, matrix_ref, middle, turned)
    for pair in range(mixed_ref.shape[0]):

        def emit(n1, value):
            at = n1 * lanes
            slot = lax.rem(at // share - group + groups, groups)
            span = slice(at % share, at % share + lanes)
            if pair == 0:
                lag_ref[slot, :, span] = value[0] * scaling
            else:
                lag_ref[slot, :, span] += value[0] * scaling

        inverse(mixed_ref.at[pair], upstream_ref.at[pair], True, emit)


def output_kernel(
    order, query_ref, key_ref, value_ref, cotangent_ref, skip_ref, home_ref, *refs
):
    *results, ready, out_sems = refs
    shards, _, lanes = home_ref.shape
    batch, tokens, all_channels = query_ref.shape
    channels, pieces = all_channels // shards, tokens // lanes
    skip = skip_ref[...]

    def columns(kind, b):
        turned = []
        for piece in range(pieces):
            at = block_rows(kind, b, piece, batch, pieces, channels)
            blocks = [home_ref[order.index(shard), at] for shard in range(shards)]
            turned.append(jnp.transpose(jnp.concatenate(blocks, axis=0)))
        return jnp.concatenate(turned, axis=0)

    def finish(i, b):
        return pltpu.make_async_copy(ready.at[i, b], results[i].at[b], out_sems.at[i, b])

    for b in range(batch):
        query, key, value, cotangent = query_ref[b], key_ref[b], value_ref[b], cotangent_ref[b]
        hidden = columns(0, b) + skip * (key * value)
        ready[0, b] = query * hidden
        finish(0, b).start()
        ready[1, b] = cotangent * hidden
        finish(1, b).start()
        mixed_grad = columns(1, b) + skip * (cotangent * query)
        ready[2, b] = mixed_grad * value
        finish(2, b).start()
        ready[3, b] = mixed_grad * key
        finish(3, b).start()
    for b in range(batch):
        for i in range(4):
            finish(i, b).wait()


def per_device(query_gate, key_gate, value_input, filters, skip_gain, cotangent, *, shards, groups):
    batch, tokens, all_channels = query_gate.shape
    channels, length = filters.shape
    lanes = 128 if 2 * length // 128 <= 64 else tokens
    count = 2 * length // lanes
    twist, matrix = tables(count, lanes)
    order = exchange_order(shards)
    lane_work = 2 * 3 * count * channels * (2 * lanes) ** 2

    def of(*shape):
        return jax.ShapeDtypeStruct(shape, jnp.float32)

    def call(kernel, name, stages, out_shape, scratch, *arrays, **options):
        return pl.pallas_call(
            kernel,
            out_shape=out_shape,
            scratch_shapes=scratch,
            compiler_params=pltpu.CompilerParams(vmem_limit_bytes=VMEM_BYTES),
            cost_estimate=pl.CostEstimate(
                flops=stages * lane_work, bytes_accessed=stages * 4 * batch * channels * length,
                transcendentals=0,
            ),
            name=name,
            **options,
        )(*arrays)

    def exchange(blocks):
        return lax.all_to_all(
            blocks, "seq", split_axis=0, concat_axis=0, tiled=True, axis_index_groups=[order]
        )

    rows = 2 * batch * channels * tokens // lanes
    swap = of(shards, rows, lanes)
    anywhere = pl.BlockSpec(memory_space=pl.ANY)
    in_vmem = pl.BlockSpec(memory_space=pltpu.VMEM)
    spectrum = of(batch // 2, count, channels, 2 * lanes)
    work = [pltpu.VMEM((count, channels, 2 * lanes), jnp.float32)] * 2
    sent = call(
        functools.partial(gate_kernel, order),
        "gate", 1, swap,
        [
            pltpu.VMEM((4, batch, tokens, all_channels), jnp.float32),
            pltpu.VMEM((shards, rows, lanes), jnp.float32),
            pltpu.SemaphoreType.DMA((4, batch)),
            pltpu.SemaphoreType.DMA((2,)),
        ],
        *(
            pltpu.with_memory_space_constraint(x, pltpu.HBM)
            for x in (query_gate, key_gate, value_input, cotangent)
        ),
        in_specs=[pl.BlockSpec(memory_space=pltpu.HBM)] * 4,
        out_specs=anywhere,
    )
    held = exchange(sent)
    filter_spec = call(
        filter_kernel, "filter", 2, of(count, channels, 2 * lanes), work, filters, twist, matrix
    )
    back, mixed_spec, upstream_spec = call(
        functools.partial(convolve_kernel, order),
        "convolve", 8, (swap, spectrum, spectrum),
        [
            pltpu.VMEM((shards, rows, lanes), jnp.float32),
            pltpu.VMEM((2, count, channels, 2 * lanes), jnp.float32),
            pltpu.VMEM((2, count, channels, 2 * lanes), jnp.float32),
            pltpu.SemaphoreType.DMA((2, tokens // lanes)),
        ],
        held, filter_spec, twist, matrix,
        out_specs=(anywhere, in_vmem, in_vmem),
    )
    home = exchange(back)
    lag = call(
        functools.partial(lag_kernel, 1.0 / (2.0 * length * math.sqrt(length))),
        "lags", 2, of(groups, channels, length // groups), work,
        mixed_spec, upstream_spec, twist, matrix,
    )
    filter_grad = lag[0]
    for step in range(1, groups):
        pairs = [(source, (source + step) % groups) for source in range(groups)]
        filter_grad = filter_grad + lax.ppermute(lag[step], "batch", pairs)
    output, query_grad, key_grad, value_grad = call(
        functools.partial(output_kernel, order),
        "outputs", 2, (of(*query_gate.shape),) * 4,
        [
            pltpu.VMEM((4, batch, tokens, all_channels), jnp.float32),
            pltpu.SemaphoreType.DMA((4, batch)),
        ],
        query_gate, key_gate, value_input, cotangent, skip_gain.reshape(1, all_channels),
        home,
        out_specs=(anywhere,) * 4,
    )
    return (output, query_grad, key_grad, value_grad, filter_grad)


def solution(mesh):
    in_specs = (
        P("batch", "seq", None),
        P("batch", "seq", None),
        P("batch", "seq", None),
        P("seq", None),
        P(),
        P("batch", "seq", None),
    )
    out_specs = (
        P("batch", "seq", None),
        P("batch", "seq", None),
        P("batch", "seq", None),
        P("batch", "seq", None),
        P("seq", "batch"),
    )
    shards, groups = mesh.shape["seq"], mesh.shape["batch"]

    def whole(*arrays):
        return per_device(*arrays, shards=shards, groups=groups)

    return jax.shard_map(whole, mesh=mesh, in_specs=in_specs, out_specs=out_specs, check_vma=False)
```

```python
import functools
import math

import jax
import jax.numpy as jnp
import ml_dtypes
import numpy as np
from jax import lax
from jax.experimental import pallas as pl
from jax.experimental.pallas import tpu as pltpu
from jax.sharding import PartitionSpec as P

VMEM_BYTES = 48 * 1024 * 1024
ROW_CHUNK = 128


def add(a, b):
    if a is None:
        return b
    if b is None:
        return a
    return a + b


def sub(a, b):
    if b is None:
        return a
    if a is None:
        return -b
    return a - b


def scale(a, factor):
    if a is None or factor == 1.0:
        return a
    if factor == -1.0:
        return -a
    return a * factor


def turn(x, step, period):
    if x is None:
        return None
    re, im = x
    step = step % period
    if (4 * step) % period == 0:
        quarter = 4 * step // period
        if quarter == 0:
            return (re, im)
        if quarter == 1:
            return (im, scale(re, -1.0))
        if quarter == 2:
            return (scale(re, -1.0), scale(im, -1.0))
        return (scale(im, -1.0), re)
    angle = -2.0 * math.pi * step / period
    c, s = math.cos(angle), math.sin(angle)
    if (8 * step) % period == 0:
        root = math.sqrt(0.5)
        total, difference = add(re, im), sub(re, im)
        if c * s > 0:
            return (scale(difference, math.copysign(root, c)), scale(total, math.copysign(root, c)))
        return (scale(total, math.copysign(root, c)), scale(sub(im, re), math.copysign(root, c)))
    return (sub(scale(re, c), scale(im, s)), add(scale(re, s), scale(im, c)))


def complex_add(x, y):
    if x is None:
        return y
    if y is None:
        return x
    return (add(x[0], y[0]), add(x[1], y[1]))


def complex_sub(x, y):
    if y is None:
        return x
    if x is None:
        return (scale(y[0], -1.0), scale(y[1], -1.0))
    return (sub(x[0], y[0]), sub(x[1], y[1]))


def small_dft(values):
    size = len(values)
    if size == 1:
        return list(values)
    even = small_dft(values[0::2])
    odd = small_dft(values[1::2])
    odd = [turn(value, step, size) for step, value in enumerate(odd)]
    return [complex_add(e, o) for e, o in zip(even, odd)] + [
        complex_sub(e, o) for e, o in zip(even, odd)
    ]


def factors_of(size):
    first = 1
    while first * first < size:
        first *= 2
    return (size // first, first)


def tables(count, lanes):
    k1 = np.arange(count)[:, None]
    n2 = np.arange(lanes)[None, :]
    phase = -2.0 * np.pi * ((k1 * n2) % (count * lanes)) / (count * lanes)
    twist = np.concatenate([np.cos(phase), np.sin(phase)], axis=1).astype(np.float32)
    j = np.arange(lanes)
    phase = -2.0 * np.pi * ((j[:, None] * j[None, :]) % lanes) / lanes
    c, s = np.cos(phase), np.sin(phase)
    matrix = np.block([[c, s], [-s, c]]).astype(np.float32)
    high = matrix.astype(ml_dtypes.bfloat16)
    low = (matrix - high.astype(np.float32)).astype(ml_dtypes.bfloat16)
    return twist, np.concatenate([high, low], axis=0)


def lane_dft(x, matrix):
    high = x.astype(jnp.bfloat16)
    low = (x - high.astype(jnp.float32)).astype(jnp.bfloat16)
    width = x.shape[1]

    def times(part, rows):
        return jnp.dot(part, rows, preferred_element_type=jnp.float32)

    return times(high, matrix[:width]) + times(high, matrix[width:]) + times(low, matrix[:width])


def exchange_order(shards):
    if shards < 8:
        return list(range(shards))
    steps = shards // 4
    uses = np.zeros((shards, shards, 2, steps, 2), np.int32)
    for a in range(shards):
        for b in range(shards):
            (za, ya), (zb, yb) = (a // 4, a // 2 % 2), (b // 4, b // 2 % 2)
            for z in range(min(za, zb), max(za, zb)):
                uses[a, b, ya, z, int(za > zb)] = 1
    uses = uses.reshape(shards, shards, -1)
    place, shift = np.arange(shards)[:, None], np.arange(1, shards)[None, :]

    def load(order):
        total = 0
        for partner in ((place + shift) % shards, place ^ shift):
            total += uses[order[place], order[partner]].sum(axis=0).max(axis=1).sum()
        return int(total)

    draw = np.random.RandomState(0)
    order = 5 * np.arange(shards) % shards
    least = load(order)
    for _ in range(24000 // shards):
        i, j = draw.randint(shards), draw.randint(shards)
        order[[i, j]] = order[[j, i]]
        now = load(order)
        if now <= least:
            least = now
        else:
            order[[i, j]] = order[[j, i]]
    return [int(shard) for shard in order]


def block_rows(kind, sequence, piece, batch, pieces, channels):
    first = ((kind * batch + sequence) * pieces + piece) * channels
    return slice(first, first + channels)


def gate_kernel(order, query_hbm, key_hbm, value_hbm, cotangent_hbm, sent_hbm, held, sent, sems, out_sems):
    shards, rows, lanes = sent.shape
    _, batch, tokens, all_channels = held.shape
    channels, pieces = all_channels // shards, tokens // lanes
    sources = (key_hbm, value_hbm, cotangent_hbm, query_hbm)

    def copy(b, i):
        return pltpu.make_async_copy(sources[i].at[b], held.at[i, b], sems.at[i, b])

    def send(kind, b):
        first = block_rows(kind, b, 0, batch, pieces, channels).start
        span = pl.ds(first, pieces * channels)
        return pltpu.make_async_copy(sent.at[:, span], sent_hbm.at[:, span], out_sems.at[kind, b])

    parts = [(kind, b) for kind in range(2) for b in range(batch)]
    for kind, b in parts:
        copy(b, 2 * kind).start()
        copy(b, 2 * kind + 1).start()
    for kind, b in parts:
        copy(b, 2 * kind).wait()
        copy(b, 2 * kind + 1).wait()
        columns = jnp.transpose(held[2 * kind, b] * held[2 * kind + 1, b])
        columns = columns.reshape(shards, channels, tokens)
        for piece in range(pieces):
            at = block_rows(kind, b, piece, batch, pieces, channels)
            for place, shard in enumerate(order):
                sent[place, at] = columns[shard, :, piece * lanes : (piece + 1) * lanes]
        send(kind, b).start()
    for kind, b in parts:
        send(kind, b).wait()


def transforms(twist_ref, matrix_ref, middle, turned):
    count, channels, width = turned.shape
    lanes = width // 2
    first, second = factors_of(count)
    in_chunk = max(1, ROW_CHUNK // channels // second)
    chunks = [range(p, min(p + in_chunk, first)) for p in range(0, first, in_chunk)]

    def store(row, value):
        re, im = value
        middle[row, :, :lanes] = jnp.zeros_like(im) if re is None else re
        middle[row, :, lanes:] = jnp.zeros_like(re) if im is None else im

    def fetch(row):
        return (middle[row, :, :lanes], middle[row, :, lanes:])

    def twist(k1, value):
        c, s = twist_ref[k1 : k1 + 1, :lanes], twist_ref[k1 : k1 + 1, lanes:]
        return (value[0] * c - value[1] * s, value[0] * s + value[1] * c)

    def places(chunk):
        return slice(chunk[0] * second, (chunk[-1] + 1) * second)

    def forward(load, spec):
        for b in range(second):
            values = small_dft([load(second * a + b) for a in range(first)])
            for p, value in enumerate(values):
                store(b * first + p, turn(value, b * p, count))
        for chunk in chunks:
            for p in chunk:
                values = small_dft([fetch(b * first + p) for b in range(second)])
                for q, value in enumerate(values):
                    place = p * second + q
                    turned[place, :, :lanes], turned[place, :, lanes:] = twist(p + first * q, value)
            x = turned[places(chunk)].reshape(-1, width)
            spec[places(chunk)] = lane_dft(x, matrix_ref[...]).reshape(-1, channels, width)

    def inverse(left, right, conjugate_left, emit):
        def along_lanes(chunk):
            part = places(chunk)
            lr, li = left[part, :, :lanes], left[part, :, lanes:]
            rr, ri = right[part, :, :lanes], right[part, :, lanes:]
            if conjugate_left:
                re, im = lr * rr + li * ri, li * rr - lr * ri
            else:
                re, im = lr * rr - li * ri, -(lr * ri + li * rr)
            x = jnp.concatenate([re.reshape(-1, lanes), im.reshape(-1, lanes)], axis=1)
            turned[part] = lane_dft(x, matrix_ref[...]).reshape(-1, channels, width)

        def along_rows(chunk):
            for p in chunk:
                values = []
                for q in range(second):
                    place = p * second + q
                    value = (turned[place, :, :lanes], turned[place, :, lanes:])
                    values.append(twist(p + first * q, value))
                for r, value in enumerate(small_dft(values)):
                    store(p * second + r, turn(value, p * r, count))

        along_lanes(chunks[0])
        for before, chunk in zip(chunks, chunks[1:]):
            along_lanes(chunk)
            along_rows(before)
        along_rows(chunks[-1])
        for r in range(second):
            values = small_dft([fetch(p * second + r) for p in range(first)])
            for t, value in enumerate(values):
                n1 = r + second * t
                if n1 < count // 2:
                    emit(n1, value)

    return forward, inverse


def token_blocks(ref, order, kind, pair, batch, channels, live):
    pieces = ref.shape[1] // (2 * batch * channels)

    def where(n1, sequence):
        at = block_rows(kind, 2 * pair + sequence, n1 % pieces, batch, pieces, channels)
        return order.index(n1 // pieces), at

    def load(n1):
        if n1 >= live:
            return None
        return (ref[where(n1, 0)], ref[where(n1, 1)])

    def emit(n1, value):
        ref[where(n1, 0)] = value[0]
        ref[where(n1, 1)] = -value[1]

    return load, emit


def filter_kernel(filter_ref, twist_ref, matrix_ref, spec_ref, middle, turned):
    length = filter_ref.shape[1]
    lanes = twist_ref.shape[1] // 2
    forward, _ = transforms(twist_ref, matrix_ref, middle, turned)

    def load(n1):
        if n1 * lanes >= length:
            return None
        return (filter_ref[:, n1 * lanes : (n1 + 1) * lanes] * (0.5 / length), None)

    forward(load, spec_ref)


def convolve_kernel(
    order, held_ref, filter_ref, twist_ref, matrix_ref, back_hbm, mixed_ref, upstream_ref,
    back, middles, turneds, out_sems,
):
    pairs, count, channels, _ = mixed_ref.shape
    half = back.shape[1] // 2
    kinds = (mixed_ref, upstream_ref)
    scratch = [
        transforms(twist_ref, matrix_ref, middles.at[kind], turneds.at[kind]) for kind in range(2)
    ]

    def send(kind):
        span = pl.ds(kind * half, half)
        return pltpu.make_async_copy(back.at[:, span], back_hbm.at[:, span], out_sems.at[kind])

    for pair in range(pairs):
        for kind in range(2):
            load, _ = token_blocks(held_ref, order, kind, pair, 2 * pairs, channels, count // 2)
            scratch[kind][0](load, kinds[kind].at[pair])
        for kind in range(2):
            _, emit = token_blocks(back, order, kind, pair, 2 * pairs, channels, count // 2)
            scratch[kind][1](filter_ref, kinds[kind].at[pair], kind == 1, emit)
            if pair == pairs - 1:
                send(kind).start()
    for kind in range(2):
        send(kind).wait()


def lag_kernel(scaling, mixed_ref, upstream_ref, twist_ref, matrix_ref, lag_ref, middle, turned):
    lanes = twist_ref.shape[1] // 2
    groups, _, share = lag_ref.shape
    group = lax.axis_index("batch")
    _, inverse = transforms(twist_ref, matrix_ref, middle, turned)
    for pair in range(mixed_ref.shape[0]):

        def emit(n1, value):
            at = n1 * lanes
            slot = lax.rem(at // share - group + groups, groups)
            span = slice(at % share, at % share + lanes)
            if pair == 0:
                lag_ref[slot, :, span] = value[0] * scaling
            else:
                lag_ref[slot, :, span] += value[0] * scaling

        inverse(mixed_ref.at[pair], upstream_ref.at[pair], True, emit)


def output_kernel(
    order, query_ref, key_ref, value_ref, cotangent_ref, skip_ref, home_ref, *refs
):
    *results, ready, out_sems = refs
    shards, _, lanes = home_ref.shape
    batch, tokens, all_channels = query_ref.shape
    channels, pieces = all_channels // shards, tokens // lanes
    skip = skip_ref[...]

    def columns(kind, b):
        turned = []
        for piece in range(pieces):
            at = block_rows(kind, b, piece, batch, pieces, channels)
            blocks = [home_ref[order.index(shard), at] for shard in range(shards)]
            turned.append(jnp.transpose(jnp.concatenate(blocks, axis=0)))
        return jnp.concatenate(turned, axis=0)

    def finish(i, b):
        return pltpu.make_async_copy(ready.at[i, b], results[i].at[b], out_sems.at[i, b])

    for b in range(batch):
        query, key, value, cotangent = query_ref[b], key_ref[b], value_ref[b], cotangent_ref[b]
        hidden = columns(0, b) + skip * (key * value)
        ready[0, b] = query * hidden
        finish(0, b).start()
        ready[1, b] = cotangent * hidden
        finish(1, b).start()
        mixed_grad = columns(1, b) + skip * (cotangent * query)
        ready[2, b] = mixed_grad * value
        finish(2, b).start()
        ready[3, b] = mixed_grad * key
        finish(3, b).start()
    for b in range(batch):
        for i in range(4):
            finish(i, b).wait()


def per_device(query_gate, key_gate, value_input, filters, skip_gain, cotangent, *, shards, groups):
    batch, tokens, all_channels = query_gate.shape
    channels, length = filters.shape
    lanes = 128 if 2 * length // 128 <= 64 else tokens
    count = 2 * length // lanes
    twist, matrix = tables(count, lanes)
    order = exchange_order(shards)
    lane_work = 2 * 3 * count * channels * (2 * lanes) ** 2

    def of(*shape):
        return jax.ShapeDtypeStruct(shape, jnp.float32)

    def call(kernel, name, stages, out_shape, scratch, *arrays, **options):
        return pl.pallas_call(
            kernel,
            out_shape=out_shape,
            scratch_shapes=scratch,
            compiler_params=pltpu.CompilerParams(vmem_limit_bytes=VMEM_BYTES),
            cost_estimate=pl.CostEstimate(
                flops=stages * lane_work, bytes_accessed=stages * 4 * batch * channels * length,
                transcendentals=0,
            ),
            name=name,
            **options,
        )(*arrays)

    def exchange(blocks):
        return lax.all_to_all(
            blocks, "seq", split_axis=0, concat_axis=0, tiled=True, axis_index_groups=[order]
        )

    rows = 2 * batch * channels * tokens // lanes
    swap = of(shards, rows, lanes)
    anywhere = pl.BlockSpec(memory_space=pl.ANY)
    in_vmem = pl.BlockSpec(memory_space=pltpu.VMEM)
    spectrum = of(batch // 2, count, channels, 2 * lanes)
    work = [pltpu.VMEM((count, channels, 2 * lanes), jnp.float32)] * 2
    sent = call(
        functools.partial(gate_kernel, order),
        "gate", 1, swap,
        [
            pltpu.VMEM((4, batch, tokens, all_channels), jnp.float32),
            pltpu.VMEM((shards, rows, lanes), jnp.float32),
            pltpu.SemaphoreType.DMA((4, batch)),
            pltpu.SemaphoreType.DMA((2, batch)),
        ],
        *(
            pltpu.with_memory_space_constraint(x, pltpu.HBM)
            for x in (query_gate, key_gate, value_input, cotangent)
        ),
        in_specs=[pl.BlockSpec(memory_space=pltpu.HBM)] * 4,
        out_specs=anywhere,
    )
    held = exchange(sent)
    filter_spec = call(
        filter_kernel, "filter", 2, of(count, channels, 2 * lanes), work, filters, twist, matrix
    )
    back, mixed_spec, upstream_spec = call(
        functools.partial(convolve_kernel, order),
        "convolve", 8, (swap, spectrum, spectrum),
        [
            pltpu.VMEM((shards, rows, lanes), jnp.float32),
            pltpu.VMEM((2, count, channels, 2 * lanes), jnp.float32),
            pltpu.VMEM((2, count, channels, 2 * lanes), jnp.float32),
            pltpu.SemaphoreType.DMA((2,)),
        ],
        held, filter_spec, twist, matrix,
        out_specs=(anywhere, in_vmem, in_vmem),
    )
    home = exchange(back)
    lag = call(
        functools.partial(lag_kernel, 1.0 / (2.0 * length * math.sqrt(length))),
        "lags", 2, of(groups, channels, length // groups), work,
        mixed_spec, upstream_spec, twist, matrix,
    )
    filter_grad = lag[0]
    for step in range(1, groups):
        pairs = [(source, (source + step) % groups) for source in range(groups)]
        filter_grad = filter_grad + lax.ppermute(lag[step], "batch", pairs)
    output, query_grad, key_grad, value_grad = call(
        functools.partial(output_kernel, order),
        "outputs", 2, (of(*query_gate.shape),) * 4,
        [
            pltpu.VMEM((4, batch, tokens, all_channels), jnp.float32),
            pltpu.SemaphoreType.DMA((4, batch)),
        ],
        query_gate, key_gate, value_input, cotangent, skip_gain.reshape(1, all_channels),
        home,
        out_specs=(anywhere,) * 4,
    )
    return (output, query_grad, key_grad, value_grad, filter_grad)


def solution(mesh):
    in_specs = (
        P("batch", "seq", None),
        P("batch", "seq", None),
        P("batch", "seq", None),
        P("seq", None),
        P(),
        P("batch", "seq", None),
    )
    out_specs = (
        P("batch", "seq", None),
        P("batch", "seq", None),
        P("batch", "seq", None),
        P("batch", "seq", None),
        P("seq", "batch"),
    )
    shards, groups = mesh.shape["seq"], mesh.shape["batch"]

    def whole(*arrays):
        return per_device(*arrays, shards=shards, groups=groups)

    return jax.shard_map(whole, mesh=mesh, in_specs=in_specs, out_specs=out_specs, check_vma=False)
```

```python
import functools
import math

import jax
import jax.numpy as jnp
import ml_dtypes
import numpy as np
from jax import lax
from jax.experimental import pallas as pl
from jax.experimental.pallas import tpu as pltpu
from jax.sharding import PartitionSpec as P

VMEM_BYTES = 48 * 1024 * 1024
ROW_CHUNK = 64


def add(a, b):
    if a is None:
        return b
    if b is None:
        return a
    return a + b


def sub(a, b):
    if b is None:
        return a
    if a is None:
        return -b
    return a - b


def scale(a, factor):
    if a is None or factor == 1.0:
        return a
    if factor == -1.0:
        return -a
    return a * factor


def turn(x, step, period):
    if x is None:
        return None
    re, im = x
    step = step % period
    if (4 * step) % period == 0:
        quarter = 4 * step // period
        if quarter == 0:
            return (re, im)
        if quarter == 1:
            return (im, scale(re, -1.0))
        if quarter == 2:
            return (scale(re, -1.0), scale(im, -1.0))
        return (scale(im, -1.0), re)
    angle = -2.0 * math.pi * step / period
    c, s = math.cos(angle), math.sin(angle)
    if (8 * step) % period == 0:
        root = math.sqrt(0.5)
        total, difference = add(re, im), sub(re, im)
        if c * s > 0:
            return (scale(difference, math.copysign(root, c)), scale(total, math.copysign(root, c)))
        return (scale(total, math.copysign(root, c)), scale(sub(im, re), math.copysign(root, c)))
    return (sub(scale(re, c), scale(im, s)), add(scale(re, s), scale(im, c)))


def complex_add(x, y):
    if x is None:
        return y
    if y is None:
        return x
    return (add(x[0], y[0]), add(x[1], y[1]))


def complex_sub(x, y):
    if y is None:
        return x
    if x is None:
        return (scale(y[0], -1.0), scale(y[1], -1.0))
    return (sub(x[0], y[0]), sub(x[1], y[1]))


def small_dft(values):
    size = len(values)
    if size == 1:
        return list(values)
    even = small_dft(values[0::2])
    odd = small_dft(values[1::2])
    odd = [turn(value, step, size) for step, value in enumerate(odd)]
    return [complex_add(e, o) for e, o in zip(even, odd)] + [
        complex_sub(e, o) for e, o in zip(even, odd)
    ]


def factors_of(size):
    first = 1
    while first * first < size:
        first *= 2
    return (size // first, first)


def tables(count, lanes):
    k1 = np.arange(count)[:, None]
    n2 = np.arange(lanes)[None, :]
    phase = -2.0 * np.pi * ((k1 * n2) % (count * lanes)) / (count * lanes)
    twist = np.concatenate([np.cos(phase), np.sin(phase)], axis=1).astype(np.float32)
    j = np.arange(lanes)
    phase = -2.0 * np.pi * ((j[:, None] * j[None, :]) % lanes) / lanes
    c, s = np.cos(phase), np.sin(phase)
    matrix = np.block([[c, s], [-s, c]]).astype(np.float32)
    high = matrix.astype(ml_dtypes.bfloat16)
    low = (matrix - high.astype(np.float32)).astype(ml_dtypes.bfloat16)
    return twist, np.concatenate([high, high, low], axis=0)


def lane_dft(x, matrix):
    high = x.astype(jnp.bfloat16)
    low = (x - high.astype(jnp.float32)).astype(jnp.bfloat16)
    return jnp.dot(
        jnp.concatenate([high, low, high], axis=1), matrix, preferred_element_type=jnp.float32
    )


def exchange_order(shards):
    if shards < 8:
        return list(range(shards))
    steps = shards // 4
    uses = np.zeros((shards, shards, 2, steps, 2), np.int32)
    for a in range(shards):
        for b in range(shards):
            (za, ya), (zb, yb) = (a // 4, a // 2 % 2), (b // 4, b // 2 % 2)
            for z in range(min(za, zb), max(za, zb)):
                uses[a, b, ya, z, int(za > zb)] = 1
    uses = uses.reshape(shards, shards, -1)
    place, shift = np.arange(shards)[:, None], np.arange(1, shards)[None, :]

    def load(order):
        total = 0
        for partner in ((place + shift) % shards, place ^ shift):
            total += uses[order[place], order[partner]].sum(axis=0).max(axis=1).sum()
        return int(total)

    draw = np.random.RandomState(0)
    order = 5 * np.arange(shards) % shards
    least = load(order)
    for _ in range(24000 // shards):
        i, j = draw.randint(shards), draw.randint(shards)
        order[[i, j]] = order[[j, i]]
        now = load(order)
        if now <= least:
            least = now
        else:
            order[[i, j]] = order[[j, i]]
    return [int(shard) for shard in order]


def block_rows(kind, sequence, piece, batch, pieces, channels):
    first = ((kind * batch + sequence) * pieces + piece) * channels
    return slice(first, first + channels)


def gate_kernel(order, query_hbm, key_hbm, value_hbm, cotangent_hbm, sent_hbm, held, sent, sems, out_sems):
    shards, rows, lanes = sent.shape
    _, batch, tokens, all_channels = held.shape
    channels, pieces = all_channels // shards, tokens // lanes
    sources = (key_hbm, value_hbm, cotangent_hbm, query_hbm)

    def copy(b, i):
        return pltpu.make_async_copy(sources[i].at[b], held.at[i, b], sems.at[i, b])

    def send(kind, b):
        first = block_rows(kind, b, 0, batch, pieces, channels).start
        span = pl.ds(first, pieces * channels)
        return pltpu.make_async_copy(sent.at[:, span], sent_hbm.at[:, span], out_sems.at[kind, b])

    parts = [(kind, b) for kind in range(2) for b in range(batch)]
    for kind, b in parts:
        copy(b, 2 * kind).start()
        copy(b, 2 * kind + 1).start()
    for kind, b in parts:
        copy(b, 2 * kind).wait()
        copy(b, 2 * kind + 1).wait()
        columns = jnp.transpose(held[2 * kind, b] * held[2 * kind + 1, b])
        columns = columns.reshape(shards, channels, tokens)
        for piece in range(pieces):
            at = block_rows(kind, b, piece, batch, pieces, channels)
            for place, shard in enumerate(order):
                sent[place, at] = columns[shard, :, piece * lanes : (piece + 1) * lanes]
        send(kind, b).start()
    for kind, b in parts:
        send(kind, b).wait()


def transforms(twist_ref, matrix_ref, middle, turned):
    count, channels, width = turned.shape
    lanes = width // 2
    first, second = factors_of(count)
    in_chunk = max(1, ROW_CHUNK // channels // second)
    chunks = [range(p, min(p + in_chunk, first)) for p in range(0, first, in_chunk)]

    def store(row, value):
        re, im = value
        middle[row, :, :lanes] = jnp.zeros_like(im) if re is None else re
        middle[row, :, lanes:] = jnp.zeros_like(re) if im is None else im

    def fetch(row):
        return (middle[row, :, :lanes], middle[row, :, lanes:])

    def twist(k1, value):
        c, s = twist_ref[k1 : k1 + 1, :lanes], twist_ref[k1 : k1 + 1, lanes:]
        return (value[0] * c - value[1] * s, value[0] * s + value[1] * c)

    def places(chunk):
        return slice(chunk[0] * second, (chunk[-1] + 1) * second)

    def forward(load, spec):
        for b in range(second):
            values = small_dft([load(second * a + b) for a in range(first)])
            for p, value in enumerate(values):
                store(b * first + p, turn(value, b * p, count))
        for chunk in chunks:
            for p in chunk:
                values = small_dft([fetch(b * first + p) for b in range(second)])
                for q, value in enumerate(values):
                    place = p * second + q
                    turned[place, :, :lanes], turned[place, :, lanes:] = twist(p + first * q, value)
            x = turned[places(chunk)].reshape(-1, width)
            spec[places(chunk)] = lane_dft(x, matrix_ref[...]).reshape(-1, channels, width)

    def inverse(left, right, conjugate_left, emit):
        def along_lanes(chunk):
            part = places(chunk)
            lr, li = left[part, :, :lanes], left[part, :, lanes:]
            rr, ri = right[part, :, :lanes], right[part, :, lanes:]
            if conjugate_left:
                re, im = lr * rr + li * ri, li * rr - lr * ri
            else:
                re, im = lr * rr - li * ri, -(lr * ri + li * rr)
            x = jnp.concatenate([re.reshape(-1, lanes), im.reshape(-1, lanes)], axis=1)
            turned[part] = lane_dft(x, matrix_ref[...]).reshape(-1, channels, width)

        def along_rows(chunk):
            for p in chunk:
                values = []
                for q in range(second):
                    place = p * second + q
                    value = (turned[place, :, :lanes], turned[place, :, lanes:])
                    values.append(twist(p + first * q, value))
                for r, value in enumerate(small_dft(values)):
                    store(p * second + r, turn(value, p * r, count))

        along_lanes(chunks[0])
        for before, chunk in zip(chunks, chunks[1:]):
            along_lanes(chunk)
            along_rows(before)
        along_rows(chunks[-1])
        for r in range(second):
            values = small_dft([fetch(p * second + r) for p in range(first)])
            for t, value in enumerate(values):
                n1 = r + second * t
                if n1 < count // 2:
                    emit(n1, value)

    return forward, inverse


def token_blocks(ref, order, kind, pair, batch, channels, live):
    pieces = ref.shape[1] // (2 * batch * channels)

    def where(n1, sequence):
        at = block_rows(kind, 2 * pair + sequence, n1 % pieces, batch, pieces, channels)
        return order.index(n1 // pieces), at

    def load(n1):
        if n1 >= live:
            return None
        return (ref[where(n1, 0)], ref[where(n1, 1)])

    def emit(n1, value):
        ref[where(n1, 0)] = value[0]
        ref[where(n1, 1)] = -value[1]

    return load, emit


def filter_kernel(filter_ref, twist_ref, matrix_ref, spec_ref, middle, turned):
    length = filter_ref.shape[1]
    lanes = twist_ref.shape[1] // 2
    forward, _ = transforms(twist_ref, matrix_ref, middle, turned)

    def load(n1):
        if n1 * lanes >= length:
            return None
        return (filter_ref[:, n1 * lanes : (n1 + 1) * lanes] * (0.5 / length), None)

    forward(load, spec_ref)


def convolve_kernel(
    order, held_ref, filter_ref, twist_ref, matrix_ref, back_hbm, mixed_ref, upstream_ref,
    back, middles, turneds, out_sems,
):
    pairs, count, channels, _ = mixed_ref.shape
    half = back.shape[1] // 2
    kinds = (mixed_ref, upstream_ref)
    scratch = [
        transforms(twist_ref, matrix_ref, middles.at[kind], turneds.at[kind]) for kind in range(2)
    ]

    def send(kind):
        span = pl.ds(kind * half, half)
        return pltpu.make_async_copy(back.at[:, span], back_hbm.at[:, span], out_sems.at[kind])

    for pair in range(pairs):
        for kind in range(2):
            load, _ = token_blocks(held_ref, order, kind, pair, 2 * pairs, channels, count // 2)
            scratch[kind][0](load, kinds[kind].at[pair])
        for kind in range(2):
            _, emit = token_blocks(back, order, kind, pair, 2 * pairs, channels, count // 2)
            scratch[kind][1](filter_ref, kinds[kind].at[pair], kind == 1, emit)
            if pair == pairs - 1:
                send(kind).start()
    for kind in range(2):
        send(kind).wait()


def lag_kernel(scaling, mixed_ref, upstream_ref, twist_ref, matrix_ref, lag_ref, middle, turned):
    lanes = twist_ref.shape[1] // 2
    groups, _, share = lag_ref.shape
    group = lax.axis_index("batch")
    _, inverse = transforms(twist_ref, matrix_ref, middle, turned)
    for pair in range(mixed_ref.shape[0]):

        def emit(n1, value):
            at = n1 * lanes
            slot = lax.rem(at // share - group + groups, groups)
            span = slice(at % share, at % share + lanes)
            if pair == 0:
                lag_ref[slot, :, span] = value[0] * scaling
            else:
                lag_ref[slot, :, span] += value[0] * scaling

        inverse(mixed_ref.at[pair], upstream_ref.at[pair], True, emit)


def output_kernel(
    order, query_ref, key_ref, value_ref, cotangent_ref, skip_ref, home_ref, *refs
):
    *results, ready, out_sems = refs
    shards, _, lanes = home_ref.shape
    batch, tokens, all_channels = query_ref.shape
    channels, pieces = all_channels // shards, tokens // lanes
    skip = skip_ref[...]

    def columns(kind, b):
        turned = []
        for piece in range(pieces):
            at = block_rows(kind, b, piece, batch, pieces, channels)
            blocks = [home_ref[order.index(shard), at] for shard in range(shards)]
            turned.append(jnp.transpose(jnp.concatenate(blocks, axis=0)))
        return jnp.concatenate(turned, axis=0)

    def finish(i, b):
        return pltpu.make_async_copy(ready.at[i, b], results[i].at[b], out_sems.at[i, b])

    for b in range(batch):
        query, key, value, cotangent = query_ref[b], key_ref[b], value_ref[b], cotangent_ref[b]
        hidden = columns(0, b) + skip * (key * value)
        ready[0, b] = query * hidden
        finish(0, b).start()
        ready[1, b] = cotangent * hidden
        finish(1, b).start()
        mixed_grad = columns(1, b) + skip * (cotangent * query)
        ready[2, b] = mixed_grad * value
        finish(2, b).start()
        ready[3, b] = mixed_grad * key
        finish(3, b).start()
    for b in range(batch):
        for i in range(4):
            finish(i, b).wait()


def per_device(query_gate, key_gate, value_input, filters, skip_gain, cotangent, *, shards, groups):
    batch, tokens, all_channels = query_gate.shape
    channels, length = filters.shape
    lanes = 128 if 2 * length // 128 <= 64 else tokens
    count = 2 * length // lanes
    twist, matrix = tables(count, lanes)
    order = exchange_order(shards)
    lane_work = 2 * 3 * count * channels * (2 * lanes) ** 2

    def of(*shape):
        return jax.ShapeDtypeStruct(shape, jnp.float32)

    def call(kernel, name, stages, out_shape, scratch, *arrays, **options):
        return pl.pallas_call(
            kernel,
            out_shape=out_shape,
            scratch_shapes=scratch,
            compiler_params=pltpu.CompilerParams(vmem_limit_bytes=VMEM_BYTES),
            cost_estimate=pl.CostEstimate(
                flops=stages * lane_work, bytes_accessed=stages * 4 * batch * channels * length,
                transcendentals=0,
            ),
            name=name,
            **options,
        )(*arrays)

    def exchange(blocks):
        return lax.all_to_all(
            blocks, "seq", split_axis=0, concat_axis=0, tiled=True, axis_index_groups=[order]
        )

    rows = 2 * batch * channels * tokens // lanes
    swap = of(shards, rows, lanes)
    anywhere = pl.BlockSpec(memory_space=pl.ANY)
    in_vmem = pl.BlockSpec(memory_space=pltpu.VMEM)
    spectrum = of(batch // 2, count, channels, 2 * lanes)
    work = [pltpu.VMEM((count, channels, 2 * lanes), jnp.float32)] * 2
    sent = call(
        functools.partial(gate_kernel, order),
        "gate", 1, swap,
        [
            pltpu.VMEM((4, batch, tokens, all_channels), jnp.float32),
            pltpu.VMEM((shards, rows, lanes), jnp.float32),
            pltpu.SemaphoreType.DMA((4, batch)),
            pltpu.SemaphoreType.DMA((2, batch)),
        ],
        *(
            pltpu.with_memory_space_constraint(x, pltpu.HBM)
            for x in (query_gate, key_gate, value_input, cotangent)
        ),
        in_specs=[pl.BlockSpec(memory_space=pltpu.HBM)] * 4,
        out_specs=anywhere,
    )
    held = exchange(sent)
    filter_spec = call(
        filter_kernel, "filter", 2, of(count, channels, 2 * lanes), work, filters, twist, matrix
    )
    back, mixed_spec, upstream_spec = call(
        functools.partial(convolve_kernel, order),
        "convolve", 8, (swap, spectrum, spectrum),
        [
            pltpu.VMEM((shards, rows, lanes), jnp.float32),
            pltpu.VMEM((2, count, channels, 2 * lanes), jnp.float32),
            pltpu.VMEM((2, count, channels, 2 * lanes), jnp.float32),
            pltpu.SemaphoreType.DMA((2,)),
        ],
        held, filter_spec, twist, matrix,
        out_specs=(anywhere, in_vmem, in_vmem),
    )
    home = exchange(back)
    lag = call(
        functools.partial(lag_kernel, 1.0 / (2.0 * length * math.sqrt(length))),
        "lags", 2, of(groups, channels, length // groups), work,
        mixed_spec, upstream_spec, twist, matrix,
    )
    filter_grad = lag[0]
    for step in range(1, groups):
        pairs = [(source, (source + step) % groups) for source in range(groups)]
        filter_grad = filter_grad + lax.ppermute(lag[step], "batch", pairs)
    output, query_grad, key_grad, value_grad = call(
        functools.partial(output_kernel, order),
        "outputs", 2, (of(*query_gate.shape),) * 4,
        [
            pltpu.VMEM((4, batch, tokens, all_channels), jnp.float32),
            pltpu.SemaphoreType.DMA((4, batch)),
        ],
        query_gate, key_gate, value_input, cotangent, skip_gain.reshape(1, all_channels),
        home,
        out_specs=(anywhere,) * 4,
    )
    return (output, query_grad, key_grad, value_grad, filter_grad)


def solution(mesh):
    in_specs = (
        P("batch", "seq", None),
        P("batch", "seq", None),
        P("batch", "seq", None),
        P("seq", None),
        P(),
        P("batch", "seq", None),
    )
    out_specs = (
        P("batch", "seq", None),
        P("batch", "seq", None),
        P("batch", "seq", None),
        P("batch", "seq", None),
        P("seq", "batch"),
    )
    shards, groups = mesh.shape["seq"], mesh.shape["batch"]

    def whole(*arrays):
        return per_device(*arrays, shards=shards, groups=groups)

    return jax.shard_map(whole, mesh=mesh, in_specs=in_specs, out_specs=out_specs, check_vma=False)
```
